512 devices in a mesh: blk: 32 (over x, y, core), head: 8 (over z_lo), rep: 2 (over z_hi).
Axes of the slice: x: 4, y: 4, z: 16 (z_hi: 2, z_lo: 8; z = z_hi * 8 + z_lo), core: 2. Of those that a mesh axis runs over, the one named last changes fastest.
Arguments:
- slab_query: bfloat16 [4096, 3072], P(('rep', 'blk', 'head')), parts along dimension 0, may hold values from -6 to 6
- slab_output: bfloat16 [4096, 3072], P(('rep', 'blk', 'head')), parts along dimension 0, may hold values from -4 to 4
- slab_cotangent: bfloat16 [4096, 3072], P(('rep', 'blk', 'head')), parts along dimension 0, may hold values from -768 to 768
- slab_logsum: float32 [4096, 24], P(('rep', 'blk'), 'head'), parts along dimension 0
- image_keys: bfloat16 [16384, 3072], P(('rep', 'blk', 'head')), parts along dimension 0, may hold values from -6 to 6
- image_values: bfloat16 [16384, 3072], P(('rep', 'blk', 'head')), parts along dimension 0, may hold values from -6 to 6
- text_query: bfloat16 [512, 3072], P('rep', 'head'), parts along dimension 0, may hold values from -6 to 6
- text_keys: bfloat16 [512, 3072], P('rep', 'head'), parts along dimension 0, may hold values from -6 to 6
- text_values: bfloat16 [512, 3072], P('rep', 'head'), parts along dimension 0, may hold values from -6 to 6
- text_output: bfloat16 [512, 3072], P('rep', 'head'), parts along dimension 0, may hold values from -4 to 4
- text_cotangent: bfloat16 [512, 3072], P('rep', 'head'), parts along dimension 0, may hold values from -768 to 768
- text_logsum: float32 [512, 24], P('rep', 'head'), parts along dimension 0
- text_count: int32 [2], P('rep'), parts along dimension 0, may hold values from 64 to 256
- slab_offsets: int32 [2], P('rep'), parts along dimension 0, may hold values from 0 to 96
Outputs:
- slab_query_grad: bfloat16 [4096, 3072], P(('rep', 'blk', 'head')), parts along dimension 0
- image_key_grad: bfloat16 [16384, 3072], P(('rep', 'blk', 'head')), parts along dimension 0
- image_value_grad: bfloat16 [16384, 3072], P(('rep', 'blk', 'head')), parts along dimension 0
- text_query_grad: bfloat16 [512, 3072], P('rep', 'head'), parts along dimension 0
- text_key_grad: bfloat16 [512, 3072], P('rep', 'head'), parts along dimension 0
- text_value_grad: bfloat16 [512, 3072], P('rep', 'head'), parts along dimension 0
The draws below stay inside these ranges and needn't reach their ends.
There are 2 independent parts, one for each index of `rep`. The reference program is written for one: setup_inputs(seed, part) draws one part's arguments, and reference() takes and returns one part's arrays. A program takes and returns all parts, laid end to end along the dimension named above; each array names one. Nothing has to cross between parts.
Inputs may be any that keep to these rules, and one draw needn't show every extreme that they name: Text rows at index text_count[0] or later are padding. The slab is the 2048 consecutive image tokens from slab_offsets[0] * 64 onward.
All inputs are finite; a program needn't handle non-finite values.
Results may differ from the reference program's by a relative error of at most 0.017.
The reference program's roundings to bfloat16 on the way count: a program that leaves them out, or rounds other values in their place, can miss the bound.
Values may be sent and summed in bfloat16 or wider, within the bound.
A program may use at most 64 MiB of HBM per device.

```python
import jax
import jax.numpy as jnp
from jax import lax

HEADS = 24
HEAD_DIM = 128
QB = 64
TXT = 256
GRID_W = 256
IMAGE = 8192
SLAB = 2048
N_BLK = 32


def normaliser(seed_key, row_count, lowest, highest):
    centre = jnp.log(jnp.float32(IMAGE + TXT)) + 0.5
    return centre + jax.random.uniform(seed_key, (row_count, HEADS), jnp.float32, lowest, highest)


def draw_slab_logsum(key, part):
    key = jax.random.fold_in(key, 11)
    return normaliser(key, SLAB, -1.0, 1.0)


def draw_text_logsum(key, part):
    key = jax.random.fold_in(key, 23)
    return normaliser(key, TXT, -1.0, 1.0)


def level_of(key, shape, cuts, smallest, high):
    def one(dim, blocks):
        heights = jax.random.uniform(jax.random.fold_in(jax.random.fold_in(key, 6), dim), (blocks,), jnp.float32, smallest / len(cuts), high / len(cuts))
        return jnp.repeat(jnp.exp(heights), shape[dim] // blocks).reshape((-1,) + (1,) * (len(shape) - dim - 1))

    level = one(*cuts[0])
    for cut in cuts[1:]:
        level = level * one(*cut)
    return level


def noise(own_key, dims, spread, most, shards=(), kind=jnp.bfloat16):
    result = jax.random.normal(own_key, dims, jnp.float32) * spread
    if len(shards) > 0:
        result = level_of(own_key, dims, shards, -0.22, 0.18) * result
    return jnp.clip(result, min=-most, max=most).astype(kind)


def setup_inputs(seed: int = 0, part: int = 0) -> dict:
    streams_of = jax.random.split(jax.random.key(seed), 15)
    part_keys = jax.random.split(jax.random.fold_in(streams_of[14], part), 15)
    return {
        "slab_query": noise(part_keys[0], (SLAB, HEADS * HEAD_DIM), 1.0, 6.0, ((0, 256),)),
        "slab_output": noise(part_keys[1], (SLAB, HEADS * HEAD_DIM), 0.25, 4.0, ((0, 256),)),
        "slab_cotangent": noise(part_keys[2], (SLAB, HEADS * HEAD_DIM), (IMAGE // 64), 768.0, ((0, 256),)),
        "slab_logsum": draw_slab_logsum(jax.random.fold_in(jax.random.fold_in(streams_of[14], part), 71), part),
        "image_keys": noise(part_keys[4], (IMAGE, HEADS * HEAD_DIM), 1.0, 6.0, ((0, 256),)),
        "image_values": noise(part_keys[5], (IMAGE, HEADS * HEAD_DIM), 1.0, 6.0, ((0, 256),)),
        "text_query": noise(part_keys[6], (TXT, HEADS * HEAD_DIM), 1.0, 6.0, ((1, 8),)),
        "text_keys": noise(part_keys[7], (TXT, HEADS * HEAD_DIM), 1.0, 6.0, ((1, 8),)),
        "text_values": noise(part_keys[8], (TXT, HEADS * HEAD_DIM), 1.0, 6.0, ((1, 8),)),
        "text_output": noise(part_keys[9], (TXT, HEADS * HEAD_DIM), 0.25, 4.0, ((1, 8),)),
        "text_cotangent": noise(part_keys[10], (TXT, HEADS * HEAD_DIM), (IMAGE // 64), 768.0, ((1, 8),)),
        "text_logsum": draw_text_logsum(jax.random.fold_in(jax.random.fold_in(streams_of[14], part), 71), part),
        "text_count": jax.random.randint(part_keys[12], (1,), TXT // 4, TXT + 1).astype(jnp.int32),
        "slab_offsets": jax.random.randint(part_keys[13], (1,), 0, IMAGE // QB - N_BLK + 1).astype(jnp.int32),
    }


def rotate(values_in, grid_row, grid_col, orient):
    row_count = values_in.shape[0]
    quarter = HEAD_DIM // 4
    halfway = HEAD_DIM // 2
    frequency = 10000.0 ** (-jnp.arange(quarter, dtype=jnp.float32) / quarter)
    angles = jnp.concatenate([grid_row[:, None] * frequency[None, :], grid_col[:, None] * frequency[None, :]], axis=1)
    cosine = jnp.cos(angles)[:, None, :]
    sine_term = orient * jnp.sin(angles)[:, None, :]
    shaped = values_in.reshape(row_count, -1, HEAD_DIM)
    front_half = shaped[..., :halfway]
    back_half = shaped[..., halfway:]
    turned = jnp.concatenate([front_half * cosine - back_half * sine_term, back_half * cosine + front_half * sine_term], axis=-1)
    return turned.reshape(row_count, -1)


def grid_place(positions):
    return (positions // GRID_W).astype(jnp.float32), (positions % GRID_W).astype(jnp.float32)


def row_products(cotangent, output):
    row_count = cotangent.shape[0]
    joined = cotangent.astype(jnp.float32) * output.astype(jnp.float32)
    return jnp.sum(joined.reshape(row_count, -1, HEAD_DIM), axis=-1)


def by_head(array):
    return jnp.transpose(array.reshape(array.shape[0], HEADS, HEAD_DIM), (1, 0, 2))


def by_rows(array):
    return jnp.transpose(array, (1, 0, 2)).reshape(array.shape[1], HEADS * HEAD_DIM)


def reference(slab_query, slab_output, slab_cotangent, slab_logsum, image_keys, image_values, text_query, text_keys, text_values, text_output, text_cotangent, text_logsum, text_count, slab_offsets):
    factor = HEAD_DIM ** -0.5
    slab_index = jnp.arange(SLAB, dtype=jnp.int32)
    slab_position = slab_offsets[0].astype(jnp.int32) * QB + slab_index
    slab_row, slab_col = grid_place(slab_position)
    image_row, image_col = grid_place(jnp.arange(IMAGE, dtype=jnp.int32))
    text_place = (GRID_W + jnp.arange(TXT, dtype=jnp.int32)).astype(jnp.float32)
    slab_turned = rotate(slab_query.astype(jnp.float32), slab_row, slab_col, 1.0).astype(jnp.bfloat16)
    image_turned = rotate(image_keys.astype(jnp.float32), image_row, image_col, 1.0).astype(jnp.bfloat16)
    text_query_turned = rotate(text_query.astype(jnp.float32), text_place, text_place, 1.0).astype(jnp.bfloat16)
    text_keys_turned = rotate(text_keys.astype(jnp.float32), text_place, text_place, 1.0).astype(jnp.bfloat16)
    queries_all = jnp.concatenate([slab_turned, text_query_turned], axis=0)
    keys_all = jnp.concatenate([image_turned, text_keys_turned], axis=0)
    values_all = jnp.concatenate([image_values, text_values], axis=0)
    cotan_all = jnp.concatenate([slab_cotangent, text_cotangent], axis=0)
    logsum_all = jnp.concatenate([slab_logsum, text_logsum], axis=0)
    deltas = jnp.concatenate([row_products(slab_cotangent, slab_output), row_products(text_cotangent, text_output)], axis=0)
    key_mask = (jnp.arange(IMAGE + TXT, dtype=jnp.int32) < IMAGE + text_count[0]).astype(jnp.float32)

    def one_head(pieces):
        query_head, key_head, value_head, cotan_head, logsum_head, delta_head = pieces
        query_wide = query_head.astype(jnp.float32)
        key_wide = key_head.astype(jnp.float32)
        cotan_wide = cotan_head.astype(jnp.float32)
        scores = jnp.dot(query_wide, key_wide.T)
        probabilities = jnp.exp(scores * factor - logsum_head[:, None]) * key_mask[None, :]
        weights = lax.optimization_barrier(probabilities.astype(jnp.bfloat16)).astype(jnp.float32)
        value_grad = jnp.dot(weights.T, cotan_wide)
        prob_grad = jnp.dot(cotan_wide, value_head.astype(jnp.float32).T)
        score_grad = (probabilities * (prob_grad - delta_head[:, None]) * factor).astype(jnp.bfloat16)
        score_wide = lax.optimization_barrier(score_grad).astype(jnp.float32)
        query_grad = jnp.dot(score_wide, key_wide)
        key_grad = jnp.dot(score_wide.T, query_wide)
        return query_grad, key_grad, value_grad

    query_grad, key_grad, value_grad = lax.map(one_head, (by_head(queries_all), by_head(keys_all), by_head(values_all), by_head(cotan_all), logsum_all.T, deltas.T))
    query_rows = by_rows(query_grad)
    key_rows = by_rows(key_grad)
    value_rows = by_rows(value_grad)
    slab_query_grad = rotate(query_rows[:SLAB], slab_row, slab_col, -1.0).astype(jnp.bfloat16)
    text_query_grad = rotate(query_rows[SLAB:], text_place, text_place, -1.0).astype(jnp.bfloat16)
    image_key_grad = rotate(key_rows[:IMAGE], image_row, image_col, -1.0).astype(jnp.bfloat16)
    text_key_grad = rotate(key_rows[IMAGE:], text_place, text_place, -1.0).astype(jnp.bfloat16)
    image_value_grad = value_rows[:IMAGE].astype(jnp.bfloat16)
    text_value_grad = value_rows[IMAGE:].astype(jnp.bfloat16)
    return (slab_query_grad, image_key_grad, image_value_grad, text_query_grad, text_key_grad, text_value_grad)
```

```python
import functools

import jax
import jax.numpy as jnp
import numpy as np
from jax import lax
from jax.experimental import pallas as pl
from jax.experimental.pallas import tpu as pltpu
from jax.sharding import PartitionSpec as P

HEAD_DIM = 128
FACTOR = HEAD_DIM ** (-0.5)
NZ = 8
NB = 16
HD = 3
W = HD * HEAD_DIM
TXT = 256
HALF = TXT // 2
ROWS = 64
KEYS = 256
SLAB_Q = NB * ROWS
SILENT = 1e30
BF = jnp.bfloat16
F32 = jnp.float32
MESH = pl.DeviceIdType.MESH


def tables():
    place = np.arange(512, dtype=np.float64)[:, None]
    frequency = 10000.0 ** (-np.arange(32, dtype=np.float64) / 32)
    angles = np.tile(place * frequency[None, :], (1, 4))
    sign = np.where(np.arange(128) < 64, -1.0, 1.0)
    return np.cos(angles).astype(np.float32), (np.sin(angles) * sign).astype(np.float32)


def nt(a, b):
    return lax.dot_general(a, b, (((1,), (1,)), ((), ())), preferred_element_type=F32)


def nn(a, b):
    return lax.dot_general(a, b, (((1,), (0,)), ((), ())), preferred_element_type=F32)


def tn(a, b):
    return lax.dot_general(a, b, (((0,), (0,)), ((), ())), preferred_element_type=F32)


def turn(x, cosine, sine):
    return x * cosine + pltpu.roll(x, 64, 1) * sine


def turn_back(x, cosine, sine):
    return x * cosine - pltpu.roll(x, 64, 1) * sine


def cols(n, width=HEAD_DIM):
    return slice(n * width, (n + 1) * width)


def attend(keys, values, queries, cotan, logsum, delta, mask=None):
    p = jnp.exp(nt(keys, queries) * FACTOR - logsum)
    if mask is not None:
        p = p * mask
    dv = nn(p.astype(BF), cotan)
    dp = nt(values, cotan)
    ds = (p * (dp - delta) * FACTOR).astype(BF)
    return tn(ds, keys), nn(ds, queries), dv


def kernel(
    off_ref, cnt_ref, sq, so, sg, sl, ik, iv, tq, tk, tv, to, tg, tl, cos_t, sin_t,
    sqg, ikg, ivg, tqg, tkg, tvg,
    qgs, dls, qgr, dlr, ks, kall, vall, qg, st, stp, tkr, tm, qtk, dqt, dkt, dvt, xt,
    dq, dk, dv, xk, dks, dvs, rss, rsr, sqs, sqr, tx,
    s_z, r_zqg, r_zd, r_zk, r_zv, s_xy, r_xyq, r_xys, s_sib, r_sib,
    s_o, r_ok, r_ov, r_oq, s_rs, r_rs, s_tx, r_tx,
):
    blk = lax.axis_index("blk")
    h = lax.axis_index("head")
    c = lax.rem(blk, 2)
    b = blk // 2
    lane = lax.broadcasted_iota(jnp.int32, (1, HEAD_DIM), 1)
    first = lax.rem(lane, 64) < 32
    sib = {"blk": 2 * b + 1 - c}

    def zdev(t):
        return lax.rem(h + t, NZ)

    def xydev(t):
        return lax.rem(b + t, NB)

    def remote(src, dst, ss, rs, dev):
        return pltpu.make_async_remote_copy(
            src_ref=src, dst_ref=dst, send_sem=ss, recv_sem=rs, device_id=dev, device_id_type=MESH
        )

    def angles(row, start, count):
        ct = cos_t[pl.ds(start, count), :]
        sn = sin_t[pl.ds(start, count), :]
        cr = cos_t[pl.ds(row, 1), :]
        sr = sin_t[pl.ds(row, 1), :]
        return jnp.where(first, cr, ct), jnp.where(first, sr, sn)

    place = off_ref[0] + blk
    row_at = lax.broadcasted_iota(jnp.int32, (32, 1), 0) == place // 4
    col_at = lax.rem(place, 4)

    def slab_angles(start, count):
        result = []
        for table in (cos_t, sin_t):
            row = jnp.sum(jnp.where(row_at, table[:32, :], 0.0), axis=0, keepdims=True)
            col = table[pl.ds(start, count), :]
            for i in range(1, 4):
                col = jnp.where(col_at == i, table[pl.ds(64 * i + start, count), :], col)
            result.append(jnp.where(first, row, col))
        return result

    bar = pltpu.get_barrier_semaphore()

    def greet_z(t, carry):
        pl.semaphore_signal(bar, inc=1, device_id={"head": zdev(t)}, device_id_type=MESH)
        return carry

    def greet_xy(t, carry):
        pl.semaphore_signal(bar, inc=1, device_id={"blk": 2 * xydev(t) + c}, device_id_type=MESH)
        return carry

    lax.fori_loop(1, NZ, greet_z, 0)
    lax.fori_loop(1, NB, greet_xy, 0)
    pl.semaphore_signal(bar, inc=1, device_id=sib, device_id_type=MESH)

    cq, sn_q = slab_angles(pl.multiple_of(8 * h, 8), 8)
    for d in range(NZ):
        acc = jnp.zeros((8, HEAD_DIM), F32)
        for j in range(HD):
            n = d * HD + j
            g = sg[:, cols(n)].astype(F32)
            q = turn(sq[:, cols(n)].astype(F32), cq, sn_q)
            qgs[:, cols(n)] = jnp.concatenate([q, g], axis=0).astype(BF)
            own = jnp.sum(g * so[:, cols(n)].astype(F32), axis=1, keepdims=True)
            acc = jnp.where(lane == j, own, acc)
        dls[d] = acc
    pl.semaphore_wait(bar, NZ + NB - 1)

    def wide(d):
        return pl.ds(pl.multiple_of(d * W, W), W)

    def z_qg(t, d):
        return remote(qgs.at[:, wide(d)], qgr.at[h], s_z.at[0, t], r_zqg.at[h], {"head": d})

    def z_dl(t, d):
        return remote(dls.at[d], dlr.at[h], s_z.at[1, t], r_zd.at[h], {"head": d})

    def key_rows(s):
        return pl.ds(pl.multiple_of(c * KEYS + s * 32, 32), 32)

    def z_k(t, d):
        return remote(ks.at[:, wide(d)], kall.at[key_rows(h), :], s_z.at[2, t], r_zk.at[h], {"head": d})

    def z_v(t, d):
        return remote(iv.at[:, wide(d)], vall.at[key_rows(h), :], s_z.at[3, t], r_zv.at[h], {"head": d})

    def go_qg(t, carry):
        z_qg(t, zdev(t)).start()
        z_dl(t, zdev(t)).start()
        return carry

    def go_v(t, carry):
        z_v(t, zdev(t)).start()
        return carry

    def go_k(t, carry):
        z_k(t, zdev(t)).start()
        return carry

    lax.fori_loop(1, NZ, go_qg, 0)
    lax.fori_loop(1, NZ, go_v, 0)
    ck, sn_k = angles(blk, pl.multiple_of(32 * h, 32), 32)
    for n in range(NZ * HD):
        ks[:, cols(n)] = turn(ik[:, cols(n)].astype(F32), ck, sn_k).astype(BF)
    lax.fori_loop(1, NZ, go_k, 0)
    kall[key_rows(h), :] = ks[:, wide(h)]
    vall[key_rows(h), :] = iv[:, wide(h)]
    qgr[h] = qgs[:, wide(h)]
    dlr[h] = dls[h]

    half = pl.ds(pl.multiple_of(HALF * c, HALF), HALF)
    ct = cos_t[pl.ds(pl.multiple_of(TXT + HALF * c, HALF), HALF), :]
    sn = sin_t[pl.ds(pl.multiple_of(TXT + HALF * c, HALF), HALF), :]
    acc = jnp.zeros((HALF, HEAD_DIM), F32)
    for j in range(HD):
        g = tg[half, cols(j)]
        qg[0, SLAB_Q:, cols(j)] = turn(tq[half, cols(j)].astype(F32), ct, sn).astype(BF)
        qg[1, SLAB_Q:, cols(j)] = g
        own = jnp.sum(g.astype(F32) * to[half, cols(j)].astype(F32), axis=1, keepdims=True)
        acc = jnp.where(lane == j, own, acc)
        acc = jnp.where(lane == HD + j, tl[half, j : j + 1], acc)
        tkr[:, cols(j)] = turn(tk[:, cols(j)].astype(F32), cos_t[TXT:, :], sin_t[TXT:, :]).astype(BF)
    tm[...] = acc
    stp[:, SLAB_Q:] = acc.T[:8, :]

    def wait_qg(t, carry):
        s = zdev(t)
        remote(qgs.at[:, wide(s)], qgr.at[s], s_z.at[0, t], r_zqg.at[s], {"head": s}).wait_recv()
        remote(dls.at[s], dlr.at[s], s_z.at[1, t], r_zd.at[s], {"head": s}).wait_recv()
        return carry

    lax.fori_loop(1, NZ, wait_qg, 0)
    both = qgr[...].astype(F32)
    own_q = both[:, :8, :].reshape(ROWS, W).astype(BF)
    own_g = both[:, 8:, :].reshape(ROWS, W).astype(BF)
    my_rows = pl.ds(pl.multiple_of(ROWS * b, ROWS), ROWS)
    qg[0, my_rows, :] = own_q
    qg[1, my_rows, :] = own_g
    stats = dlr[...].reshape(ROWS, HEAD_DIM)
    for j in range(HD):
        stats = jnp.where(lane == HD + j, sl[:, j : j + 1], stats)
    odd = lax.rem(b, 2) == 1
    blank = jnp.zeros_like(stats)
    spread = jnp.concatenate([jnp.where(odd, blank, stats), jnp.where(odd, stats, blank)], axis=0)
    st[b] = spread.T[:8, :]

    def xy_qg(t, e):
        return remote(
            qg.at[:, my_rows, :], qg.at[:, my_rows, :], s_xy.at[0, t], r_xyq.at[b], {"blk": 2 * e + c}
        )

    def xy_st(t, e):
        return remote(st.at[b], st.at[b], s_xy.at[1, t], r_xys.at[b], {"blk": 2 * e + c})

    def go_xy(t, carry):
        xy_qg(t, xydev(t)).start()
        xy_st(t, xydev(t)).start()
        return carry

    lax.fori_loop(1, NB, go_xy, 0)

    pair = pl.multiple_of(16 * (b // 2), 16)
    qtk[0, :ROWS, :] = own_q
    qtk[1, :ROWS, :] = own_g
    for i in range(2):
        qtk[i, ROWS : ROWS + 16, :] = qg[i, pl.ds(SLAB_Q + pair, 16), :]
        qtk[i, ROWS + 16 :, :] = jnp.zeros((HEAD_DIM - ROWS - 16, W), BF)
    index = lax.broadcasted_iota(jnp.int32, (16, 1), 0) // 8
    is_l = jnp.logical_and(lane >= HD, lane < 2 * HD)
    text_stats = jnp.where(
        jnp.logical_and(index != lax.rem(b, 2), is_l), SILENT, tm[pl.ds(pair, 16), :]
    )
    rest = jnp.broadcast_to(jnp.where(is_l, SILENT, 0.0), (HEAD_DIM - ROWS - 16, HEAD_DIM))
    tstats = jnp.concatenate([stats, text_stats, rest], axis=0).T
    key_index = lax.broadcasted_iota(jnp.int32, (TXT, 1), 0)
    mask = (key_index < cnt_ref[0]).astype(F32)
    for j in range(HD):
        one_q, one_k, one_v = attend(
            tkr[:, cols(j)], tv[:, cols(j)], qtk[0, :, cols(j)], qtk[1, :, cols(j)],
            tstats[HD + j : HD + j + 1, :], tstats[j : j + 1, :], mask,
        )
        dqt[:, cols(j)] = one_q
        dkt[:, cols(j)] = one_k
        dvt[:, cols(j)] = one_v
    other = pl.ds(pl.multiple_of(HALF * (1 - c), HALF), HALF)
    sib_tk = remote(dkt.at[other, :], xt.at[0], s_sib.at[0], r_sib.at[0], sib)
    sib_tv = remote(dvt.at[other, :], xt.at[1], s_sib.at[1], r_sib.at[1], sib)
    sib_tk.start()
    sib_tv.start()

    def wait_kv(t, carry):
        s = zdev(t)
        remote(iv.at[:, wide(s)], vall.at[key_rows(s), :], s_z.at[3, t], r_zv.at[s], {"head": s}).wait_recv()
        remote(ks.at[:, wide(s)], kall.at[key_rows(s), :], s_z.at[2, t], r_zk.at[s], {"head": s}).wait_recv()
        return carry

    lax.fori_loop(1, NZ, wait_kv, 0)
    mine = pl.ds(pl.multiple_of(KEYS * c, KEYS), KEYS)
    theirs = pl.ds(pl.multiple_of(KEYS * (1 - c), KEYS), KEYS)
    sib_k = remote(kall.at[mine, :], kall.at[mine, :], s_sib.at[2], r_sib.at[2], sib)
    sib_v = remote(vall.at[mine, :], vall.at[mine, :], s_sib.at[3], r_sib.at[3], sib)
    sib_k.start()
    sib_v.start()

    def wait_xy(t, carry):
        s = xydev(t)
        rows = pl.ds(pl.multiple_of(ROWS * s, ROWS), ROWS)
        remote(qg.at[:, rows, :], qg.at[:, rows, :], s_xy.at[0, t], r_xyq.at[s], {"blk": 2 * s + c}).wait_recv()
        remote(st.at[s], st.at[s], s_xy.at[1, t], r_xys.at[s], {"blk": 2 * s + c}).wait_recv()
        return carry

    lax.fori_loop(1, NB, wait_xy, 0)
    for i in range(NB // 2):
        stp[:, cols(i)] = st[2 * i] + st[2 * i + 1]
    remote(kall.at[theirs, :], kall.at[theirs, :], s_sib.at[2], r_sib.at[2], sib).wait_recv()
    remote(vall.at[theirs, :], vall.at[theirs, :], s_sib.at[3], r_sib.at[3], sib).wait_recv()

    for j in range(HD):
        keys = kall[:, cols(j)]
        values = vall[:, cols(j)]
        one_q, one_k, one_v = attend(
            keys, values, qg[0, SLAB_Q:, cols(j)], qg[1, SLAB_Q:, cols(j)],
            stp[HD + j : HD + j + 1, SLAB_Q:], stp[j : j + 1, SLAB_Q:],
        )
        dq[SLAB_Q:, cols(j)] = one_q
        dk[:, cols(j)] = one_k
        dv[:, cols(j)] = one_v

        def chunk(i, carry, j=j):
            rows = pl.ds(pl.multiple_of(i * 256, 256), 256)
            one_q, one_k, one_v = attend(
                kall[:, cols(j)], vall[:, cols(j)], qg[0, rows, cols(j)], qg[1, rows, cols(j)],
                stp[HD + j : HD + j + 1, rows], stp[j : j + 1, rows],
            )
            dq[rows, cols(j)] = one_q
            dk[:, cols(j)] += one_k
            dv[:, cols(j)] += one_v
            return carry

        lax.fori_loop(0, SLAB_Q // 256, chunk, 0)

    sib_dk = remote(dk.at[theirs, :], xk.at[0], s_sib.at[4], r_sib.at[4], sib)
    sib_dv = remote(dv.at[theirs, :], xk.at[1], s_sib.at[5], r_sib.at[5], sib)
    sib_dk.start()
    sib_dv.start()

    sib_tk.wait()
    sib_tv.wait()
    text_terms = [
        dq[SLAB_Q:, :].reshape(NB, 8, W),
        (dkt[half, :] + xt[0]).reshape(NB, 8, W),
        (dvt[half, :] + xt[1]).reshape(NB, 8, W),
        jnp.zeros((NB, 8, W), F32),
    ]
    rss[:, ROWS:, :] = jnp.concatenate(text_terms, axis=1).astype(BF)
    rss[:, :ROWS, :] = dq[:SLAB_Q, :].reshape(NB, ROWS, W).astype(BF)
    rsr[b] = rss[b]

    def rs(t, e):
        return remote(rss.at[e], rsr.at[b], s_rs.at[t], r_rs.at[b], {"blk": 2 * e + c})

    def go_rs(t, carry):
        rs(t, xydev(t)).start()
        return carry

    lax.fori_loop(1, NB, go_rs, 0)

    sib_dv.wait()
    sib_dk.wait()
    dvs[...] = (dv[mine, :] + xk[1]).astype(BF)
    ck, sn_k = angles(blk, 0, KEYS)
    for j in range(HD):
        dks[:, cols(j)] = turn_back(dk[mine, cols(j)] + xk[0, :, cols(j)], ck, sn_k).astype(BF)

    def token_rows(s):
        return pl.ds(pl.multiple_of(s * 32, 32), 32)

    def out_k(t, d):
        return remote(dks.at[token_rows(d), :], ikg.at[:, wide(h)], s_o.at[0, t], r_ok.at[h], {"head": d})

    def out_v(t, d):
        return remote(dvs.at[token_rows(d), :], ivg.at[:, wide(h)], s_o.at[1, t], r_ov.at[h], {"head": d})

    def go_out(t, carry):
        out_k(t, zdev(t)).start()
        out_v(t, zdev(t)).start()
        return carry

    lax.fori_loop(1, NZ, go_out, 0)
    ikg[:, wide(h)] = dks[token_rows(h), :]
    ivg[:, wide(h)] = dvs[token_rows(h), :]

    def wait_rs(t, carry):
        s = xydev(t)
        remote(rss.at[s], rsr.at[s], s_rs.at[t], r_rs.at[s], {"blk": 2 * s + c}).wait_recv()
        return carry

    lax.fori_loop(1, NB, wait_rs, 0)
    total = rsr[0].astype(F32)
    for i in range(1, NB):
        total = total + rsr[i].astype(F32)
    slab_total = total[:ROWS, :] + dqt[:ROWS, :]
    extra = jnp.where(odd, dqt[ROWS + 8 : ROWS + 16, :], dqt[ROWS : ROWS + 8, :])
    text_q = total[ROWS : ROWS + 8, :] + extra
    text_k = total[ROWS + 8 : ROWS + 16, :]
    text_v = total[ROWS + 16 : ROWS + 24, :]
    cq, sn_q = slab_angles(0, ROWS)
    text_at = pl.ds(pl.multiple_of(TXT + HALF * c + 8 * b, 8), 8)
    ct = cos_t[text_at, :]
    sn = sin_t[text_at, :]
    slab_parts = []
    text_parts = []
    for j in range(HD):
        slab_parts.append(turn_back(slab_total[:, cols(j)], cq, sn_q).reshape(NZ, 8, HEAD_DIM))
        text_parts.append(
            jnp.concatenate(
                [
                    turn_back(text_q[:, cols(j)], ct, sn),
                    turn_back(text_k[:, cols(j)], ct, sn),
                    text_v[:, cols(j)],
                    jnp.zeros((8, HEAD_DIM), F32),
                ],
                axis=0,
            )
        )
    for j in range(HD):
        tx[c, b, :, cols(j)] = text_parts[j].astype(BF)

    def tx_copy(t, e):
        return remote(tx.at[c, b], tx.at[c, b], s_tx.at[t], r_tx.at[b], {"blk": 2 * e + c})

    def go_tx(t, carry):
        tx_copy(t, xydev(t)).start()
        return carry

    lax.fori_loop(1, NB, go_tx, 0)
    low = jnp.concatenate([slab_parts[0], slab_parts[2]], axis=1).astype(BF)
    high = jnp.concatenate([slab_parts[1], jnp.zeros((NZ, 8, HEAD_DIM), F32)], axis=1).astype(BF)
    sqs[:, :, :HEAD_DIM] = low
    sqs[:, :, HEAD_DIM:] = high

    def out_q(t, d):
        return remote(sqs.at[d], sqr.at[h], s_o.at[2, t], r_oq.at[h], {"head": d})

    def go_oq(t, carry):
        out_q(t, zdev(t)).start()
        return carry

    lax.fori_loop(1, NZ, go_oq, 0)
    sqr[h] = sqs[h]

    def wait_tx(t, carry):
        s = xydev(t)
        remote(tx.at[c, s], tx.at[c, s], s_tx.at[t], r_tx.at[s], {"blk": 2 * s + c}).wait_recv()
        return carry

    lax.fori_loop(1, NB, wait_tx, 0)
    sib_tx = remote(tx.at[c], tx.at[c], s_sib.at[6], r_sib.at[6], sib)
    sib_tx.start()

    def wait_oq(t, carry):
        s = zdev(t)
        remote(sqs.at[s], sqr.at[s], s_o.at[2, t], r_oq.at[s], {"head": s}).wait_recv()
        return carry

    lax.fori_loop(1, NZ, wait_oq, 0)
    for s in range(NZ):
        piece = sqr[s].astype(F32)
        sqg[:, s * W : s * W + 128] = piece[:8, :128].astype(BF)
        sqg[:, s * W + 128 : s * W + 256] = piece[:8, 128:].astype(BF)
        sqg[:, s * W + 256 : s * W + 384] = piece[8:, :128].astype(BF)

    def wait_out(t, carry):
        s = zdev(t)
        remote(dks.at[token_rows(s), :], ikg.at[:, wide(s)], s_o.at[0, t], r_ok.at[s], {"head": s}).wait_recv()
        remote(dvs.at[token_rows(s), :], ivg.at[:, wide(s)], s_o.at[1, t], r_ov.at[s], {"head": s}).wait_recv()
        return carry

    lax.fori_loop(1, NZ, wait_out, 0)
    remote(tx.at[1 - c], tx.at[1 - c], s_sib.at[6], r_sib.at[6], sib).wait_recv()
    for core in range(2):
        block = tx[core].astype(F32)
        rows = slice(core * HALF, (core + 1) * HALF)
        tqg[rows, :] = block[:, :8, :].reshape(HALF, W).astype(BF)
        tkg[rows, :] = block[:, 8:16, :].reshape(HALF, W).astype(BF)
        tvg[rows, :] = block[:, 16:24, :].reshape(HALF, W).astype(BF)

    def drain_z(t, carry):
        d = zdev(t)
        z_qg(t, d).wait_send()
        z_dl(t, d).wait_send()
        z_k(t, d).wait_send()
        z_v(t, d).wait_send()
        out_k(t, d).wait_send()
        out_v(t, d).wait_send()
        out_q(t, d).wait_send()
        return carry

    def drain_xy(t, carry):
        e = xydev(t)
        xy_qg(t, e).wait_send()
        xy_st(t, e).wait_send()
        rs(t, e).wait_send()
        tx_copy(t, e).wait_send()
        return carry

    lax.fori_loop(1, NZ, drain_z, 0)
    lax.fori_loop(1, NB, drain_xy, 0)
    sib_k.wait_send()
    sib_v.wait_send()
    sib_tx.wait_send()


def on_device(
    slab_query, slab_output, slab_cotangent, slab_logsum, image_keys, image_values,
    text_query, text_keys, text_values, text_output, text_cotangent, text_logsum,
    text_count, slab_offsets,
):
    cos_t, sin_t = tables()
    vmem = pl.BlockSpec(memory_space=pltpu.VMEM)
    smem = pl.BlockSpec(memory_space=pltpu.SMEM)
    dma = pltpu.SemaphoreType.DMA
    shapes = [
        jax.ShapeDtypeStruct(x.shape, BF)
        for x in (slab_query, image_keys, image_values, text_query, text_keys, text_values)
    ]
    return pl.pallas_call(
        kernel,
        out_shape=shapes,
        in_specs=[smem, smem] + [vmem] * 14,
        out_specs=[vmem] * 6,
        scratch_shapes=[
            pltpu.VMEM((16, NZ * W), BF),
            pltpu.VMEM((NZ, 8, HEAD_DIM), F32),
            pltpu.VMEM((NZ, 16, W), BF),
            pltpu.VMEM((NZ, 8, HEAD_DIM), F32),
            pltpu.VMEM((32, NZ * W), BF),
            pltpu.VMEM((2 * KEYS, W), BF),
            pltpu.VMEM((2 * KEYS, W), BF),
            pltpu.VMEM((2, SLAB_Q + HALF, W), BF),
            pltpu.VMEM((NB, 8, HEAD_DIM), F32),
            pltpu.VMEM((8, SLAB_Q + HALF), F32),
            pltpu.VMEM((TXT, W), BF),
            pltpu.VMEM((HALF, HEAD_DIM), F32),
            pltpu.VMEM((2, HEAD_DIM, W), BF),
            pltpu.VMEM((HEAD_DIM, W), F32),
            pltpu.VMEM((TXT, W), F32),
            pltpu.VMEM((TXT, W), F32),
            pltpu.VMEM((2, HALF, W), F32),
            pltpu.VMEM((SLAB_Q + HALF, W), F32),
            pltpu.VMEM((2 * KEYS, W), F32),
            pltpu.VMEM((2 * KEYS, W), F32),
            pltpu.VMEM((2, KEYS, W), F32),
            pltpu.VMEM((KEYS, W), BF),
            pltpu.VMEM((KEYS, W), BF),
            pltpu.VMEM((NB, 96, W), BF),
            pltpu.VMEM((NB, 96, W), BF),
            pltpu.VMEM((NZ, 16, 256), BF),
            pltpu.VMEM((NZ, 16, 256), BF),
            pltpu.VMEM((2, NB, 32, W), BF),
            dma((4, NZ)), dma((NZ,)), dma((NZ,)), dma((NZ,)), dma((NZ,)),
            dma((2, NB)), dma((NB,)), dma((NB,)),
            dma((7,)), dma((7,)),
            dma((3, NZ)), dma((NZ,)), dma((NZ,)), dma((NZ,)),
            dma((NB,)), dma((NB,)), dma((NB,)), dma((NB,)),
        ],
        compiler_params=pltpu.CompilerParams(
            collective_id=0, has_side_effects=True, vmem_limit_bytes=48 * 1024 * 1024
        ),
        cost_estimate=pl.CostEstimate(
            flops=2_500_000_000, bytes_accessed=4_000_000, transcendentals=2_000_000
        ),
        name="joint_backward",
    )(
        slab_offsets, text_count, slab_query, slab_output, slab_cotangent, slab_logsum,
        image_keys, image_values, text_query, text_keys, text_values, text_output,
        text_cotangent, text_logsum, cos_t, sin_t,
    )


def solution(mesh):
    tokens = P(("rep", "blk", "head"), None)
    text = P("rep", "head")
    in_specs = (
        tokens, tokens, tokens, P(("rep", "blk"), "head"), tokens, tokens,
        text, text, text, text, text, text, P("rep"), P("rep"),
    )
    out_specs = (tokens, tokens, tokens, text, text, text)
    return jax.shard_map(
        on_device, mesh=mesh, in_specs=in_specs, out_specs=out_specs, check_vma=False
    )
```

```python
import jax
import jax.numpy as jnp
import numpy as np
from jax import lax
from jax.experimental import pallas as pl
from jax.experimental.pallas import tpu as pltpu
from jax.sharding import PartitionSpec as P

HEAD_DIM = 128
FACTOR = HEAD_DIM ** (-0.5)
NZ = 8
NX = 4
NB = NX * NX
HD = 3
W = HD * HEAD_DIM
ALL = NZ * W
TXT = 256
HALF = TXT // 2
ROWS = 64
KEYS = 256
SLAB_Q = NB * ROWS
STEP = 256
SILENT = 1e30
BF = jnp.bfloat16
F32 = jnp.float32
MESH = pl.DeviceIdType.MESH

TREE = (
    ((1, 0), (0, 0)),
    ((-1, 0), (0, 0)),
    ((0, 1), (0, 0)),
    ((0, -1), (0, 0)),
    ((1, 1), (1, 0)),
    ((-1, -1), (-1, 0)),
    ((1, -1), (0, -1)),
    ((-1, 1), (0, 1)),
    ((2, 0), (-1, 0)),
    ((0, 2), (0, -1)),
    ((2, 1), (1, 1)),
    ((2, -1), (1, -1)),
    ((1, 2), (1, 1)),
    ((-1, 2), (-1, 1)),
    ((2, 2), (-1, 2)),
)
NODE = [child for child, _ in TREE]
BELOW = {p: [k for k, (_, q) in enumerate(TREE) if q == p] for p in [(0, 0)] + NODE}
LEVELS = ((0, 1, 2, 3), (4, 5, 6, 7, 8, 9), (10, 11, 12, 13), (14,))
LEAVES = (14, 10, 12, 11, 8, 9, 5)
INNER = (13, 4, 6, 7, 0, 1, 2, 3)


def one_hop(step):
    return -1 if step in (-1, 3) else (1 if step in (1, -3) else 0 if step == 0 else -1)


def edge(k):
    (cx, cy), (px, py) = TREE[k]
    return one_hop(cx - px), one_hop(cy - py)


def tables():
    place = np.arange(512, dtype=np.float64)[:, None]
    frequency = 10000.0 ** (-np.arange(32, dtype=np.float64) / 32)
    angles = np.tile(place * frequency[None, :], (1, 4))
    sign = np.where(np.arange(128) < 64, -1.0, 1.0)
    return np.stack([np.cos(angles), np.sin(angles) * sign]).astype(np.float32)


def nt(a, b):
    return lax.dot_general(a, b, (((1,), (1,)), ((), ())), preferred_element_type=F32)


def nn(a, b):
    return lax.dot_general(a, b, (((1,), (0,)), ((), ())), preferred_element_type=F32)


def turn(x, cosine, sine):
    return x * cosine + pltpu.roll(x, 64, 1) * sine


def turn_back(x, cosine, sine):
    return x * cosine - pltpu.roll(x, 64, 1) * sine


def cols(n):
    return slice(n * HEAD_DIM, (n + 1) * HEAD_DIM)


def attend(keys, keys_t, values, queries, cotan, logsum, delta, mask=None):
    p = jnp.exp(nt(keys, queries) * FACTOR - logsum)
    if mask is not None:
        p = p * mask
    dv = nn(p.astype(BF), cotan)
    dp = nt(values, cotan)
    ds = (p * (dp - delta) * FACTOR).astype(BF)
    return nn(keys_t, ds).T, nn(ds, queries), dv


def kernel(
    off_ref, cnt_ref, sq_h, so_h, sg_h, sl_h, ik_h, iv_h, tq_h, tk_h, tv_h, to_h, tg_h, tl_h, tab_h,
    sqo, okv, txo,
    sq, so, sg, sl, ik, tq, tk, tv, to, tg, tl, tab,
    qgs, dls, qgr, dlr, kvs, kv, qg, st, stp, tkr, tst, qtk, dqt, dkvt, xt,
    dq, dkv, xk, dkvs, ts_s, ts_r, rs_s, rs_r, sqs, sqr, tx,
    s_in, s_z, r_zqg, r_zd, s_kv, r_kv, s_xy, r_xy, s_sib, r_sib, s_skv, r_skv, s_sd, r_sd,
    s_o, r_o, s_oq, r_oq, s_ts, r_ts, s_rs, r_rs, s_tx, r_tx,
):
    blk = lax.axis_index("blk")
    h = lax.axis_index("head")
    c = lax.rem(blk, 2)
    b = blk // 2
    bx = b // NX
    by = lax.rem(b, NX)
    lane = lax.broadcasted_iota(jnp.int32, (1, HEAD_DIM), 1)
    first = lax.rem(lane, 64) < 32
    sib = {"blk": 2 * b + 1 - c}

    def zdev(t):
        return lax.rem(h + t, NZ)

    def chip(dx, dy):
        return lax.rem(bx + dx + NX, NX) * NX + lax.rem(by + dy + NX, NX)

    def on_chip(e):
        return {"blk": 2 * e + c}

    def remote(src, dst, ss, rs, dev):
        return pltpu.make_async_remote_copy(
            src_ref=src, dst_ref=dst, send_sem=ss, recv_sem=rs, device_id=dev, device_id_type=MESH
        )

    def rows_of(e, count):
        return pl.ds(pl.multiple_of(e * count, count), count)

    def wide(d):
        return rows_of(d, W)

    def head_cols(d, j):
        return pl.ds(pl.multiple_of(d * W + j * HEAD_DIM, HEAD_DIM), HEAD_DIM)

    def fetch(i, src, dst):
        copy = pltpu.make_async_copy(src, dst, s_in.at[i])
        copy.start()
        return copy

    f_tab = fetch(0, tab_h, tab)
    f_slab = [fetch(1, sq_h, sq), fetch(2, sg_h, sg), fetch(3, so_h, so)]
    f_k = fetch(4, ik_h, ik)
    f_v = fetch(5, iv_h, kvs.at[1])
    f_text = [
        fetch(6, tq_h, tq), fetch(7, tg_h, tg), fetch(8, to_h, to), fetch(9, tk_h, tk),
        fetch(10, tv_h, tv), fetch(11, tl_h, tl), fetch(12, sl_h, sl),
    ]

    bar = pltpu.get_barrier_semaphore()

    def greet_z(t, carry):
        pl.semaphore_signal(bar, inc=1, device_id={"head": zdev(t)}, device_id_type=MESH)
        return carry

    lax.fori_loop(1, NZ, greet_z, 0)
    for dx, dy in ((1, 0), (-1, 0), (0, 1), (0, -1)):
        pl.semaphore_signal(bar, inc=1, device_id=on_chip(chip(dx, dy)), device_id_type=MESH)
    pl.semaphore_signal(bar, inc=1, device_id=sib, device_id_type=MESH)

    cos_t, sin_t = tab.at[0], tab.at[1]

    def angles(row, start, count):
        ct = cos_t[pl.ds(start, count), :]
        sn = sin_t[pl.ds(start, count), :]
        cr = cos_t[pl.ds(row, 1), :]
        sr = sin_t[pl.ds(row, 1), :]
        return jnp.where(first, cr, ct), jnp.where(first, sr, sn)

    place = off_ref[0] + blk
    row_at = lax.broadcasted_iota(jnp.int32, (32, 1), 0) == place // 4
    col_at = lax.rem(place, 4)

    def slab_angles(start, count):
        result = []
        for table in (cos_t, sin_t):
            row = jnp.sum(jnp.where(row_at, table[:32, :], 0.0), axis=0, keepdims=True)
            col = table[pl.ds(start, count), :]
            for i in range(1, 4):
                col = jnp.where(col_at == i, table[pl.ds(64 * i + start, count), :], col)
            result.append(jnp.where(first, row, col))
        return result

    f_tab.wait()
    for copy in f_slab:
        copy.wait()
    cq, sn_q = slab_angles(pl.multiple_of(8 * h, 8), 8)
    for d in range(NZ):
        acc = jnp.zeros((8, HEAD_DIM), F32)
        for j in range(HD):
            n = d * HD + j
            g = sg[:, cols(n)].astype(F32)
            q = turn(sq[:, cols(n)].astype(F32), cq, sn_q)
            qgs[:, cols(n)] = jnp.concatenate([q, g], axis=0).astype(BF)
            own = jnp.sum(g * so[:, cols(n)].astype(F32), axis=1, keepdims=True)
            acc = jnp.where(lane == j, own, acc)
        dls[d] = acc
    pl.semaphore_wait(bar, NZ + NX)

    def z_qg(t, d):
        return remote(qgs.at[:, wide(d)], qgr.at[h], s_z.at[0, t], r_zqg.at[h], {"head": d})

    def z_dl(t, d):
        return remote(dls.at[d], dlr.at[h], s_z.at[1, t], r_zd.at[h], {"head": d})

    def key_rows(s):
        return pl.ds(pl.multiple_of(c * KEYS + s * 32, 32), 32)

    def z_kv(j, t, d):
        return remote(
            kvs.at[:, :, head_cols(d, j)], kv.at[:, key_rows(h), cols(j)],
            s_kv.at[j, t], r_kv.at[j, h], {"head": d},
        )

    def go_qg(t, carry):
        z_qg(t, zdev(t)).start()
        z_dl(t, zdev(t)).start()
        return carry

    lax.fori_loop(1, NZ, go_qg, 0)
    f_k.wait()
    f_v.wait()
    ck, sn_k = angles(blk, pl.multiple_of(32 * h, 32), 32)
    for j in range(HD):
        for d in range(NZ):
            n = d * HD + j
            kvs[0, :, cols(n)] = turn(ik[:, cols(n)].astype(F32), ck, sn_k).astype(BF)

        def go_kv(t, carry, j=j):
            z_kv(j, t, zdev(t)).start()
            return carry

        lax.fori_loop(1, NZ, go_kv, 0)
    kv[:, key_rows(h), :] = kvs[:, :, wide(h)]
    qgr[h] = qgs[:, wide(h)]
    dlr[h] = dls[h]

    for copy in f_text:
        copy.wait()
    half = rows_of(c, HALF)
    text_at = pl.ds(pl.multiple_of(TXT + HALF * c, HALF), HALF)
    ct = cos_t[text_at, :]
    sn = sin_t[text_at, :]
    acc = jnp.zeros((HALF, HEAD_DIM), F32)
    for j in range(HD):
        g = tg[half, cols(j)]
        qg[0, SLAB_Q:, cols(j)] = turn(tq[half, cols(j)].astype(F32), ct, sn).astype(BF)
        qg[1, SLAB_Q:, cols(j)] = g
        own = jnp.sum(g.astype(F32) * to[half, cols(j)].astype(F32), axis=1, keepdims=True)
        acc = jnp.where(lane == j, own, acc)
        tkr[:, cols(j)] = turn(tk[:, cols(j)].astype(F32), cos_t[TXT:, :], sin_t[TXT:, :]).astype(BF)
    stp[:, SLAB_Q:] = acc.T[:8, :]
    stp[HD : 2 * HD, SLAB_Q:] = tl[:, half]

    def wait_qg(t, carry):
        s = zdev(t)
        remote(qgs.at[:, wide(s)], qgr.at[s], s_z.at[0, t], r_zqg.at[s], {"head": s}).wait_recv()
        remote(dls.at[s], dlr.at[s], s_z.at[1, t], r_zd.at[s], {"head": s}).wait_recv()
        return carry

    lax.fori_loop(1, NZ, wait_qg, 0)
    both = qgr[...].astype(F32)
    own_q = both[:, :8, :].reshape(ROWS, W).astype(BF)
    own_g = both[:, 8:, :].reshape(ROWS, W).astype(BF)
    my_rows = rows_of(b, ROWS)
    qg[0, my_rows, :] = own_q
    qg[1, my_rows, :] = own_g
    odd = lax.rem(b, 2) == 1
    delta = dlr[...].reshape(ROWS, HEAD_DIM)
    blank = jnp.zeros_like(delta)
    spread = jnp.concatenate([jnp.where(odd, blank, delta), jnp.where(odd, delta, blank)], axis=0)
    here = (lane // 64) == lax.rem(b, 2)
    logs = jnp.concatenate([sl[...], sl[...]], axis=1)
    st[b] = spread.T[:8, :]
    st[b, HD : 2 * HD, :] = jnp.where(here, logs, 0.0)

    def ag(k, s, e):
        return (
            remote(qg.at[:, rows_of(s, ROWS), :], qg.at[:, rows_of(s, ROWS), :], s_xy.at[0, k], r_xy.at[0, k], on_chip(e)),
            remote(st.at[s], st.at[s], s_xy.at[1, k], r_xy.at[1, k], on_chip(e)),
        )

    def ag_send(k):
        (_, _), (px, py) = TREE[k]
        dx, dy = edge(k)
        return ag(k, chip(-px, -py), chip(dx, dy))

    def ag_start(node):
        for k in BELOW[node]:
            for copy in ag_send(k):
                copy.start()

    def ag_level(level):
        for k in LEVELS[level]:
            cx, cy = NODE[k]
            for copy in ag(k, chip(-cx, -cy), b):
                copy.wait_recv()
            ag_start(NODE[k])

    ag_start((0, 0))

    pair = pl.multiple_of(16 * (b // 2), 16)
    qtk[0, :ROWS, :] = own_q
    qtk[1, :ROWS, :] = own_g
    for i in range(2):
        qtk[i, ROWS : ROWS + 16, :] = qg[i, pl.ds(SLAB_Q + pair, 16), :]
        qtk[i, ROWS + 16 :, :] = jnp.zeros((HEAD_DIM - ROWS - 16, W), BF)
    own_st = st[b]
    own_st = jnp.where(odd, pltpu.roll(own_st, 64, 1), own_st)
    text_st = pltpu.roll(stp[:, SLAB_Q:], lax.rem(ROWS - pair + HEAD_DIM, HEAD_DIM), 1)
    mine_at = lane // 8 == ROWS // 8 + lax.rem(b, 2)
    stat_row = lax.broadcasted_iota(jnp.int32, (8, 1), 0)
    silent = jnp.where(jnp.logical_and(stat_row >= HD, stat_row < 2 * HD), SILENT, 0.0)
    tst[...] = jnp.where(lane < ROWS, own_st, jnp.where(mine_at, text_st, silent))
    key_index = lax.broadcasted_iota(jnp.int32, (TXT, 1), 0)
    mask = (key_index < cnt_ref[0]).astype(F32)

    def text_keys(j):
        keys = tkr[:, cols(j)]
        one_q, one_k, one_v = attend(
            keys, keys.T, tv[:, cols(j)], qtk[0, :, cols(j)], qtk[1, :, cols(j)],
            tst[HD + j : HD + j + 1, :], tst[j : j + 1, :], mask,
        )
        dqt[:, cols(j)] = one_q
        dkvt[0, :, cols(j)] = one_k
        dkvt[1, :, cols(j)] = one_v

    text_keys(0)
    ag_level(0)
    text_keys(1)
    text_keys(2)
    other = rows_of(1 - c, HALF)
    sib_t = remote(dkvt.at[:, other, :], xt, s_sib.at[0], r_sib.at[0], sib)
    sib_t.start()
    ag_level(1)

    mine = rows_of(c, KEYS)
    theirs = rows_of(1 - c, KEYS)

    def sib_kv(j, rows):
        part = kv.at[:, rows, cols(j)]
        return remote(part, part, s_skv.at[j], r_skv.at[j], sib)

    def share_kv(j):
        def wait_kv(t, carry):
            s = zdev(t)
            remote(
                kvs.at[:, :, head_cols(s, j)], kv.at[:, key_rows(s), cols(j)],
                s_kv.at[j, t], r_kv.at[j, s], {"head": s},
            ).wait_recv()
            return carry

        lax.fori_loop(1, NZ, wait_kv, 0)
        sib_kv(j, mine).start()

    share_kv(0)
    ag_level(2)
    ag_level(3)
    for i in range(NB // 2):
        stp[:, cols(i)] = st[2 * i] + st[2 * i + 1]
    share_kv(1)

    def image_keys(j, keys_t, rows, start):
        one_q, one_k, one_v = attend(
            kv[0, :, cols(j)], keys_t, kv[1, :, cols(j)], qg[0, rows, cols(j)], qg[1, rows, cols(j)],
            stp[HD + j : HD + j + 1, rows], stp[j : j + 1, rows],
        )
        dq[rows, cols(j)] = one_q
        if start:
            dkv[0, :, cols(j)] = one_k
            dkv[1, :, cols(j)] = one_v
        else:
            dkv[0, :, cols(j)] += one_k
            dkv[1, :, cols(j)] += one_v

    def slab_queries(j, keys_t):
        for i in range(SLAB_Q // STEP):
            image_keys(j, keys_t, slice(i * STEP, (i + 1) * STEP), False)

    def sib_d(j):
        return remote(dkv.at[:, theirs, cols(j)], xk.at[:, :, cols(j)], s_sd.at[j], r_sd.at[j], sib)

    ck, sn_k = angles(blk, 0, KEYS)

    def token_rows(s):
        return rows_of(s, 32)

    def z_out(j, t, d):
        return remote(
            dkvs.at[:, token_rows(d), cols(j)], okv.at[:, :, head_cols(h, j)],
            s_o.at[j, t], r_o.at[j, h], {"head": d},
        )

    def finish_kv(j):
        sib_d(j).wait()
        dkvs[0, :, cols(j)] = turn_back(dkv[0, mine, cols(j)] + xk[0, :, cols(j)], ck, sn_k).astype(BF)
        dkvs[1, :, cols(j)] = (dkv[1, mine, cols(j)] + xk[1, :, cols(j)]).astype(BF)

        def go_out(t, carry):
            z_out(j, t, zdev(t)).start()
            return carry

        lax.fori_loop(1, NZ, go_out, 0)
        okv[:, :, head_cols(h, j)] = dkvs[:, token_rows(h), cols(j)]

    def make_sum(own, sent, got, ss, rs):
        def send(k):
            dx, dy = edge(k)
            return remote(sent.at[k], got.at[k], ss.at[k], rs.at[k], on_chip(chip(-dx, -dy)))

        def gather(node):
            value = own(chip(-node[0], -node[1]))
            for k in BELOW[node]:
                send(k).wait_recv()
                value = value + got[k].astype(F32)
            return value

        def pass_on(k):
            sent[k] = gather(NODE[k]).astype(BF)
            send(k).start()

        return send, gather, pass_on

    def own_text(e):
        at = rows_of(e, 8)
        at_half = pl.ds(pl.multiple_of(HALF * c + e * 8, 8), 8)
        return jnp.concatenate(
            [
                dq[pl.ds(pl.multiple_of(SLAB_Q + e * 8, 8), 8), :],
                dkvt[0, at_half, :] + xt[0, at, :],
                dkvt[1, at_half, :] + xt[1, at, :],
                jnp.zeros((8, W), F32),
            ],
            axis=0,
        )

    def own_slab(e):
        return dq[rows_of(e, ROWS), :]

    ts_send, ts_gather, ts_pass = make_sum(own_text, ts_s, ts_r, s_ts, r_ts)
    rs_send, rs_gather, rs_pass = make_sum(own_slab, rs_s, rs_r, s_rs, r_rs)

    for j in range(HD):
        sib_kv(j, theirs).wait_recv()
        keys_t = kv[0, :, cols(j)].T
        image_keys(j, keys_t, slice(SLAB_Q, SLAB_Q + HALF), True)
        if j == HD - 1:
            sib_t.wait()
            for k in LEAVES:
                ts_pass(k)
        slab_queries(j, keys_t)
        sib_d(j).start()
        if j == 0:
            share_kv(2)
        if j > 0:
            finish_kv(j - 1)
    for k in LEAVES:
        rs_pass(k)
    ts_pass(INNER[0])
    finish_kv(HD - 1)
    rs_pass(INNER[0])
    for k in INNER[1:]:
        ts_pass(k)
        rs_pass(k)

    total = ts_gather((0, 0))
    extra = jnp.where(odd, dqt[ROWS + 8 : ROWS + 16, :], dqt[ROWS : ROWS + 8, :])
    text_q = total[:8, :] + extra
    text_k = total[8:16, :]
    text_v = total[16:24, :]
    own_at = pl.ds(pl.multiple_of(TXT + HALF * c + 8 * b, 8), 8)
    ct = cos_t[own_at, :]
    sn = sin_t[own_at, :]
    for j in range(HD):
        tx[c, b, :, cols(j)] = jnp.concatenate(
            [
                turn_back(text_q[:, cols(j)], ct, sn),
                turn_back(text_k[:, cols(j)], ct, sn),
                text_v[:, cols(j)],
                jnp.zeros((8, HEAD_DIM), F32),
            ],
            axis=0,
        ).astype(BF)

    def tx_copy(k, s, e):
        return remote(tx.at[c, s], tx.at[c, s], s_tx.at[k], r_tx.at[k], on_chip(e))

    def tx_send(k):
        (_, _), (px, py) = TREE[k]
        dx, dy = edge(k)
        return tx_copy(k, chip(-px, -py), chip(dx, dy))

    def tx_start(node):
        for k in BELOW[node]:
            tx_send(k).start()

    def tx_level(level):
        for k in LEVELS[level]:
            cx, cy = NODE[k]
            tx_copy(k, chip(-cx, -cy), b).wait_recv()
            tx_start(NODE[k])

    tx_start((0, 0))
    slab_total = rs_gather((0, 0)) + dqt[:ROWS, :]
    cq, sn_q = slab_angles(0, ROWS)
    parts = [turn_back(slab_total[:, cols(j)], cq, sn_q).reshape(NZ, 8, HEAD_DIM) for j in range(HD)]
    sqs[:, :, :HEAD_DIM] = jnp.concatenate([parts[0], parts[2]], axis=1).astype(BF)
    sqs[:, :, HEAD_DIM:] = jnp.concatenate([parts[1], jnp.zeros_like(parts[1])], axis=1).astype(BF)

    def out_q(t, d):
        return remote(sqs.at[d], sqr.at[h], s_oq.at[t], r_oq.at[h], {"head": d})

    def go_oq(t, carry):
        out_q(t, zdev(t)).start()
        return carry

    lax.fori_loop(1, NZ, go_oq, 0)
    sqr[h] = sqs[h]
    for level in range(4):
        tx_level(level)
    sib_tx = remote(tx.at[c], tx.at[c], s_sib.at[1], r_sib.at[1], sib)
    sib_tx.start()

    def wait_oq(t, carry):
        s = zdev(t)
        remote(sqs.at[s], sqr.at[s], s_oq.at[t], r_oq.at[s], {"head": s}).wait_recv()
        return carry

    lax.fori_loop(1, NZ, wait_oq, 0)
    for s in range(NZ):
        piece = sqr[s].astype(F32)
        sqo[:, s * W : s * W + 128] = piece[:8, :128].astype(BF)
        sqo[:, s * W + 128 : s * W + 256] = piece[:8, 128:].astype(BF)
        sqo[:, s * W + 256 : s * W + 384] = piece[8:, :128].astype(BF)
    remote(tx.at[1 - c], tx.at[1 - c], s_sib.at[1], r_sib.at[1], sib).wait_recv()
    for core in range(2):
        block = tx[core].astype(F32)
        rows = slice(core * HALF, (core + 1) * HALF)
        for i in range(3):
            txo[i, rows, :] = block[:, 8 * i : 8 * i + 8, :].reshape(HALF, W).astype(BF)
    for j in range(HD):

        def wait_out(t, carry, j=j):
            s = zdev(t)
            remote(
                dkvs.at[:, token_rows(s), cols(j)], okv.at[:, :, head_cols(s, j)],
                s_o.at[j, t], r_o.at[j, s], {"head": s},
            ).wait_recv()
            return carry

        lax.fori_loop(1, NZ, wait_out, 0)

    def drain_z(t, carry):
        d = zdev(t)
        z_qg(t, d).wait_send()
        z_dl(t, d).wait_send()
        out_q(t, d).wait_send()
        for j in range(HD):
            z_kv(j, t, d).wait_send()
            z_out(j, t, d).wait_send()
        return carry

    lax.fori_loop(1, NZ, drain_z, 0)
    for k in range(len(TREE)):
        for copy in ag_send(k):
            copy.wait_send()
        ts_send(k).wait_send()
        rs_send(k).wait_send()
        tx_send(k).wait_send()
    for j in range(HD):
        sib_kv(j, mine).wait_send()
    sib_tx.wait_send()


def deliver(sqo, okv, txo, sqg, ikg, ivg, tqg, tkg, tvg, sems):
    pairs = (
        (sqo, sqg), (okv.at[0], ikg), (okv.at[1], ivg),
        (txo.at[0], tqg), (txo.at[1], tkg), (txo.at[2], tvg),
    )
    copies = [pltpu.make_async_copy(a, b, sems.at[i]) for i, (a, b) in enumerate(pairs)]
    for copy in copies:
        copy.start()
    for copy in copies:
        copy.wait()


def on_device(
    slab_query, slab_output, slab_cotangent, slab_logsum, image_keys, image_values,
    text_query, text_keys, text_values, text_output, text_cotangent, text_logsum,
    text_count, slab_offsets,
):
    vmem = pl.BlockSpec(memory_space=pltpu.VMEM)
    smem = pl.BlockSpec(memory_space=pltpu.SMEM)
    hbm = pl.BlockSpec(memory_space=pltpu.HBM)
    dma = pltpu.SemaphoreType.DMA
    edges = len(TREE)
    slab = pltpu.VMEM((8, ALL), BF)
    text = pltpu.VMEM((TXT, W), BF)
    sqo, okv, txo = pl.pallas_call(
        kernel,
        out_shape=[
            jax.ShapeDtypeStruct((8, ALL), BF),
            jax.ShapeDtypeStruct((2, 32, ALL), BF),
            jax.ShapeDtypeStruct((3, TXT, W), BF),
        ],
        in_specs=[smem, smem] + [hbm] * 13,
        out_specs=[vmem] * 3,
        scratch_shapes=[
            slab, slab, slab,
            pltpu.VMEM((HD, ROWS), F32),
            pltpu.VMEM((32, ALL), BF),
            text, text, text, text, text,
            pltpu.VMEM((HD, TXT), F32),
            pltpu.VMEM((2, 512, HEAD_DIM), F32),
            pltpu.VMEM((16, ALL), BF),
            pltpu.VMEM((NZ, 8, HEAD_DIM), F32),
            pltpu.VMEM((NZ, 16, W), BF),
            pltpu.VMEM((NZ, 8, HEAD_DIM), F32),
            pltpu.VMEM((2, 32, ALL), BF),
            pltpu.VMEM((2, 2 * KEYS, W), BF),
            pltpu.VMEM((2, SLAB_Q + HALF, W), BF),
            pltpu.VMEM((NB, 8, HEAD_DIM), F32),
            pltpu.VMEM((8, SLAB_Q + HALF), F32),
            pltpu.VMEM((TXT, W), BF),
            pltpu.VMEM((8, HEAD_DIM), F32),
            pltpu.VMEM((2, HEAD_DIM, W), BF),
            pltpu.VMEM((HEAD_DIM, W), F32),
            pltpu.VMEM((2, TXT, W), F32),
            pltpu.VMEM((2, HALF, W), F32),
            pltpu.VMEM((SLAB_Q + HALF, W), F32),
            pltpu.VMEM((2, 2 * KEYS, W), F32),
            pltpu.VMEM((2, KEYS, W), F32),
            pltpu.VMEM((2, KEYS, W), BF),
            pltpu.VMEM((edges, 32, W), BF),
            pltpu.VMEM((edges, 32, W), BF),
            pltpu.VMEM((edges, ROWS, W), BF),
            pltpu.VMEM((edges, ROWS, W), BF),
            pltpu.VMEM((NZ, 16, 256), BF),
            pltpu.VMEM((NZ, 16, 256), BF),
            pltpu.VMEM((2, NB, 32, W), BF),
            dma((13,)),
            dma((2, NZ)), dma((NZ,)), dma((NZ,)),
            dma((HD, NZ)), dma((HD, NZ)),
            dma((2, edges)), dma((2, edges)),
            dma((2,)), dma((2,)),
            dma((HD,)), dma((HD,)), dma((HD,)), dma((HD,)),
            dma((HD, NZ)), dma((HD, NZ)),
            dma((NZ,)), dma((NZ,)),
            dma((edges,)), dma((edges,)),
            dma((edges,)), dma((edges,)),
            dma((edges,)), dma((edges,)),
        ],
        compiler_params=pltpu.CompilerParams(
            collective_id=0, has_side_effects=True, vmem_limit_bytes=48 * 1024 * 1024
        ),
        cost_estimate=pl.CostEstimate(
            flops=2_500_000_000, bytes_accessed=4_000_000, transcendentals=2_000_000
        ),
        name="joint_backward",
    )(
        slab_offsets, text_count, slab_query, slab_output, slab_cotangent, slab_logsum.T,
        image_keys, image_values, text_query, text_keys, text_values, text_output,
        text_cotangent, text_logsum.T, tables(),
    )
    shapes = [
        jax.ShapeDtypeStruct(x.shape, BF)
        for x in (slab_query, image_keys, image_values, text_query, text_keys, text_values)
    ]
    anywhere = pl.BlockSpec(memory_space=pl.ANY)
    return pl.pallas_call(
        deliver,
        out_shape=shapes,
        in_specs=[anywhere] * 3,
        out_specs=[anywhere] * 6,
        scratch_shapes=[dma((6,))],
        name="deliver",
    )(sqo, okv, txo)


def solution(mesh):
    tokens = P(("rep", "blk", "head"), None)
    text = P("rep", "head")
    in_specs = (
        tokens, tokens, tokens, P(("rep", "blk"), "head"), tokens, tokens,
        text, text, text, text, text, text, P("rep"), P("rep"),
    )
    out_specs = (tokens, tokens, tokens, text, text, text)
    return jax.shard_map(
        on_device, mesh=mesh, in_specs=in_specs, out_specs=out_specs, check_vma=False
    )
```

```python
import jax
import jax.numpy as jnp
import numpy as np
from jax import lax
from jax.experimental import pallas as pl
from jax.experimental.pallas import tpu as pltpu
from jax.sharding import PartitionSpec as P

HEAD_DIM = 128
FACTOR = HEAD_DIM ** (-0.5)
NZ = 8
NX = 4
NB = NX * NX
HD = 3
W = HD * HEAD_DIM
ALL = NZ * W
TXT = 256
HALF = TXT // 2
ROWS = 64
KEYS = 256
SLAB_Q = NB * ROWS
STEP = 256
SILENT = 1e30
BF = jnp.bfloat16
F32 = jnp.float32
MESH = pl.DeviceIdType.MESH

TREE = (
    ((1, 0), (0, 0), (1, 0)),
    ((-1, 0), (0, 0), (-1, 0)),
    ((0, 1), (0, 0), (0, 1)),
    ((0, -1), (0, 0), (0, -1)),
    ((1, 1), (0, 0), (1, 1)),
    ((1, -1), (0, 0), (1, -1)),
    ((-1, 1), (0, 0), (-1, 1)),
    ((-1, -1), (0, 0), (-1, -1)),
    ((2, 0), (-1, 0), (-1, 0)),
    ((0, 2), (0, -1), (0, -1)),
    ((2, 1), (1, 1), (1, 0)),
    ((2, -1), (-1, -1), (-1, 0)),
    ((1, 2), (1, 1), (0, 1)),
    ((-1, 2), (-1, 1), (0, 1)),
    ((2, 2), (1, -1), (1, -1)),
)
EDGES = len(TREE)
BELOW = {child: [k for k, e in enumerate(TREE) if e[1] == child] for child, _, _ in TREE}
RELAYS = (1, 3, 4, 7, 6, 5)
LEAVES = (14, 8, 9, 10, 11, 12, 13, 0, 2)
AROUND = [e[2] for e in TREE[:8]]


def tables():
    place = np.arange(512, dtype=np.float64)[:, None]
    frequency = 10000.0 ** (-np.arange(32, dtype=np.float64) / 32)
    angles = np.tile(place * frequency[None, :], (1, 4))
    sign = np.where(np.arange(128) < 64, -1.0, 1.0)
    return np.stack([np.cos(angles), np.sin(angles) * sign]).astype(np.float32)


def nt(a, b):
    return lax.dot_general(a, b, (((1,), (1,)), ((), ())), preferred_element_type=F32)


def nn(a, b):
    return lax.dot_general(a, b, (((1,), (0,)), ((), ())), preferred_element_type=F32)


def turn(x, cosine, sine):
    return x * cosine + pltpu.roll(x, 64, 1) * sine


def turn_back(x, cosine, sine):
    return x * cosine - pltpu.roll(x, 64, 1) * sine


def cols(n):
    return slice(n * HEAD_DIM, (n + 1) * HEAD_DIM)


def attend(keys, keys_t, values, queries, cotan, logsum, delta, mask=None):
    p = jnp.exp(nt(keys, queries) * FACTOR - logsum)
    if mask is not None:
        p = p * mask
    dv = nn(p.astype(BF), cotan)
    dp = nt(values, cotan)
    ds = (p * (dp - delta) * FACTOR).astype(BF)
    return nn(keys_t, ds).T, nn(ds, queries), dv


def kernel(
    off_ref, cnt_ref, sq_h, so_h, sg_h, sl_h, ik_h, iv_h, tq_h, tk_h, tv_h, to_h, tg_h, tl_h, tab_h,
    sqo, okv, txo,
    sq, so, sg, sl, ik, iv, tq, tk, tv, to, tg, tl, tab,
    qgs, dls, qgr, dlr, kvs, kv, qg, st, stp, tkr, tst, qtk, dqt, dkvt, xt,
    dq, dkv, xk, dkvs, rs_s, rs_r, sqs, sqr, tx,
    s_in, s_z, r_zqg, r_zd, s_kv, r_kv, s_xy, r_xy, s_st, r_st, s_sib, r_sib, s_skv, r_skv, s_sd, r_sd,
    s_o, r_o, s_oq, r_oq, s_rs, r_rs, s_tx, r_tx,
):
    blk = lax.axis_index("blk")
    h = lax.axis_index("head")
    c = lax.rem(blk, 2)
    b = blk // 2
    bx = b // NX
    by = lax.rem(b, NX)
    lane = lax.broadcasted_iota(jnp.int32, (1, HEAD_DIM), 1)
    first = lax.rem(lane, 64) < 32
    sib = {"blk": 2 * b + 1 - c}

    def zdev(t):
        return lax.rem(h + t, NZ)

    def chip(dx, dy):
        return lax.rem(bx + dx + NX, NX) * NX + lax.rem(by + dy + NX, NX)

    def on_chip(e):
        return {"blk": 2 * e + c}

    def remote(src, dst, ss, rs, dev):
        return pltpu.make_async_remote_copy(
            src_ref=src, dst_ref=dst, send_sem=ss, recv_sem=rs, device_id=dev, device_id_type=MESH
        )

    def rows_of(e, count):
        return pl.ds(pl.multiple_of(e * count, count), count)

    def wide(d):
        return rows_of(d, W)

    def fetch(i, src, dst):
        copy = pltpu.make_async_copy(src, dst, s_in.at[i])
        copy.start()
        return copy

    f_slab = [fetch(1, sq_h, sq), fetch(2, sg_h, sg), fetch(3, so_h, so)]
    f_tab = fetch(0, tab_h, tab)
    f_k = fetch(4, ik_h, ik)
    f_v = fetch(5, iv_h, iv)
    f_text = [
        fetch(6, tq_h, tq), fetch(7, tg_h, tg), fetch(8, to_h, to), fetch(9, tk_h, tk),
        fetch(10, tv_h, tv), fetch(11, tl_h, tl), fetch(12, sl_h, sl),
    ]

    bar = pltpu.get_barrier_semaphore()

    def greet_z(t, carry):
        pl.semaphore_signal(bar, inc=1, device_id={"head": zdev(t)}, device_id_type=MESH)
        return carry

    lax.fori_loop(1, NZ, greet_z, 0)
    for dx, dy in AROUND:
        pl.semaphore_signal(bar, inc=1, device_id=on_chip(chip(dx, dy)), device_id_type=MESH)
    pl.semaphore_signal(bar, inc=1, device_id=sib, device_id_type=MESH)

    cos_t, sin_t = tab.at[0], tab.at[1]

    def angles(row, start, count):
        ct = cos_t[pl.ds(start, count), :]
        sn = sin_t[pl.ds(start, count), :]
        cr = cos_t[pl.ds(row, 1), :]
        sr = sin_t[pl.ds(row, 1), :]
        return jnp.where(first, cr, ct), jnp.where(first, sr, sn)

    place = off_ref[0] + blk
    row_at = lax.broadcasted_iota(jnp.int32, (32, 1), 0) == place // 4
    col_at = lax.rem(place, 4)

    def slab_angles(start, count):
        result = []
        for table in (cos_t, sin_t):
            row = jnp.sum(jnp.where(row_at, table[:32, :], 0.0), axis=0, keepdims=True)
            col = table[pl.ds(start, count), :]
            for i in range(1, 4):
                col = jnp.where(col_at == i, table[pl.ds(64 * i + start, count), :], col)
            result.append(jnp.where(first, row, col))
        return result

    f_tab.wait()
    for copy in f_slab:
        copy.wait()
    cq, sn_q = slab_angles(pl.multiple_of(8 * h, 8), 8)
    for d in range(NZ):
        acc = jnp.zeros((8, HEAD_DIM), F32)
        for j in range(HD):
            n = d * HD + j
            g = sg[:, cols(n)].astype(F32)
            q = turn(sq[:, cols(n)].astype(F32), cq, sn_q)
            qgs[d, :, cols(j)] = jnp.concatenate([q, g], axis=0).astype(BF)
            own = jnp.sum(g * so[:, cols(n)].astype(F32), axis=1, keepdims=True)
            acc = jnp.where(lane == j, own, acc)
        dls[d] = acc
    pl.semaphore_wait(bar, NZ + len(AROUND))

    def z_qg(t, d):
        return remote(qgs.at[d], qgr.at[h], s_z.at[0, t], r_zqg.at[h], {"head": d})

    def z_dl(t, d):
        return remote(dls.at[d], dlr.at[h], s_z.at[1, t], r_zd.at[h], {"head": d})

    def key_rows(s):
        return pl.ds(pl.multiple_of(c * KEYS + s * 32, 32), 32)

    def z_kv(j, t, d):
        return remote(
            kvs.at[d * HD + j], kv.at[j, :, key_rows(h), :], s_kv.at[j, t], r_kv.at[j, h], {"head": d}
        )

    def go_qg(t, carry):
        z_qg(t, zdev(t)).start()
        z_dl(t, zdev(t)).start()
        return carry

    lax.fori_loop(1, NZ, go_qg, 0)
    f_k.wait()
    f_v.wait()
    ck, sn_k = angles(blk, pl.multiple_of(32 * h, 32), 32)
    for j in range(HD):
        for d in range(NZ):
            n = d * HD + j
            kvs[n, 0] = turn(ik[:, cols(n)].astype(F32), ck, sn_k).astype(BF)
            kvs[n, 1] = iv[:, cols(n)]

        def go_kv(t, carry, j=j):
            z_kv(j, t, zdev(t)).start()
            return carry

        lax.fori_loop(1, NZ, go_kv, 0)
        kv[j, :, key_rows(h), :] = kvs[h * HD + j]
    qgr[h] = qgs[h]
    dlr[h] = dls[h]

    for copy in f_text:
        copy.wait()
    half = rows_of(c, HALF)
    text_at = pl.ds(pl.multiple_of(TXT + HALF * c, HALF), HALF)
    ct = cos_t[text_at, :]
    sn = sin_t[text_at, :]
    acc = jnp.zeros((HALF, HEAD_DIM), F32)
    for j in range(HD):
        g = tg[half, cols(j)]
        qg[j, 0, SLAB_Q:, :] = turn(tq[half, cols(j)].astype(F32), ct, sn).astype(BF)
        qg[j, 1, SLAB_Q:, :] = g
        own = jnp.sum(g.astype(F32) * to[half, cols(j)].astype(F32), axis=1, keepdims=True)
        acc = jnp.where(lane == j, own, acc)
        tkr[j] = turn(tk[:, cols(j)].astype(F32), cos_t[TXT:, :], sin_t[TXT:, :]).astype(BF)
    stp[:, SLAB_Q:] = acc.T[:8, :]
    stp[HD : 2 * HD, SLAB_Q:] = tl[:, half]

    def wait_qg(t, carry):
        s = zdev(t)
        remote(qgs.at[s], qgr.at[s], s_z.at[0, t], r_zqg.at[s], {"head": s}).wait_recv()
        remote(dls.at[s], dlr.at[s], s_z.at[1, t], r_zd.at[s], {"head": s}).wait_recv()
        return carry

    lax.fori_loop(1, NZ, wait_qg, 0)
    my_rows = rows_of(b, ROWS)
    odd = lax.rem(b, 2) == 1
    delta = dlr[...].reshape(ROWS, HEAD_DIM)
    blank = jnp.zeros_like(delta)
    spread = jnp.concatenate([jnp.where(odd, blank, delta), jnp.where(odd, delta, blank)], axis=0)
    here = (lane // 64) == lax.rem(b, 2)
    logs = jnp.concatenate([sl[...], sl[...]], axis=1)
    st[b] = spread.T[:8, :]
    st[b, HD : 2 * HD, :] = jnp.where(here, logs, 0.0)

    def ag(j, k, s, e):
        block = qg.at[j, :, rows_of(s, ROWS), :]
        return remote(block, block, s_xy.at[j, k], r_xy.at[j, k], on_chip(e))

    def ag_st(k, s, e):
        return remote(st.at[s], st.at[s], s_st.at[k], r_st.at[k], on_chip(e))

    def source(k):
        return chip(-TREE[k][0][0], -TREE[k][0][1])

    def from_parent(k, copy):
        _, (px, py), (dx, dy) = TREE[k]
        return copy(k, chip(-px, -py), chip(dx, dy))

    def ag_of(j):
        return lambda k, s, e: ag(j, k, s, e)

    for j in range(HD):
        both = qgr[:, :, cols(j)].astype(F32)
        qg[j, 0, my_rows, :] = both[:, :8, :].reshape(ROWS, HEAD_DIM).astype(BF)
        qg[j, 1, my_rows, :] = both[:, 8:, :].reshape(ROWS, HEAD_DIM).astype(BF)
        for k in range(8):
            if j == 0:
                from_parent(k, ag_st).start()
            from_parent(k, ag_of(j)).start()

    def ag_relay(j):
        for k in RELAYS:
            if j == 0:
                ag_st(k, source(k), b).wait_recv()
            ag(j, k, source(k), b).wait_recv()
            for child in BELOW[TREE[k][0]]:
                if j == 0:
                    from_parent(child, ag_st).start()
                from_parent(child, ag_of(j)).start()

    def ag_rest(j):
        for k in range(EDGES):
            if k not in RELAYS:
                if j == 0:
                    ag_st(k, source(k), b).wait_recv()
                ag(j, k, source(k), b).wait_recv()

    pair = pl.multiple_of(16 * (b // 2), 16)
    own_st = st[b]
    own_st = jnp.where(odd, pltpu.roll(own_st, 64, 1), own_st)
    text_st = pltpu.roll(stp[:, SLAB_Q:], lax.rem(ROWS - pair + HEAD_DIM, HEAD_DIM), 1)
    mine_at = lane // 8 == ROWS // 8 + lax.rem(b, 2)
    stat_row = lax.broadcasted_iota(jnp.int32, (8, 1), 0)
    silent = jnp.where(jnp.logical_and(stat_row >= HD, stat_row < 2 * HD), SILENT, 0.0)
    tst[...] = jnp.where(lane < ROWS, own_st, jnp.where(mine_at, text_st, silent))
    key_index = lax.broadcasted_iota(jnp.int32, (TXT, 1), 0)
    mask = (key_index < cnt_ref[0]).astype(F32)

    def text_keys(j):
        for i in range(2):
            qtk[i, :ROWS, :] = qg[j, i, my_rows, :]
            qtk[i, ROWS : ROWS + 16, :] = qg[j, i, pl.ds(SLAB_Q + pair, 16), :]
            qtk[i, ROWS + 16 :, :] = jnp.zeros((HEAD_DIM - ROWS - 16, HEAD_DIM), BF)
        keys = tkr[j]
        one_q, one_k, one_v = attend(
            keys, keys.T, tv[:, cols(j)], qtk[0], qtk[1],
            tst[HD + j : HD + j + 1, :], tst[j : j + 1, :], mask,
        )
        dqt[j] = one_q
        dkvt[j, 0] = one_k
        dkvt[j, 1] = one_v

    mine = rows_of(c, KEYS)
    theirs = rows_of(1 - c, KEYS)

    def sib_kv(j, rows):
        part = kv.at[j, :, rows, :]
        return remote(part, part, s_skv.at[j], r_skv.at[j], sib)

    def share_kv(j):
        def wait_kv(t, carry):
            s = zdev(t)
            remote(
                kvs.at[s * HD + j], kv.at[j, :, key_rows(s), :], s_kv.at[j, t], r_kv.at[j, s], {"head": s}
            ).wait_recv()
            return carry

        lax.fori_loop(1, NZ, wait_kv, 0)
        sib_kv(j, mine).start()

    text_keys(0)
    ag_relay(0)
    text_keys(1)
    share_kv(0)
    ag_relay(1)
    text_keys(2)
    other = rows_of(1 - c, HALF)
    sib_t = remote(dkvt.at[:, :, other, :], xt, s_sib.at[0], r_sib.at[0], sib)
    sib_t.start()
    ag_rest(0)
    for i in range(NB // 2):
        stp[:, cols(i)] = st[2 * i] + st[2 * i + 1]

    def image_keys(j, keys_t, rows, start):
        one_q, one_k, one_v = attend(
            kv[j, 0], keys_t, kv[j, 1], qg[j, 0, rows, :], qg[j, 1, rows, :],
            stp[HD + j : HD + j + 1, rows], stp[j : j + 1, rows],
        )
        dq[j, rows, :] = one_q
        if start:
            dkv[j, 0] = one_k
            dkv[j, 1] = one_v
        else:
            dkv[j, 0] += one_k
            dkv[j, 1] += one_v

    def sib_d(j):
        return remote(dkv.at[j, :, theirs, :], xk.at[j], s_sd.at[j], r_sd.at[j], sib)

    ck, sn_k = angles(blk, 0, KEYS)

    def token_rows(s):
        return rows_of(s, 32)

    def z_out(j, t, d):
        return remote(
            dkvs.at[j, :, token_rows(d), :], okv.at[h * HD + j], s_o.at[j, t], r_o.at[j, h], {"head": d}
        )

    def finish_kv(j):
        sib_d(j).wait()
        dkvs[j, 0] = turn_back(dkv[j, 0, mine, :] + xk[j, 0], ck, sn_k).astype(BF)
        dkvs[j, 1] = (dkv[j, 1, mine, :] + xk[j, 1]).astype(BF)

        def go_out(t, carry):
            z_out(j, t, zdev(t)).start()
            return carry

        lax.fori_loop(1, NZ, go_out, 0)
        okv[h * HD + j] = dkvs[j, :, token_rows(h), :]

    def own_rows(j, e):
        at = rows_of(e, 8)
        at_half = pl.ds(pl.multiple_of(HALF * c + e * 8, 8), 8)
        return jnp.concatenate(
            [
                dq[j, rows_of(e, ROWS), :],
                dq[j, pl.ds(pl.multiple_of(SLAB_Q + e * 8, 8), 8), :],
                dkvt[j, 0, at_half, :] + xt[j, 0, at, :],
                dkvt[j, 1, at_half, :] + xt[j, 1, at, :],
                jnp.zeros((8, HEAD_DIM), F32),
            ],
            axis=0,
        )

    def rs_copy(j, k):
        dx, dy = TREE[k][2]
        return remote(rs_s.at[j, k], rs_r.at[j, k], s_rs.at[j, k], r_rs.at[j, k], on_chip(chip(-dx, -dy)))

    def rs_gather(j, e, below):
        value = own_rows(j, e)
        for k in below:
            rs_copy(j, k).wait_recv()
            value = value + rs_r[j, k].astype(F32)
        return value

    def rs_pass(j, some):
        for k in some:
            rs_s[j, k] = rs_gather(j, source(k), BELOW[TREE[k][0]]).astype(BF)
            rs_copy(j, k).start()

    for j in range(HD):
        if j > 0:
            ag_rest(j)
        sib_kv(j, theirs).wait_recv()
        if j == 0:
            ag_relay(2)
        keys_t = kv[j, 0].T
        image_keys(j, keys_t, slice(SLAB_Q, SLAB_Q + HALF), True)
        for i in range(SLAB_Q // STEP):
            image_keys(j, keys_t, slice(i * STEP, (i + 1) * STEP), False)
        sib_d(j).start()
        if j == 0:
            sib_t.wait()
        if j < HD - 1:
            share_kv(j + 1)
        if j > 0:
            finish_kv(j - 1)
        rs_pass(j, LEAVES)
        if j > 0:
            rs_pass(j - 1, RELAYS)
    finish_kv(HD - 1)
    rs_pass(HD - 1, RELAYS)

    cq, sn_q = slab_angles(0, ROWS)
    own_at = pl.ds(pl.multiple_of(TXT + HALF * c + 8 * b, 8), 8)
    ct = cos_t[own_at, :]
    sn = sin_t[own_at, :]
    parts = []
    for j in range(HD):
        total = rs_gather(j, b, range(8))
        extra = jnp.where(odd, dqt[j, ROWS + 8 : ROWS + 16, :], dqt[j, ROWS : ROWS + 8, :])
        tx[c, b, :, cols(j)] = jnp.concatenate(
            [
                turn_back(total[ROWS : ROWS + 8, :] + extra, ct, sn),
                turn_back(total[ROWS + 8 : ROWS + 16, :], ct, sn),
                total[ROWS + 16 :, :],
            ],
            axis=0,
        ).astype(BF)
        parts.append(turn_back(total[:ROWS, :] + dqt[j, :ROWS, :], cq, sn_q).reshape(NZ, 8, HEAD_DIM))

    def tx_copy(k, s, e):
        return remote(tx.at[c, s], tx.at[c, s], s_tx.at[k], r_tx.at[k], on_chip(e))

    for k in range(8):
        from_parent(k, tx_copy).start()
    sqs[:, :, :HEAD_DIM] = jnp.concatenate([parts[0], parts[2]], axis=1).astype(BF)
    sqs[:, :, HEAD_DIM:] = jnp.concatenate([parts[1], jnp.zeros_like(parts[1])], axis=1).astype(BF)

    def out_q(t, d):
        return remote(sqs.at[d], sqr.at[h], s_oq.at[t], r_oq.at[h], {"head": d})

    def go_oq(t, carry):
        out_q(t, zdev(t)).start()
        return carry

    lax.fori_loop(1, NZ, go_oq, 0)
    sqr[h] = sqs[h]
    for k in RELAYS:
        tx_copy(k, source(k), b).wait_recv()
        for child in BELOW[TREE[k][0]]:
            from_parent(child, tx_copy).start()
    for k in range(EDGES):
        if k not in RELAYS:
            tx_copy(k, source(k), b).wait_recv()
    sib_tx = remote(tx.at[c], tx.at[c], s_sib.at[1], r_sib.at[1], sib)
    sib_tx.start()

    def wait_oq(t, carry):
        s = zdev(t)
        remote(sqs.at[s], sqr.at[s], s_oq.at[t], r_oq.at[s], {"head": s}).wait_recv()
        return carry

    lax.fori_loop(1, NZ, wait_oq, 0)
    for s in range(NZ):
        piece = sqr[s].astype(F32)
        sqo[:, s * W : s * W + 128] = piece[:8, :128].astype(BF)
        sqo[:, s * W + 128 : s * W + 256] = piece[:8, 128:].astype(BF)
        sqo[:, s * W + 256 : s * W + 384] = piece[8:, :128].astype(BF)
    remote(tx.at[1 - c], tx.at[1 - c], s_sib.at[1], r_sib.at[1], sib).wait_recv()
    for core in range(2):
        block = tx[core].astype(F32)
        rows = slice(core * HALF, (core + 1) * HALF)
        for i in range(3):
            txo[i, rows, :] = block[:, 8 * i : 8 * i + 8, :].reshape(HALF, W).astype(BF)
    for j in range(HD):

        def wait_out(t, carry, j=j):
            s = zdev(t)
            remote(
                dkvs.at[j, :, token_rows(s), :], okv.at[s * HD + j], s_o.at[j, t], r_o.at[j, s], {"head": s}
            ).wait_recv()
            return carry

        lax.fori_loop(1, NZ, wait_out, 0)

    def drain_z(t, carry):
        d = zdev(t)
        z_qg(t, d).wait_send()
        z_dl(t, d).wait_send()
        out_q(t, d).wait_send()
        for j in range(HD):
            z_kv(j, t, d).wait_send()
            z_out(j, t, d).wait_send()
        return carry

    lax.fori_loop(1, NZ, drain_z, 0)
    for k in range(EDGES):
        from_parent(k, ag_st).wait_send()
        from_parent(k, tx_copy).wait_send()
        for j in range(HD):
            from_parent(k, ag_of(j)).wait_send()
            rs_copy(j, k).wait_send()
    for j in range(HD):
        sib_kv(j, mine).wait_send()
    sib_tx.wait_send()


def deliver(sqo, okv, txo, sqg, ikg, ivg, tqg, tkg, tvg):
    sqg[...] = sqo[...]
    for n in range(NZ * HD):
        ikg[:, cols(n)] = okv[n, 0]
        ivg[:, cols(n)] = okv[n, 1]
    tqg[...] = txo[0]
    tkg[...] = txo[1]
    tvg[...] = txo[2]


def on_device(
    slab_query, slab_output, slab_cotangent, slab_logsum, image_keys, image_values,
    text_query, text_keys, text_values, text_output, text_cotangent, text_logsum,
    text_count, slab_offsets,
):
    vmem = pl.BlockSpec(memory_space=pltpu.VMEM)
    smem = pl.BlockSpec(memory_space=pltpu.SMEM)
    hbm = pl.BlockSpec(memory_space=pltpu.HBM)
    dma = pltpu.SemaphoreType.DMA
    slab = pltpu.VMEM((8, ALL), BF)
    text = pltpu.VMEM((TXT, W), BF)
    sqo, okv, txo = pl.pallas_call(
        kernel,
        out_shape=[
            jax.ShapeDtypeStruct((8, ALL), BF),
            jax.ShapeDtypeStruct((NZ * HD, 2, 32, HEAD_DIM), BF),
            jax.ShapeDtypeStruct((3, TXT, W), BF),
        ],
        in_specs=[smem, smem] + [hbm] * 13,
        out_specs=[vmem] * 3,
        scratch_shapes=[
            slab, slab, slab,
            pltpu.VMEM((HD, ROWS), F32),
            pltpu.VMEM((32, ALL), BF),
            pltpu.VMEM((32, ALL), BF),
            text, text, text, text, text,
            pltpu.VMEM((HD, TXT), F32),
            pltpu.VMEM((2, 512, HEAD_DIM), F32),
            pltpu.VMEM((NZ, 16, W), BF),
            pltpu.VMEM((NZ, 8, HEAD_DIM), F32),
            pltpu.VMEM((NZ, 16, W), BF),
            pltpu.VMEM((NZ, 8, HEAD_DIM), F32),
            pltpu.VMEM((NZ * HD, 2, 32, HEAD_DIM), BF),
            pltpu.VMEM((HD, 2, 2 * KEYS, HEAD_DIM), BF),
            pltpu.VMEM((HD, 2, SLAB_Q + HALF, HEAD_DIM), BF),
            pltpu.VMEM((NB, 8, HEAD_DIM), F32),
            pltpu.VMEM((8, SLAB_Q + HALF), F32),
            pltpu.VMEM((HD, TXT, HEAD_DIM), BF),
            pltpu.VMEM((8, HEAD_DIM), F32),
            pltpu.VMEM((2, HEAD_DIM, HEAD_DIM), BF),
            pltpu.VMEM((HD, HEAD_DIM, HEAD_DIM), F32),
            pltpu.VMEM((HD, 2, TXT, HEAD_DIM), F32),
            pltpu.VMEM((HD, 2, HALF, HEAD_DIM), F32),
            pltpu.VMEM((HD, SLAB_Q + HALF, HEAD_DIM), F32),
            pltpu.VMEM((HD, 2, 2 * KEYS, HEAD_DIM), F32),
            pltpu.VMEM((HD, 2, KEYS, HEAD_DIM), F32),
            pltpu.VMEM((HD, 2, KEYS, HEAD_DIM), BF),
            pltpu.VMEM((HD, EDGES, 96, HEAD_DIM), BF),
            pltpu.VMEM((HD, EDGES, 96, HEAD_DIM), BF),
            pltpu.VMEM((NZ, 16, 256), BF),
            pltpu.VMEM((NZ, 16, 256), BF),
            pltpu.VMEM((2, NB, 32, W), BF),
            dma((13,)),
            dma((2, NZ)), dma((NZ,)), dma((NZ,)),
            dma((HD, NZ)), dma((HD, NZ)),
            dma((HD, EDGES)), dma((HD, EDGES)),
            dma((EDGES,)), dma((EDGES,)),
            dma((2,)), dma((2,)),
            dma((HD,)), dma((HD,)), dma((HD,)), dma((HD,)),
            dma((HD, NZ)), dma((HD, NZ)),
            dma((NZ,)), dma((NZ,)),
            dma((HD, EDGES)), dma((HD, EDGES)),
            dma((EDGES,)), dma((EDGES,)),
        ],
        compiler_params=pltpu.CompilerParams(
            collective_id=0, has_side_effects=True, vmem_limit_bytes=63 * 1024 * 1024
        ),
        cost_estimate=pl.CostEstimate(
            flops=2_500_000_000, bytes_accessed=4_000_000, transcendentals=2_000_000
        ),
        name="joint_backward",
    )(
        slab_offsets, text_count, slab_query, slab_output, slab_cotangent, slab_logsum.T,
        image_keys, image_values, text_query, text_keys, text_values, text_output,
        text_cotangent, text_logsum.T, tables(),
    )
    shapes = [
        jax.ShapeDtypeStruct(x.shape, BF)
        for x in (slab_query, image_keys, image_values, text_query, text_keys, text_values)
    ]
    return pl.pallas_call(
        deliver, out_shape=shapes, in_specs=[vmem] * 3, out_specs=[vmem] * 6, name="deliver"
    )(sqo, okv, txo)


def solution(mesh):
    tokens = P(("rep", "blk", "head"), None)
    text = P("rep", "head")
    in_specs = (
        tokens, tokens, tokens, P(("rep", "blk"), "head"), tokens, tokens,
        text, text, text, text, text, text, P("rep"), P("rep"),
    )
    out_specs = (tokens, tokens, tokens, text, text, text)
    return jax.shard_map(
        on_device, mesh=mesh, in_specs=in_specs, out_specs=out_specs, check_vma=False
    )
```

```python
import jax
import jax.numpy as jnp
import numpy as np
from jax import lax
from jax.experimental import pallas as pl
from jax.experimental.pallas import tpu as pltpu
from jax.sharding import PartitionSpec as P

HEAD_DIM = 128
FACTOR = HEAD_DIM ** (-0.5)
NZ = 8
NX = 4
NB = NX * NX
HD = 3
W = HD * HEAD_DIM
ALL = NZ * W
TXT = 256
HALF = TXT // 2
ROWS = 64
KEYS = 256
SLAB_Q = NB * ROWS
STEP = 256
SILENT = 1e30
BF = jnp.bfloat16
F32 = jnp.float32
MESH = pl.DeviceIdType.MESH

TREE = (
    ((1, 0), (0, 0), (1, 0)),
    ((-1, 0), (0, 0), (-1, 0)),
    ((0, 1), (0, 0), (0, 1)),
    ((0, -1), (0, 0), (0, -1)),
    ((1, 1), (0, 0), (1, 1)),
    ((1, -1), (0, 0), (1, -1)),
    ((-1, 1), (0, 0), (-1, 1)),
    ((-1, -1), (0, 0), (-1, -1)),
    ((2, 0), (-1, 0), (-1, 0)),
    ((0, 2), (0, -1), (0, -1)),
    ((2, 1), (1, 1), (1, 0)),
    ((2, -1), (-1, -1), (-1, 0)),
    ((1, 2), (1, 1), (0, 1)),
    ((-1, 2), (-1, 1), (0, 1)),
    ((2, 2), (1, -1), (1, -1)),
)
EDGES = len(TREE)
BELOW = {child: [k for k, e in enumerate(TREE) if e[1] == child] for child, _, _ in TREE}
RELAYS = (1, 3, 4, 7, 6, 5)
LEAVES = (14, 8, 9, 10, 11, 12, 13, 0, 2)
AROUND = [e[2] for e in TREE[:8]]


def tables():
    place = np.arange(512, dtype=np.float64)[:, None]
    frequency = 10000.0 ** (-np.arange(32, dtype=np.float64) / 32)
    angles = np.tile(place * frequency[None, :], (1, 4))
    sign = np.where(np.arange(128) < 64, -1.0, 1.0)
    return np.stack([np.cos(angles), np.sin(angles) * sign]).astype(np.float32)


def nt(a, b):
    return lax.dot_general(a, b, (((1,), (1,)), ((), ())), preferred_element_type=F32)


def nn(a, b):
    return lax.dot_general(a, b, (((1,), (0,)), ((), ())), preferred_element_type=F32)


def turn(x, cosine, sine):
    return x * cosine + pltpu.roll(x, 64, 1) * sine


def turn_back(x, cosine, sine):
    return x * cosine - pltpu.roll(x, 64, 1) * sine


def cols(n):
    return slice(n * HEAD_DIM, (n + 1) * HEAD_DIM)


def attend(keys, keys_t, values, queries, cotan, logsum, delta, mask=None):
    p = jnp.exp(nt(keys, queries) * FACTOR - logsum)
    if mask is not None:
        p = p * mask
    dv = nn(p.astype(BF), cotan)
    dp = nt(values, cotan)
    ds = (p * (dp - delta) * FACTOR).astype(BF)
    return nn(keys_t, ds).T, nn(ds, queries), dv


def kernel(
    off_ref, cnt_ref, sq_h, so_h, sg_h, sl_h, ik_h, iv_h, tq_h, tk_h, tv_h, to_h, tg_h, tl_h, tab_h,
    sqo, okv, txo,
    sq, so, sg, sl, ik, iv, tq, tk, tv, to, tg, tl, tab,
    qgs, dls, qgr, dlr, kvs, kv, qg, st, stp, tkr, tst, qtk, dqt, dkvt, xt,
    dq, dkv, xs, xk, dkvs, rs_s, rs_r, tk_s, tk_r, sqs, sqr, tx, tkx,
    s_in, s_z, r_zqg, r_zd, s_kv, r_kv, s_xy, r_xy, s_st, r_st, s_sib, r_sib, s_skv, r_skv, s_sd, r_sd,
    s_o, r_o, s_oq, r_oq, s_rs, r_rs, s_tx, r_tx, s_tk, r_tk, s_tkx, r_tkx,
):
    blk = lax.axis_index("blk")
    h = lax.axis_index("head")
    c = lax.rem(blk, 2)
    b = blk // 2
    bx = b // NX
    by = lax.rem(b, NX)
    lane = lax.broadcasted_iota(jnp.int32, (1, HEAD_DIM), 1)
    sub = lax.broadcasted_iota(jnp.int32, (8, 1), 0)
    first = lax.rem(lane, 64) < 32
    sib = {"blk": 2 * b + 1 - c}

    def zdev(t):
        return lax.rem(h + t, NZ)

    def chip(dx, dy):
        return lax.rem(bx + dx + NX, NX) * NX + lax.rem(by + dy + NX, NX)

    def on_chip(e):
        return {"blk": 2 * e + c}

    def remote(src, dst, ss, rs, dev):
        return pltpu.make_async_remote_copy(
            src_ref=src, dst_ref=dst, send_sem=ss, recv_sem=rs, device_id=dev, device_id_type=MESH
        )

    def rows_of(e, count):
        return pl.ds(pl.multiple_of(e * count, count), count)

    def wide(d):
        return rows_of(d, W)

    def fetch(i, src, dst):
        copy = pltpu.make_async_copy(src, dst, s_in.at[i])
        copy.start()
        return copy

    f_slab = [fetch(1, sq_h, sq), fetch(2, sg_h, sg), fetch(3, so_h, so)]
    f_tab = fetch(0, tab_h, tab)
    f_k = fetch(4, ik_h, ik)
    f_v = fetch(5, iv_h, iv)
    f_text = [
        fetch(6, tq_h, tq), fetch(7, tg_h, tg), fetch(8, to_h, to), fetch(9, tk_h, tk),
        fetch(10, tv_h, tv), fetch(11, tl_h, tl), fetch(12, sl_h, sl),
    ]

    bar = pltpu.get_barrier_semaphore()

    def greet_z(t, carry):
        pl.semaphore_signal(bar, inc=1, device_id={"head": zdev(t)}, device_id_type=MESH)
        return carry

    lax.fori_loop(1, NZ, greet_z, 0)
    for dx, dy in AROUND:
        pl.semaphore_signal(bar, inc=1, device_id=on_chip(chip(dx, dy)), device_id_type=MESH)
    pl.semaphore_signal(bar, inc=1, device_id=sib, device_id_type=MESH)

    cos_t, sin_t = tab.at[0], tab.at[1]

    def angles(row, start, count):
        ct = cos_t[pl.ds(start, count), :]
        sn = sin_t[pl.ds(start, count), :]
        cr = cos_t[pl.ds(row, 1), :]
        sr = sin_t[pl.ds(row, 1), :]
        return jnp.where(first, cr, ct), jnp.where(first, sr, sn)

    place = off_ref[0] + blk
    row_at = lax.broadcasted_iota(jnp.int32, (32, 1), 0) == place // 4
    col_at = lax.rem(place, 4)

    def slab_angles(start, count):
        result = []
        for table in (cos_t, sin_t):
            row = jnp.sum(jnp.where(row_at, table[:32, :], 0.0), axis=0, keepdims=True)
            col = table[pl.ds(start, count), :]
            for i in range(1, 4):
                col = jnp.where(col_at == i, table[pl.ds(64 * i + start, count), :], col)
            result.append(jnp.where(first, row, col))
        return result

    f_tab.wait()
    for copy in f_slab:
        copy.wait()
    cq, sn_q = slab_angles(pl.multiple_of(8 * h, 8), 8)
    for d in range(NZ):
        acc = jnp.zeros((8, HEAD_DIM), F32)
        for j in range(HD):
            n = d * HD + j
            g = sg[:, cols(n)].astype(F32)
            q = turn(sq[:, cols(n)].astype(F32), cq, sn_q)
            qgs[d, :, cols(j)] = jnp.concatenate([q, g], axis=0).astype(BF)
            own = jnp.sum(g * so[:, cols(n)].astype(F32), axis=1, keepdims=True)
            acc = jnp.where(lane == 8 * j + sub, own, acc)
        dls[d] = jnp.sum(acc, axis=0, keepdims=True)
    pl.semaphore_wait(bar, NZ + len(AROUND))

    def z_qg(t, d):
        return remote(qgs.at[d], qgr.at[h], s_z.at[0, t], r_zqg.at[h], {"head": d})

    def z_dl(t, d):
        return remote(dls.at[d], dlr.at[h], s_z.at[1, t], r_zd.at[h], {"head": d})

    def key_rows(s):
        return pl.ds(pl.multiple_of(c * KEYS + s * 32, 32), 32)

    def z_kv(j, t, d):
        return remote(
            kvs.at[d * HD + j], kv.at[j, :, key_rows(h), :], s_kv.at[j, t], r_kv.at[j, h], {"head": d}
        )

    def go_qg(t, carry):
        z_qg(t, zdev(t)).start()
        z_dl(t, zdev(t)).start()
        return carry

    lax.fori_loop(1, NZ, go_qg, 0)
    f_k.wait()
    f_v.wait()
    ck, sn_k = angles(blk, pl.multiple_of(32 * h, 32), 32)
    for j in range(HD):
        for d in range(NZ):
            n = d * HD + j
            kvs[n, 0] = turn(ik[:, cols(n)].astype(F32), ck, sn_k).astype(BF)
            kvs[n, 1] = iv[:, cols(n)]

        def go_kv(t, carry, j=j):
            z_kv(j, t, zdev(t)).start()
            return carry

        lax.fori_loop(1, NZ, go_kv, 0)
        kv[j, :, key_rows(h), :] = kvs[h * HD + j]
    qgr[h] = qgs[h]
    dlr[h] = dls[h]

    for copy in f_text:
        copy.wait()
    half = rows_of(c, HALF)
    text_at = pl.ds(pl.multiple_of(TXT + HALF * c, HALF), HALF)
    ct = cos_t[text_at, :]
    sn = sin_t[text_at, :]
    acc = jnp.zeros((HALF, HEAD_DIM), F32)
    for j in range(HD):
        g = tg[half, cols(j)]
        qg[j, 0, SLAB_Q:, :] = turn(tq[half, cols(j)].astype(F32), ct, sn).astype(BF)
        qg[j, 1, SLAB_Q:, :] = g
        own = jnp.sum(g.astype(F32) * to[half, cols(j)].astype(F32), axis=1, keepdims=True)
        acc = jnp.where(lane == j, own, acc)
        tkr[j] = turn(tk[:, cols(j)].astype(F32), cos_t[TXT:, :], sin_t[TXT:, :]).astype(BF)
    stp[:, SLAB_Q:] = acc.T[:8, :]
    stp[HD : 2 * HD, SLAB_Q:] = tl[:, half]

    def wait_qg(t, carry):
        s = zdev(t)
        remote(qgs.at[s], qgr.at[s], s_z.at[0, t], r_zqg.at[s], {"head": s}).wait_recv()
        remote(dls.at[s], dlr.at[s], s_z.at[1, t], r_zd.at[s], {"head": s}).wait_recv()
        return carry

    lax.fori_loop(1, NZ, wait_qg, 0)
    my_rows = rows_of(b, ROWS)
    odd = lax.rem(b, 2) == 1
    delta = dlr[...].reshape(NZ, HEAD_DIM)
    shift = ROWS * lax.rem(b, 2)
    here = (lane // 64) == lax.rem(b, 2)
    logs = jnp.concatenate([sl[...], sl[...]], axis=1)
    st[b] = jnp.zeros((8, HEAD_DIM), F32)
    moved = [pltpu.roll(delta[i : i + 1, :], 8 * i, 1) if i else delta[:1, :] for i in range(NZ)]
    for j in range(HD):
        row = jnp.zeros((1, HEAD_DIM), F32)
        for i in range(NZ):
            row = jnp.where(lane // 8 == i + j, moved[i], row)
        st[b, j : j + 1, :] = pltpu.roll(row, lax.rem(shift + HEAD_DIM - 8 * j, HEAD_DIM), 1)
    st[b, HD : 2 * HD, :] = jnp.where(here, logs, 0.0)

    def ag(j, k, s, e):
        block = qg.at[j, :, rows_of(s, ROWS), :]
        return remote(block, block, s_xy.at[j, k], r_xy.at[j, k], on_chip(e))

    def ag_st(k, s, e):
        return remote(st.at[s], st.at[s], s_st.at[k], r_st.at[k], on_chip(e))

    def source(k):
        return chip(-TREE[k][0][0], -TREE[k][0][1])

    def from_parent(k, copy):
        _, (px, py), (dx, dy) = TREE[k]
        return copy(k, chip(-px, -py), chip(dx, dy))

    def ag_of(j):
        return lambda k, s, e: ag(j, k, s, e)

    for j in range(HD):
        both = qgr[:, :, cols(j)].astype(F32)
        qg[j, 0, my_rows, :] = both[:, :8, :].reshape(ROWS, HEAD_DIM).astype(BF)
        qg[j, 1, my_rows, :] = both[:, 8:, :].reshape(ROWS, HEAD_DIM).astype(BF)
        for k in range(8):
            if j == 0:
                from_parent(k, ag_st).start()
            from_parent(k, ag_of(j)).start()

    def ag_relay(j):
        for k in RELAYS:
            if j == 0:
                ag_st(k, source(k), b).wait_recv()
            ag(j, k, source(k), b).wait_recv()
            for child in BELOW[TREE[k][0]]:
                if j == 0:
                    from_parent(child, ag_st).start()
                from_parent(child, ag_of(j)).start()

    def ag_rest(j):
        for k in range(EDGES):
            if k not in RELAYS:
                if j == 0:
                    ag_st(k, source(k), b).wait_recv()
                ag(j, k, source(k), b).wait_recv()

    pair = pl.multiple_of(16 * (b // 2), 16)
    own_st = st[b]
    own_st = jnp.where(odd, pltpu.roll(own_st, 64, 1), own_st)
    text_st = pltpu.roll(stp[:, SLAB_Q:], lax.rem(ROWS - pair + HEAD_DIM, HEAD_DIM), 1)
    mine_at = lane // 8 == ROWS // 8 + lax.rem(b, 2)
    stat_row = lax.broadcasted_iota(jnp.int32, (8, 1), 0)
    silent = jnp.where(jnp.logical_and(stat_row >= HD, stat_row < 2 * HD), SILENT, 0.0)
    tst[...] = jnp.where(lane < ROWS, own_st, jnp.where(mine_at, text_st, silent))
    key_index = lax.broadcasted_iota(jnp.int32, (TXT, 1), 0)
    mask = (key_index < cnt_ref[0]).astype(F32)

    def text_keys(j):
        for i in range(2):
            qtk[i, :ROWS, :] = qg[j, i, my_rows, :]
            qtk[i, ROWS : ROWS + 16, :] = qg[j, i, pl.ds(SLAB_Q + pair, 16), :]
            qtk[i, ROWS + 16 :, :] = jnp.zeros((HEAD_DIM - ROWS - 16, HEAD_DIM), BF)
        keys = tkr[j]
        one_q, one_k, one_v = attend(
            keys, keys.T, tv[:, cols(j)], qtk[0], qtk[1],
            tst[HD + j : HD + j + 1, :], tst[j : j + 1, :], mask,
        )
        dqt[j] = one_q
        dkvt[j, 0] = one_k
        dkvt[j, 1] = one_v

    mine = rows_of(c, KEYS)
    theirs = rows_of(1 - c, KEYS)

    def sib_kv(j, rows):
        part = kv.at[j, :, rows, :]
        return remote(part, part, s_skv.at[j], r_skv.at[j], sib)

    def share_kv(j):
        def wait_kv(t, carry):
            s = zdev(t)
            remote(
                kvs.at[s * HD + j], kv.at[j, :, key_rows(s), :], s_kv.at[j, t], r_kv.at[j, s], {"head": s}
            ).wait_recv()
            return carry

        lax.fori_loop(1, NZ, wait_kv, 0)
        sib_kv(j, mine).start()

    text_keys(0)
    ag_relay(0)
    text_keys(1)
    share_kv(0)
    ag_relay(1)
    text_keys(2)
    other = rows_of(1 - c, HALF)
    sib_t = remote(dkvt.at[:, :, other, :], xt, s_sib.at[0], r_sib.at[0], sib)
    sib_t.start()
    ag_rest(0)
    for i in range(NB // 2):
        stp[:, cols(i)] = st[2 * i] + st[2 * i + 1]

    def image_keys(j, keys_t, rows, start):
        one_q, one_k, one_v = attend(
            kv[j, 0], keys_t, kv[j, 1], qg[j, 0, rows, :], qg[j, 1, rows, :],
            stp[HD + j : HD + j + 1, rows], stp[j : j + 1, rows],
        )
        dq[j, rows, :] = one_q
        if start:
            dkv[j, 0] = one_k
            dkv[j, 1] = one_v
        else:
            dkv[j, 0] += one_k
            dkv[j, 1] += one_v

    def sib_d(j):
        return remote(xs.at[j], xk.at[j], s_sd.at[j], r_sd.at[j], sib)

    ck, sn_k = angles(blk, 0, KEYS)

    def token_rows(s):
        return rows_of(s, 32)

    def z_out(j, t, d):
        return remote(
            dkvs.at[j, :, token_rows(d), :], okv.at[h * HD + j], s_o.at[j, t], r_o.at[j, h], {"head": d}
        )

    def finish_kv(j):
        sib_d(j).wait()
        dkvs[j, 0] = turn_back(dkv[j, 0, mine, :] + xk[j, 0].astype(F32), ck, sn_k).astype(BF)
        dkvs[j, 1] = (dkv[j, 1, mine, :] + xk[j, 1].astype(F32)).astype(BF)

        def go_out(t, carry):
            z_out(j, t, zdev(t)).start()
            return carry

        lax.fori_loop(1, NZ, go_out, 0)
        okv[h * HD + j] = dkvs[j, :, token_rows(h), :]

    def make_sum(own, copy, sent, got):
        def gather(e, below):
            value = own(e)
            for k in below:
                copy(k).wait_recv()
                value = value + got[k].astype(F32)
            return value

        def pass_on(some):
            for k in some:
                sent[k] = gather(source(k), BELOW[TREE[k][0]]).astype(BF)
                copy(k).start()

        return gather, pass_on

    def towards_root(k, src, dst, ss, rs):
        dx, dy = TREE[k][2]
        return remote(src, dst, ss, rs, on_chip(chip(-dx, -dy)))

    def rs_copy(j, k):
        return towards_root(k, rs_s.at[j, k], rs_r.at[j, k], s_rs.at[j, k], r_rs.at[j, k])

    def tk_copy(k):
        return towards_root(k, tk_s.at[k], tk_r.at[k], s_tk.at[k], r_tk.at[k])

    def own_rows(j):
        def own(e):
            text = dq[j, pl.ds(pl.multiple_of(SLAB_Q + e * 8, 8), 8), :]
            return jnp.concatenate([dq[j, rows_of(e, ROWS), :], text, jnp.zeros_like(text)], axis=0)

        return own

    def own_text(e):
        at = rows_of(e, 8)
        at_half = pl.ds(pl.multiple_of(HALF * c + e * 8, 8), 8)
        heads = [
            jnp.concatenate([dkvt[j, i, at_half, :] + xt[j, i, at, :] for i in range(2)], axis=0)
            for j in range(HD)
        ]
        return jnp.concatenate(heads, axis=1)

    rs_sums = [
        make_sum(own_rows(j), lambda k, j=j: rs_copy(j, k), rs_s.at[j], rs_r.at[j]) for j in range(HD)
    ]
    tk_gather, tk_pass = make_sum(own_text, tk_copy, tk_s, tk_r)

    def tx_copy(k, s, e):
        return remote(tx.at[c, s], tx.at[c, s], s_tx.at[k], r_tx.at[k], on_chip(e))

    def tkx_copy(k, s, e):
        return remote(tkx.at[c, s], tkx.at[c, s], s_tkx.at[k], r_tkx.at[k], on_chip(e))

    def spread_out(copy):
        for k in range(8):
            from_parent(k, copy).start()

    def spread_on(copy):
        for k in RELAYS:
            copy(k, source(k), b).wait_recv()
            for child in BELOW[TREE[k][0]]:
                from_parent(child, copy).start()

    def spread_end(copy):
        for k in range(EDGES):
            if k not in RELAYS:
                copy(k, source(k), b).wait_recv()

    own_at = pl.ds(pl.multiple_of(TXT + HALF * c + 8 * b, 8), 8)
    ct = cos_t[own_at, :]
    sn = sin_t[own_at, :]

    def text_key_result():
        total = tk_gather(b, range(8))
        for j in range(HD):
            tkx[c, b, :, cols(j)] = jnp.concatenate(
                [turn_back(total[:8, cols(j)], ct, sn), total[8:, cols(j)]], axis=0
            ).astype(BF)
        spread_out(tkx_copy)

    sib_tkx = remote(tkx.at[c], tkx.at[c], s_sib.at[2], r_sib.at[2], sib)
    sib_tx = remote(tx.at[c], tx.at[c], s_sib.at[1], r_sib.at[1], sib)

    sib_t.wait()
    tk_pass(LEAVES)
    for j in range(HD):
        if j > 0:
            ag_rest(j)
        sib_kv(j, theirs).wait_recv()
        if j == 0:
            ag_relay(2)
        keys_t = kv[j, 0].T
        image_keys(j, keys_t, slice(SLAB_Q, SLAB_Q + HALF), True)
        for i in range(SLAB_Q // STEP):
            image_keys(j, keys_t, slice(i * STEP, (i + 1) * STEP), False)
            if i == 1 and j > 0:
                finish_kv(j - 1)
        xs[j] = dkv[j, :, theirs, :].astype(BF)
        sib_d(j).start()
        if j < HD - 1:
            share_kv(j + 1)
        rs_sums[j][1](LEAVES)
        if j == 0:
            tk_pass(RELAYS)
        else:
            rs_sums[j - 1][1](RELAYS)
        if j == 1:
            text_key_result()
        if j == 2:
            spread_on(tkx_copy)
    finish_kv(HD - 1)
    rs_sums[HD - 1][1](RELAYS)

    cq, sn_q = slab_angles(0, ROWS)
    parts = []
    text_parts = []
    for j in range(HD):
        total = rs_sums[j][0](b, range(8))
        extra = jnp.where(odd, dqt[j, ROWS + 8 : ROWS + 16, :], dqt[j, ROWS : ROWS + 8, :])
        text_parts.append(turn_back(total[ROWS : ROWS + 8, :] + extra, ct, sn))
        parts.append(turn_back(total[:ROWS, :] + dqt[j, :ROWS, :], cq, sn_q).reshape(NZ, 8, HEAD_DIM))
    tx[c, b, :, :HEAD_DIM] = jnp.concatenate([text_parts[0], text_parts[2]], axis=0).astype(BF)
    tx[c, b, :, HEAD_DIM:] = jnp.concatenate(
        [text_parts[1], jnp.zeros_like(text_parts[1])], axis=0
    ).astype(BF)
    spread_out(tx_copy)
    sqs[:, :, :HEAD_DIM] = jnp.concatenate([parts[0], parts[2]], axis=1).astype(BF)
    sqs[:, :, HEAD_DIM:] = jnp.concatenate([parts[1], jnp.zeros_like(parts[1])], axis=1).astype(BF)

    def out_q(t, d):
        return remote(sqs.at[d], sqr.at[h], s_oq.at[t], r_oq.at[h], {"head": d})

    def go_oq(t, carry):
        out_q(t, zdev(t)).start()
        return carry

    lax.fori_loop(1, NZ, go_oq, 0)
    sqr[h] = sqs[h]
    spread_end(tkx_copy)
    sib_tkx.start()
    spread_on(tx_copy)
    spread_end(tx_copy)
    sib_tx.start()

    def wait_oq(t, carry):
        s = zdev(t)
        remote(sqs.at[s], sqr.at[s], s_oq.at[t], r_oq.at[s], {"head": s}).wait_recv()
        return carry

    lax.fori_loop(1, NZ, wait_oq, 0)
    for s in range(NZ):
        piece = sqr[s].astype(F32)
        sqo[:, s * W : s * W + 128] = piece[:8, :128].astype(BF)
        sqo[:, s * W + 128 : s * W + 256] = piece[:8, 128:].astype(BF)
        sqo[:, s * W + 256 : s * W + 384] = piece[8:, :128].astype(BF)
    remote(tkx.at[1 - c], tkx.at[1 - c], s_sib.at[2], r_sib.at[2], sib).wait_recv()
    for core in range(2):
        rows = slice(core * HALF, (core + 1) * HALF)
        block = tkx[core].astype(F32)
        txo[1, rows, :] = block[:, :8, :].reshape(HALF, W).astype(BF)
        txo[2, rows, :] = block[:, 8:, :].reshape(HALF, W).astype(BF)
    remote(tx.at[1 - c], tx.at[1 - c], s_sib.at[1], r_sib.at[1], sib).wait_recv()
    for core in range(2):
        rows = slice(core * HALF, (core + 1) * HALF)
        block = tx[core].astype(F32)
        txo[0, rows, :HEAD_DIM] = block[:, :8, :HEAD_DIM].reshape(HALF, HEAD_DIM).astype(BF)
        txo[0, rows, HEAD_DIM : 2 * HEAD_DIM] = block[:, :8, HEAD_DIM:].reshape(HALF, HEAD_DIM).astype(BF)
        txo[0, rows, 2 * HEAD_DIM :] = block[:, 8:, :HEAD_DIM].reshape(HALF, HEAD_DIM).astype(BF)
    for j in range(HD):

        def wait_out(t, carry, j=j):
            s = zdev(t)
            remote(
                dkvs.at[j, :, token_rows(s), :], okv.at[s * HD + j], s_o.at[j, t], r_o.at[j, s], {"head": s}
            ).wait_recv()
            return carry

        lax.fori_loop(1, NZ, wait_out, 0)

    def drain_z(t, carry):
        d = zdev(t)
        z_qg(t, d).wait_send()
        z_dl(t, d).wait_send()
        out_q(t, d).wait_send()
        for j in range(HD):
            z_kv(j, t, d).wait_send()
            z_out(j, t, d).wait_send()
        return carry

    lax.fori_loop(1, NZ, drain_z, 0)
    for k in range(EDGES):
        from_parent(k, ag_st).wait_send()
        from_parent(k, tx_copy).wait_send()
        from_parent(k, tkx_copy).wait_send()
        tk_copy(k).wait_send()
        for j in range(HD):
            from_parent(k, ag_of(j)).wait_send()
            rs_copy(j, k).wait_send()
    for j in range(HD):
        sib_kv(j, mine).wait_send()
    sib_tx.wait_send()
    sib_tkx.wait_send()


def deliver(sqo, okv, txo, sqg, ikg, ivg, tqg, tkg, tvg):
    sqg[...] = sqo[...]
    for n in range(NZ * HD):
        ikg[:, cols(n)] = okv[n, 0]
        ivg[:, cols(n)] = okv[n, 1]
    tqg[...] = txo[0]
    tkg[...] = txo[1]
    tvg[...] = txo[2]


def on_device(
    slab_query, slab_output, slab_cotangent, slab_logsum, image_keys, image_values,
    text_query, text_keys, text_values, text_output, text_cotangent, text_logsum,
    text_count, slab_offsets,
):
    vmem = pl.BlockSpec(memory_space=pltpu.VMEM)
    smem = pl.BlockSpec(memory_space=pltpu.SMEM)
    hbm = pl.BlockSpec(memory_space=pltpu.HBM)
    dma = pltpu.SemaphoreType.DMA
    slab = pltpu.VMEM((8, ALL), BF)
    text = pltpu.VMEM((TXT, W), BF)
    sqo, okv, txo = pl.pallas_call(
        kernel,
        out_shape=[
            jax.ShapeDtypeStruct((8, ALL), BF),
            jax.ShapeDtypeStruct((NZ * HD, 2, 32, HEAD_DIM), BF),
            jax.ShapeDtypeStruct((3, TXT, W), BF),
        ],
        in_specs=[smem, smem] + [hbm] * 13,
        out_specs=[vmem] * 3,
        scratch_shapes=[
            slab, slab, slab,
            pltpu.VMEM((HD, ROWS), F32),
            pltpu.VMEM((32, ALL), BF),
            pltpu.VMEM((32, ALL), BF),
            text, text, text, text, text,
            pltpu.VMEM((HD, TXT), F32),
            pltpu.VMEM((2, 512, HEAD_DIM), F32),
            pltpu.VMEM((NZ, 16, W), BF),
            pltpu.VMEM((NZ, 1, HEAD_DIM), F32),
            pltpu.VMEM((NZ, 16, W), BF),
            pltpu.VMEM((NZ, 1, HEAD_DIM), F32),
            pltpu.VMEM((NZ * HD, 2, 32, HEAD_DIM), BF),
            pltpu.VMEM((HD, 2, 2 * KEYS, HEAD_DIM), BF),
            pltpu.VMEM((HD, 2, SLAB_Q + HALF, HEAD_DIM), BF),
            pltpu.VMEM((NB, 8, HEAD_DIM), F32),
            pltpu.VMEM((8, SLAB_Q + HALF), F32),
            pltpu.VMEM((HD, TXT, HEAD_DIM), BF),
            pltpu.VMEM((8, HEAD_DIM), F32),
            pltpu.VMEM((2, HEAD_DIM, HEAD_DIM), BF),
            pltpu.VMEM((HD, HEAD_DIM, HEAD_DIM), F32),
            pltpu.VMEM((HD, 2, TXT, HEAD_DIM), F32),
            pltpu.VMEM((HD, 2, HALF, HEAD_DIM), F32),
            pltpu.VMEM((HD, SLAB_Q + HALF, HEAD_DIM), F32),
            pltpu.VMEM((HD, 2, 2 * KEYS, HEAD_DIM), F32),
            pltpu.VMEM((HD, 2, KEYS, HEAD_DIM), BF),
            pltpu.VMEM((HD, 2, KEYS, HEAD_DIM), BF),
            pltpu.VMEM((HD, 2, KEYS, HEAD_DIM), BF),
            pltpu.VMEM((HD, EDGES, 80, HEAD_DIM), BF),
            pltpu.VMEM((HD, EDGES, 80, HEAD_DIM), BF),
            pltpu.VMEM((EDGES, 16, W), BF),
            pltpu.VMEM((EDGES, 16, W), BF),
            pltpu.VMEM((NZ, 16, 256), BF),
            pltpu.VMEM((NZ, 16, 256), BF),
            pltpu.VMEM((2, NB, 16, 256), BF),
            pltpu.VMEM((2, NB, 16, W), BF),
            dma((13,)),
            dma((2, NZ)), dma((NZ,)), dma((NZ,)),
            dma((HD, NZ)), dma((HD, NZ)),
            dma((HD, EDGES)), dma((HD, EDGES)),
            dma((EDGES,)), dma((EDGES,)),
            dma((3,)), dma((3,)),
            dma((HD,)), dma((HD,)), dma((HD,)), dma((HD,)),
            dma((HD, NZ)), dma((HD, NZ)),
            dma((NZ,)), dma((NZ,)),
            dma((HD, EDGES)), dma((HD, EDGES)),
            dma((EDGES,)), dma((EDGES,)),
            dma((EDGES,)), dma((EDGES,)),
            dma((EDGES,)), dma((EDGES,)),
        ],
        compiler_params=pltpu.CompilerParams(
            collective_id=0, has_side_effects=True, vmem_limit_bytes=63 * 1024 * 1024
        ),
        cost_estimate=pl.CostEstimate(
            flops=2_500_000_000, bytes_accessed=4_000_000, transcendentals=2_000_000
        ),
        name="joint_backward",
    )(
        slab_offsets, text_count, slab_query, slab_output, slab_cotangent, slab_logsum.T,
        image_keys, image_values, text_query, text_keys, text_values, text_output,
        text_cotangent, text_logsum.T, tables(),
    )
    shapes = [
        jax.ShapeDtypeStruct(x.shape, BF)
        for x in (slab_query, image_keys, image_values, text_query, text_keys, text_values)
    ]
    return pl.pallas_call(
        deliver, out_shape=shapes, in_specs=[vmem] * 3, out_specs=[vmem] * 6, name="deliver"
    )(sqo, okv, txo)


def solution(mesh):
    tokens = P(("rep", "blk", "head"), None)
    text = P("rep", "head")
    in_specs = (
        tokens, tokens, tokens, P(("rep", "blk"), "head"), tokens, tokens,
        text, text, text, text, text, text, P("rep"), P("rep"),
    )
    out_specs = (tokens, tokens, tokens, text, text, text)
    return jax.shard_map(
        on_device, mesh=mesh, in_specs=in_specs, out_specs=out_specs, check_vma=False
    )
```

```python
import jax
import jax.numpy as jnp
import numpy as np
from jax import lax
from jax.experimental import pallas as pl
from jax.experimental.pallas import tpu as pltpu
from jax.sharding import PartitionSpec as P

HEAD_DIM = 128
FACTOR = HEAD_DIM ** (-0.5)
NZ = 8
NX = 4
NB = NX * NX
HD = 3
W = HD * HEAD_DIM
ALL = NZ * W
TXT = 256
HALF = TXT // 2
ROWS = 64
KEYS = 256
SLAB_Q = NB * ROWS
STEP = 256
SILENT = 1e30
BF = jnp.bfloat16
F32 = jnp.float32
MESH = pl.DeviceIdType.MESH

TREE = (
    ((1, 0), (0, 0), (1, 0)),
    ((-1, 0), (0, 0), (-1, 0)),
    ((0, 1), (0, 0), (0, 1)),
    ((0, -1), (0, 0), (0, -1)),
    ((1, 1), (0, 0), (1, 1)),
    ((1, -1), (0, 0), (1, -1)),
    ((-1, 1), (0, 0), (-1, 1)),
    ((-1, -1), (0, 0), (-1, -1)),
    ((2, 0), (-1, 0), (-1, 0)),
    ((0, 2), (0, -1), (0, -1)),
    ((2, 1), (1, 1), (1, 0)),
    ((2, -1), (-1, -1), (-1, 0)),
    ((1, 2), (1, 1), (0, 1)),
    ((-1, 2), (-1, 1), (0, 1)),
    ((2, 2), (1, -1), (1, -1)),
)
EDGES = len(TREE)
BELOW = {child: [k for k, e in enumerate(TREE) if e[1] == child] for child, _, _ in TREE}
RELAYS = (1, 3, 4, 7, 6, 5)
LEAVES = (14, 8, 9, 10, 11, 12, 13, 0, 2)
AROUND = [e[2] for e in TREE[:8]]


def tables():
    place = np.arange(512, dtype=np.float64)[:, None]
    frequency = 10000.0 ** (-np.arange(32, dtype=np.float64) / 32)
    angles = np.tile(place * frequency[None, :], (1, 4))
    sign = np.where(np.arange(128) < 64, -1.0, 1.0)
    return np.stack([np.cos(angles), np.sin(angles) * sign]).astype(np.float32)


def nt(a, b):
    return lax.dot_general(a, b, (((1,), (1,)), ((), ())), preferred_element_type=F32)


def nn(a, b):
    return lax.dot_general(a, b, (((1,), (0,)), ((), ())), preferred_element_type=F32)


def turn(x, cosine, sine):
    return x * cosine + pltpu.roll(x, 64, 1) * sine


def turn_back(x, cosine, sine):
    return x * cosine - pltpu.roll(x, 64, 1) * sine


def cols(n):
    return slice(n * HEAD_DIM, (n + 1) * HEAD_DIM)


def attend(keys, keys_t, values, queries, cotan, logsum, delta, mask=None):
    p = jnp.exp(nt(keys, queries) * FACTOR - logsum)
    if mask is not None:
        p = p * mask
    dv = nn(p.astype(BF), cotan)
    dp = nt(values, cotan)
    ds = (p * (dp - delta) * FACTOR).astype(BF)
    return nn(keys_t, ds).T, nn(ds, queries), dv


def kernel(
    off_ref, cnt_ref, sq_h, so_h, sg_h, sl_h, ik_h, iv_h, tq_h, tk_h, tv_h, to_h, tg_h, tl_h, tab_h,
    sqo, okv, txo,
    sq, so, sg, sl, ik, iv, tq, tk, tv, to, tg, tl, tab,
    qgs, dls, qgr, dlr, kvs, kv, qg, st, stp, tkr, tst, qtk, dqt, dkvt, xt,
    dq, dkv, xs, xk, dkvs, rs_s, rs_r, tk_s, tk_r, sqs, sqr, tx, tkx,
    s_in, s_z, r_zqg, r_zd, s_kv, r_kv, s_xy, r_xy, s_st, r_st, s_sib, r_sib, s_skv, r_skv, s_sd, r_sd,
    s_o, r_o, s_oq, r_oq, s_rs, r_rs, s_tx, r_tx, s_tk, r_tk, s_tkx, r_tkx,
):
    blk = lax.axis_index("blk")
    h = lax.axis_index("head")
    c = lax.rem(blk, 2)
    b = blk // 2
    bx = b // NX
    by = lax.rem(b, NX)
    lane = lax.broadcasted_iota(jnp.int32, (1, HEAD_DIM), 1)
    sub = lax.broadcasted_iota(jnp.int32, (8, 1), 0)
    first = lax.rem(lane, 64) < 32
    sib = {"blk": 2 * b + 1 - c}

    side = h // (NZ // 2)

    def zdev(t):
        over = (1 - side) * (NZ // 2) + lax.rem(h + t, NZ // 2)
        near = side * (NZ // 2) + lax.rem(h + t, NZ // 2)
        return jnp.where(t <= NZ // 2, over, near)

    def chip(dx, dy):
        return lax.rem(bx + dx + NX, NX) * NX + lax.rem(by + dy + NX, NX)

    def on_chip(e):
        return {"blk": 2 * e + c}

    def remote(src, dst, ss, rs, dev):
        return pltpu.make_async_remote_copy(
            src_ref=src, dst_ref=dst, send_sem=ss, recv_sem=rs, device_id=dev, device_id_type=MESH
        )

    def rows_of(e, count):
        return pl.ds(pl.multiple_of(e * count, count), count)

    def wide(d):
        return rows_of(d, W)

    def fetch(i, src, dst):
        copy = pltpu.make_async_copy(src, dst, s_in.at[i])
        copy.start()
        return copy

    f_slab = [fetch(1, sq_h, sq), fetch(2, sg_h, sg), fetch(3, so_h, so)]
    f_tab = fetch(0, tab_h, tab)
    f_k = fetch(4, ik_h, ik)
    f_v = fetch(5, iv_h, iv)
    f_text = [
        fetch(6, tq_h, tq), fetch(7, tg_h, tg), fetch(8, to_h, to), fetch(9, tk_h, tk),
        fetch(10, tv_h, tv), fetch(11, tl_h, tl), fetch(12, sl_h, sl),
    ]

    bar = pltpu.get_barrier_semaphore()

    def greet_z(t, carry):
        pl.semaphore_signal(bar, inc=1, device_id={"head": zdev(t)}, device_id_type=MESH)
        return carry

    lax.fori_loop(1, NZ, greet_z, 0)
    for dx, dy in AROUND:
        pl.semaphore_signal(bar, inc=1, device_id=on_chip(chip(dx, dy)), device_id_type=MESH)
    pl.semaphore_signal(bar, inc=1, device_id=sib, device_id_type=MESH)

    cos_t, sin_t = tab.at[0], tab.at[1]

    def angles(row, start, count):
        ct = cos_t[pl.ds(start, count), :]
        sn = sin_t[pl.ds(start, count), :]
        cr = cos_t[pl.ds(row, 1), :]
        sr = sin_t[pl.ds(row, 1), :]
        return jnp.where(first, cr, ct), jnp.where(first, sr, sn)

    place = off_ref[0] + blk
    row_at = lax.broadcasted_iota(jnp.int32, (32, 1), 0) == place // 4
    col_at = lax.rem(place, 4)

    def slab_angles(start, count):
        result = []
        for table in (cos_t, sin_t):
            row = jnp.sum(jnp.where(row_at, table[:32, :], 0.0), axis=0, keepdims=True)
            col = table[pl.ds(start, count), :]
            for i in range(1, 4):
                col = jnp.where(col_at == i, table[pl.ds(64 * i + start, count), :], col)
            result.append(jnp.where(first, row, col))
        return result

    f_tab.wait()
    for copy in f_slab:
        copy.wait()
    cq, sn_q = slab_angles(pl.multiple_of(8 * h, 8), 8)
    for d in range(NZ):
        acc = jnp.zeros((8, HEAD_DIM), F32)
        for j in range(HD):
            n = d * HD + j
            g = sg[:, cols(n)].astype(F32)
            q = turn(sq[:, cols(n)].astype(F32), cq, sn_q)
            qgs[d, :, cols(j)] = jnp.concatenate([q, g], axis=0).astype(BF)
            own = jnp.sum(g * so[:, cols(n)].astype(F32), axis=1, keepdims=True)
            acc = jnp.where(lane == 8 * j + sub, own, acc)
        dls[d] = jnp.sum(acc, axis=0, keepdims=True)
    pl.semaphore_wait(bar, NZ + len(AROUND))

    def z_qg(t, d):
        return remote(qgs.at[d], qgr.at[h], s_z.at[0, t], r_zqg.at[h], {"head": d})

    def z_dl(t, d):
        return remote(dls.at[d], dlr.at[h], s_z.at[1, t], r_zd.at[h], {"head": d})

    def key_rows(s):
        return pl.ds(pl.multiple_of(c * KEYS + s * 32, 32), 32)

    def z_kv(j, t, d):
        return remote(
            kvs.at[d * HD + j], kv.at[j, :, key_rows(h), :], s_kv.at[j, t], r_kv.at[j, h], {"head": d}
        )

    def go_qg(t, carry):
        z_qg(t, zdev(t)).start()
        z_dl(t, zdev(t)).start()
        return carry

    lax.fori_loop(1, NZ, go_qg, 0)
    f_k.wait()
    f_v.wait()
    ck, sn_k = angles(blk, pl.multiple_of(32 * h, 32), 32)
    for j in range(HD):
        for d in range(NZ):
            n = d * HD + j
            kvs[n, 0] = turn(ik[:, cols(n)].astype(F32), ck, sn_k).astype(BF)
            kvs[n, 1] = iv[:, cols(n)]

        def go_kv(t, carry, j=j):
            z_kv(j, t, zdev(t)).start()
            return carry

        lax.fori_loop(1, NZ, go_kv, 0)
        kv[j, :, key_rows(h), :] = kvs[h * HD + j]
    qgr[h] = qgs[h]
    dlr[h] = dls[h]

    for copy in f_text:
        copy.wait()
    half = rows_of(c, HALF)
    text_at = pl.ds(pl.multiple_of(TXT + HALF * c, HALF), HALF)
    ct = cos_t[text_at, :]
    sn = sin_t[text_at, :]
    acc = jnp.zeros((HALF, HEAD_DIM), F32)
    for j in range(HD):
        g = tg[half, cols(j)]
        qg[j, 0, SLAB_Q:, :] = turn(tq[half, cols(j)].astype(F32), ct, sn).astype(BF)
        qg[j, 1, SLAB_Q:, :] = g
        own = jnp.sum(g.astype(F32) * to[half, cols(j)].astype(F32), axis=1, keepdims=True)
        acc = jnp.where(lane == j, own, acc)
        tkr[j] = turn(tk[:, cols(j)].astype(F32), cos_t[TXT:, :], sin_t[TXT:, :]).astype(BF)
    stp[:, SLAB_Q:] = acc.T[:8, :]
    stp[HD : 2 * HD, SLAB_Q:] = tl[:, half]

    def wait_qg(t, carry):
        s = zdev(t)
        remote(qgs.at[s], qgr.at[s], s_z.at[0, t], r_zqg.at[s], {"head": s}).wait_recv()
        remote(dls.at[s], dlr.at[s], s_z.at[1, t], r_zd.at[s], {"head": s}).wait_recv()
        return carry

    lax.fori_loop(1, NZ, wait_qg, 0)
    my_rows = rows_of(b, ROWS)
    odd = lax.rem(b, 2) == 1
    delta = dlr[...].reshape(NZ, HEAD_DIM)
    shift = ROWS * lax.rem(b, 2)
    here = (lane // 64) == lax.rem(b, 2)
    logs = jnp.concatenate([sl[...], sl[...]], axis=1)
    st[b] = jnp.zeros((8, HEAD_DIM), F32)
    moved = [pltpu.roll(delta[i : i + 1, :], 8 * i, 1) if i else delta[:1, :] for i in range(NZ)]
    for j in range(HD):
        row = jnp.zeros((1, HEAD_DIM), F32)
        for i in range(NZ):
            row = jnp.where(lane // 8 == i + j, moved[i], row)
        st[b, j : j + 1, :] = pltpu.roll(row, lax.rem(shift + HEAD_DIM - 8 * j, HEAD_DIM), 1)
    st[b, HD : 2 * HD, :] = jnp.where(here, logs, 0.0)

    def ag(j, k, s, e):
        block = qg.at[j, :, rows_of(s, ROWS), :]
        return remote(block, block, s_xy.at[j, k], r_xy.at[j, k], on_chip(e))

    def ag_st(k, s, e):
        return remote(st.at[s], st.at[s], s_st.at[k], r_st.at[k], on_chip(e))

    def source(k):
        return chip(-TREE[k][0][0], -TREE[k][0][1])

    def from_parent(k, copy):
        _, (px, py), (dx, dy) = TREE[k]
        return copy(k, chip(-px, -py), chip(dx, dy))

    def ag_of(j):
        return lambda k, s, e: ag(j, k, s, e)

    for j in range(HD):
        both = qgr[:, :, cols(j)].astype(F32)
        qg[j, 0, my_rows, :] = both[:, :8, :].reshape(ROWS, HEAD_DIM).astype(BF)
        qg[j, 1, my_rows, :] = both[:, 8:, :].reshape(ROWS, HEAD_DIM).astype(BF)
        for k in range(8):
            if j == 0:
                from_parent(k, ag_st).start()
            from_parent(k, ag_of(j)).start()

    def ag_relay(j):
        for k in RELAYS:
            if j == 0:
                ag_st(k, source(k), b).wait_recv()
            ag(j, k, source(k), b).wait_recv()
            for child in BELOW[TREE[k][0]]:
                if j == 0:
                    from_parent(child, ag_st).start()
                from_parent(child, ag_of(j)).start()

    def ag_rest(j):
        for k in range(EDGES):
            if k not in RELAYS:
                if j == 0:
                    ag_st(k, source(k), b).wait_recv()
                ag(j, k, source(k), b).wait_recv()

    pair = pl.multiple_of(16 * (b // 2), 16)
    own_st = st[b]
    own_st = jnp.where(odd, pltpu.roll(own_st, 64, 1), own_st)
    text_st = pltpu.roll(stp[:, SLAB_Q:], lax.rem(ROWS - pair + HEAD_DIM, HEAD_DIM), 1)
    mine_at = lane // 8 == ROWS // 8 + lax.rem(b, 2)
    stat_row = lax.broadcasted_iota(jnp.int32, (8, 1), 0)
    silent = jnp.where(jnp.logical_and(stat_row >= HD, stat_row < 2 * HD), SILENT, 0.0)
    tst[...] = jnp.where(lane < ROWS, own_st, jnp.where(mine_at, text_st, silent))
    key_index = lax.broadcasted_iota(jnp.int32, (TXT, 1), 0)
    mask = (key_index < cnt_ref[0]).astype(F32)

    def text_keys(j):
        for i in range(2):
            qtk[i, :ROWS, :] = qg[j, i, my_rows, :]
            qtk[i, ROWS : ROWS + 16, :] = qg[j, i, pl.ds(SLAB_Q + pair, 16), :]
            qtk[i, ROWS + 16 :, :] = jnp.zeros((HEAD_DIM - ROWS - 16, HEAD_DIM), BF)
        keys = tkr[j]
        one_q, one_k, one_v = attend(
            keys, keys.T, tv[:, cols(j)], qtk[0], qtk[1],
            tst[HD + j : HD + j + 1, :], tst[j : j + 1, :], mask,
        )
        dqt[j] = one_q
        dkvt[j, 0] = one_k
        dkvt[j, 1] = one_v

    mine = rows_of(c, KEYS)
    theirs = rows_of(1 - c, KEYS)

    def sib_kv(j, rows):
        part = kv.at[j, :, rows, :]
        return remote(part, part, s_skv.at[j], r_skv.at[j], sib)

    def share_kv(j):
        def wait_kv(t, carry):
            s = zdev(t)
            remote(
                kvs.at[s * HD + j], kv.at[j, :, key_rows(s), :], s_kv.at[j, t], r_kv.at[j, s], {"head": s}
            ).wait_recv()
            return carry

        lax.fori_loop(1, NZ, wait_kv, 0)
        sib_kv(j, mine).start()

    text_keys(0)
    ag_relay(0)
    text_keys(1)
    share_kv(0)
    ag_relay(1)
    text_keys(2)
    other = rows_of(1 - c, HALF)
    sib_t = remote(dkvt.at[:, :, other, :], xt, s_sib.at[0], r_sib.at[0], sib)
    sib_t.start()
    ag_rest(0)
    for i in range(NB // 2):
        stp[:, cols(i)] = st[2 * i] + st[2 * i + 1]

    def image_keys(j, keys_t, rows, start):
        one_q, one_k, one_v = attend(
            kv[j, 0], keys_t, kv[j, 1], qg[j, 0, rows, :], qg[j, 1, rows, :],
            stp[HD + j : HD + j + 1, rows], stp[j : j + 1, rows],
        )
        dq[j, rows, :] = one_q
        if start:
            dkv[j, 0] = one_k
            dkv[j, 1] = one_v
        else:
            dkv[j, 0] += one_k
            dkv[j, 1] += one_v

    def sib_d(j):
        return remote(xs.at[j], xk.at[j], s_sd.at[j], r_sd.at[j], sib)

    ck, sn_k = angles(blk, 0, KEYS)

    def token_rows(s):
        return rows_of(s, 32)

    def z_out(j, t, d):
        return remote(
            dkvs.at[j, :, token_rows(d), :], okv.at[h * HD + j], s_o.at[j, t], r_o.at[j, h], {"head": d}
        )

    def finish_kv(j):
        sib_d(j).wait()
        dkvs[j, 0] = turn_back(dkv[j, 0, mine, :] + xk[j, 0].astype(F32), ck, sn_k).astype(BF)
        dkvs[j, 1] = (dkv[j, 1, mine, :] + xk[j, 1].astype(F32)).astype(BF)

        def go_out(t, carry):
            z_out(j, t, zdev(t)).start()
            return carry

        lax.fori_loop(1, NZ, go_out, 0)
        okv[h * HD + j] = dkvs[j, :, token_rows(h), :]

    def make_sum(own, copy, sent, got):
        def gather(e, below):
            value = own(e)
            for k in below:
                copy(k).wait_recv()
                value = value + got[k].astype(F32)
            return value

        def pass_on(some):
            for k in some:
                sent[k] = gather(source(k), BELOW[TREE[k][0]]).astype(BF)
                copy(k).start()

        return gather, pass_on

    def towards_root(k, src, dst, ss, rs):
        dx, dy = TREE[k][2]
        return remote(src, dst, ss, rs, on_chip(chip(-dx, -dy)))

    def rs_copy(j, k):
        return towards_root(k, rs_s.at[j, k], rs_r.at[j, k], s_rs.at[j, k], r_rs.at[j, k])

    def tk_copy(k):
        return towards_root(k, tk_s.at[k], tk_r.at[k], s_tk.at[k], r_tk.at[k])

    def own_rows(j):
        def own(e):
            text = dq[j, pl.ds(pl.multiple_of(SLAB_Q + e * 8, 8), 8), :]
            return jnp.concatenate([dq[j, rows_of(e, ROWS), :], text, jnp.zeros_like(text)], axis=0)

        return own

    def own_text(e):
        at = rows_of(e, 8)
        at_half = pl.ds(pl.multiple_of(HALF * c + e * 8, 8), 8)
        heads = [
            jnp.concatenate([dkvt[j, i, at_half, :] + xt[j, i, at, :] for i in range(2)], axis=0)
            for j in range(HD)
        ]
        return jnp.concatenate(heads, axis=1)

    rs_sums = [
        make_sum(own_rows(j), lambda k, j=j: rs_copy(j, k), rs_s.at[j], rs_r.at[j]) for j in range(HD)
    ]
    tk_gather, tk_pass = make_sum(own_text, tk_copy, tk_s, tk_r)

    def tx_copy(k, s, e):
        return remote(tx.at[c, s], tx.at[c, s], s_tx.at[k], r_tx.at[k], on_chip(e))

    def tkx_copy(k, s, e):
        return remote(tkx.at[c, s], tkx.at[c, s], s_tkx.at[k], r_tkx.at[k], on_chip(e))

    def spread_out(copy):
        for k in range(8):
            from_parent(k, copy).start()

    def spread_on(copy):
        for k in RELAYS:
            copy(k, source(k), b).wait_recv()
            for child in BELOW[TREE[k][0]]:
                from_parent(child, copy).start()

    def spread_end(copy):
        for k in range(EDGES):
            if k not in RELAYS:
                copy(k, source(k), b).wait_recv()

    own_at = pl.ds(pl.multiple_of(TXT + HALF * c + 8 * b, 8), 8)
    ct = cos_t[own_at, :]
    sn = sin_t[own_at, :]

    def text_key_result():
        total = tk_gather(b, range(8))
        for j in range(HD):
            tkx[c, b, :, cols(j)] = jnp.concatenate(
                [turn_back(total[:8, cols(j)], ct, sn), total[8:, cols(j)]], axis=0
            ).astype(BF)
        spread_out(tkx_copy)

    sib_tkx = remote(tkx.at[c], tkx.at[c], s_sib.at[2], r_sib.at[2], sib)
    sib_tx = remote(tx.at[c], tx.at[c], s_sib.at[1], r_sib.at[1], sib)

    sib_t.wait()
    tk_pass(LEAVES)
    for j in range(HD):
        if j > 0:
            ag_rest(j)
        sib_kv(j, theirs).wait_recv()
        if j == 0:
            ag_relay(2)
        keys_t = kv[j, 0].T
        image_keys(j, keys_t, slice(SLAB_Q, SLAB_Q + HALF), True)
        for i in range(SLAB_Q // STEP):
            image_keys(j, keys_t, slice(i * STEP, (i + 1) * STEP), False)
            if i == 1 and j > 0:
                finish_kv(j - 1)
        if j == HD - 1:
            rs_sums[j][1](LEAVES)
        xs[j] = dkv[j, :, theirs, :].astype(BF)
        sib_d(j).start()
        if j == 0:
            share_kv(1)
            rs_sums[0][1](LEAVES)
            tk_pass(RELAYS)
        elif j == 1:
            rs_sums[1][1](LEAVES)
            rs_sums[0][1](RELAYS)
            share_kv(2)
            text_key_result()
        else:
            rs_sums[1][1](RELAYS)

    cq, sn_q = slab_angles(0, ROWS)

    def own_result(j):
        total = rs_sums[j][0](b, range(8))
        extra = jnp.where(odd, dqt[j, ROWS + 8 : ROWS + 16, :], dqt[j, ROWS : ROWS + 8, :])
        text = turn_back(total[ROWS : ROWS + 8, :] + extra, ct, sn)
        return turn_back(total[:ROWS, :] + dqt[j, :ROWS, :], cq, sn_q).reshape(NZ, 8, HEAD_DIM), text

    def out_q(i, t, d):
        return remote(sqs.at[d, i], sqr.at[h, i], s_oq.at[i, t], r_oq.at[i, h], {"head": d})

    def send_q(i):
        def go_oq(t, carry):
            out_q(i, t, zdev(t)).start()
            return carry

        lax.fori_loop(1, NZ, go_oq, 0)
        sqr[h, i] = sqs[h, i]

    part_0, text_0 = own_result(0)
    finish_kv(HD - 1)
    rs_sums[HD - 1][1](RELAYS)
    part_1, text_1 = own_result(1)
    sqs[:, 0] = jnp.concatenate([part_0, part_1], axis=1).astype(BF)
    send_q(0)
    spread_on(tkx_copy)
    part_2, text_2 = own_result(2)
    sqs[:, 1] = jnp.concatenate([part_2, jnp.zeros_like(part_2)], axis=1).astype(BF)
    send_q(1)
    tx[c, b, :, :HEAD_DIM] = jnp.concatenate([text_0, text_2], axis=0).astype(BF)
    tx[c, b, :, HEAD_DIM:] = jnp.concatenate([text_1, jnp.zeros_like(text_1)], axis=0).astype(BF)
    spread_out(tx_copy)
    spread_end(tkx_copy)
    sib_tkx.start()
    spread_on(tx_copy)
    spread_end(tx_copy)
    sib_tx.start()

    def wait_oq(t, carry):
        s = zdev(t)
        for i in range(2):
            remote(sqs.at[s, i], sqr.at[s, i], s_oq.at[i, t], r_oq.at[i, s], {"head": s}).wait_recv()
        return carry

    lax.fori_loop(1, NZ, wait_oq, 0)
    for s in range(NZ):
        piece = sqr[s].astype(F32)
        for j in range(HD):
            sqo[:, cols(s * HD + j)] = piece[j // 2, 8 * (j % 2) : 8 * (j % 2) + 8, :].astype(BF)
    remote(tkx.at[1 - c], tkx.at[1 - c], s_sib.at[2], r_sib.at[2], sib).wait_recv()
    for core in range(2):
        rows = slice(core * HALF, (core + 1) * HALF)
        block = tkx[core].astype(F32)
        txo[1, rows, :] = block[:, :8, :].reshape(HALF, W).astype(BF)
        txo[2, rows, :] = block[:, 8:, :].reshape(HALF, W).astype(BF)
    remote(tx.at[1 - c], tx.at[1 - c], s_sib.at[1], r_sib.at[1], sib).wait_recv()
    for core in range(2):
        rows = slice(core * HALF, (core + 1) * HALF)
        block = tx[core].astype(F32)
        txo[0, rows, :HEAD_DIM] = block[:, :8, :HEAD_DIM].reshape(HALF, HEAD_DIM).astype(BF)
        txo[0, rows, HEAD_DIM : 2 * HEAD_DIM] = block[:, :8, HEAD_DIM:].reshape(HALF, HEAD_DIM).astype(BF)
        txo[0, rows, 2 * HEAD_DIM :] = block[:, 8:, :HEAD_DIM].reshape(HALF, HEAD_DIM).astype(BF)
    for j in range(HD):

        def wait_out(t, carry, j=j):
            s = zdev(t)
            remote(
                dkvs.at[j, :, token_rows(s), :], okv.at[s * HD + j], s_o.at[j, t], r_o.at[j, s], {"head": s}
            ).wait_recv()
            return carry

        lax.fori_loop(1, NZ, wait_out, 0)

    def drain_z(t, carry):
        d = zdev(t)
        z_qg(t, d).wait_send()
        z_dl(t, d).wait_send()
        out_q(0, t, d).wait_send()
        out_q(1, t, d).wait_send()
        for j in range(HD):
            z_kv(j, t, d).wait_send()
            z_out(j, t, d).wait_send()
        return carry

    lax.fori_loop(1, NZ, drain_z, 0)
    for k in range(EDGES):
        from_parent(k, ag_st).wait_send()
        from_parent(k, tx_copy).wait_send()
        from_parent(k, tkx_copy).wait_send()
        tk_copy(k).wait_send()
        for j in range(HD):
            from_parent(k, ag_of(j)).wait_send()
            rs_copy(j, k).wait_send()
    for j in range(HD):
        sib_kv(j, mine).wait_send()
    sib_tx.wait_send()
    sib_tkx.wait_send()


def deliver(sqo, okv, txo, sqg, ikg, ivg, tqg, tkg, tvg):
    sqg[...] = sqo[...]
    for n in range(NZ * HD):
        ikg[:, cols(n)] = okv[n, 0]
        ivg[:, cols(n)] = okv[n, 1]
    tqg[...] = txo[0]
    tkg[...] = txo[1]
    tvg[...] = txo[2]


def on_device(
    slab_query, slab_output, slab_cotangent, slab_logsum, image_keys, image_values,
    text_query, text_keys, text_values, text_output, text_cotangent, text_logsum,
    text_count, slab_offsets,
):
    vmem = pl.BlockSpec(memory_space=pltpu.VMEM)
    smem = pl.BlockSpec(memory_space=pltpu.SMEM)
    hbm = pl.BlockSpec(memory_space=pltpu.HBM)
    dma = pltpu.SemaphoreType.DMA
    slab = pltpu.VMEM((8, ALL), BF)
    text = pltpu.VMEM((TXT, W), BF)
    sqo, okv, txo = pl.pallas_call(
        kernel,
        out_shape=[
            jax.ShapeDtypeStruct((8, ALL), BF),
            jax.ShapeDtypeStruct((NZ * HD, 2, 32, HEAD_DIM), BF),
            jax.ShapeDtypeStruct((3, TXT, W), BF),
        ],
        in_specs=[smem, smem] + [hbm] * 13,
        out_specs=[vmem] * 3,
        scratch_shapes=[
            slab, slab, slab,
            pltpu.VMEM((HD, ROWS), F32),
            pltpu.VMEM((32, ALL), BF),
            pltpu.VMEM((32, ALL), BF),
            text, text, text, text, text,
            pltpu.VMEM((HD, TXT), F32),
            pltpu.VMEM((2, 512, HEAD_DIM), F32),
            pltpu.VMEM((NZ, 16, W), BF),
            pltpu.VMEM((NZ, 1, HEAD_DIM), F32),
            pltpu.VMEM((NZ, 16, W), BF),
            pltpu.VMEM((NZ, 1, HEAD_DIM), F32),
            pltpu.VMEM((NZ * HD, 2, 32, HEAD_DIM), BF),
            pltpu.VMEM((HD, 2, 2 * KEYS, HEAD_DIM), BF),
            pltpu.VMEM((HD, 2, SLAB_Q + HALF, HEAD_DIM), BF),
            pltpu.VMEM((NB, 8, HEAD_DIM), F32),
            pltpu.VMEM((8, SLAB_Q + HALF), F32),
            pltpu.VMEM((HD, TXT, HEAD_DIM), BF),
            pltpu.VMEM((8, HEAD_DIM), F32),
            pltpu.VMEM((2, HEAD_DIM, HEAD_DIM), BF),
            pltpu.VMEM((HD, HEAD_DIM, HEAD_DIM), F32),
            pltpu.VMEM((HD, 2, TXT, HEAD_DIM), F32),
            pltpu.VMEM((HD, 2, HALF, HEAD_DIM), F32),
            pltpu.VMEM((HD, SLAB_Q + HALF, HEAD_DIM), F32),
            pltpu.VMEM((HD, 2, 2 * KEYS, HEAD_DIM), F32),
            pltpu.VMEM((HD, 2, KEYS, HEAD_DIM), BF),
            pltpu.VMEM((HD, 2, KEYS, HEAD_DIM), BF),
            pltpu.VMEM((HD, 2, KEYS, HEAD_DIM), BF),
            pltpu.VMEM((HD, EDGES, 80, HEAD_DIM), BF),
            pltpu.VMEM((HD, EDGES, 80, HEAD_DIM), BF),
            pltpu.VMEM((EDGES, 16, W), BF),
            pltpu.VMEM((EDGES, 16, W), BF),
            pltpu.VMEM((NZ, 2, 16, HEAD_DIM), BF),
            pltpu.VMEM((NZ, 2, 16, HEAD_DIM), BF),
            pltpu.VMEM((2, NB, 16, 256), BF),
            pltpu.VMEM((2, NB, 16, W), BF),
            dma((13,)),
            dma((2, NZ)), dma((NZ,)), dma((NZ,)),
            dma((HD, NZ)), dma((HD, NZ)),
            dma((HD, EDGES)), dma((HD, EDGES)),
            dma((EDGES,)), dma((EDGES,)),
            dma((3,)), dma((3,)),
            dma((HD,)), dma((HD,)), dma((HD,)), dma((HD,)),
            dma((HD, NZ)), dma((HD, NZ)),
            dma((2, NZ)), dma((2, NZ)),
            dma((HD, EDGES)), dma((HD, EDGES)),
            dma((EDGES,)), dma((EDGES,)),
            dma((EDGES,)), dma((EDGES,)),
            dma((EDGES,)), dma((EDGES,)),
        ],
        compiler_params=pltpu.CompilerParams(
            collective_id=0, has_side_effects=True, vmem_limit_bytes=63 * 1024 * 1024
        ),
        cost_estimate=pl.CostEstimate(
            flops=2_500_000_000, bytes_accessed=4_000_000, transcendentals=2_000_000
        ),
        name="joint_backward",
    )(
        slab_offsets, text_count, slab_query, slab_output, slab_cotangent, slab_logsum.T,
        image_keys, image_values, text_query, text_keys, text_values, text_output,
        text_cotangent, text_logsum.T, tables(),
    )
    shapes = [
        jax.ShapeDtypeStruct(x.shape, BF)
        for x in (slab_query, image_keys, image_values, text_query, text_keys, text_values)
    ]
    return pl.pallas_call(
        deliver, out_shape=shapes, in_specs=[vmem] * 3, out_specs=[vmem] * 6, name="deliver"
    )(sqo, okv, txo)


def solution(mesh):
    tokens = P(("rep", "blk", "head"), None)
    text = P("rep", "head")
    in_specs = (
        tokens, tokens, tokens, P(("rep", "blk"), "head"), tokens, tokens,
        text, text, text, text, text, text, P("rep"), P("rep"),
    )
    out_specs = (tokens, tokens, tokens, text, text, text)
    return jax.shard_map(
        on_device, mesh=mesh, in_specs=in_specs, out_specs=out_specs, check_vma=False
    )
```

```python
import jax
import jax.numpy as jnp
import numpy as np
from jax import lax
from jax.experimental import pallas as pl
from jax.experimental.pallas import tpu as pltpu
from jax.sharding import PartitionSpec as P

HEAD_DIM = 128
FACTOR = HEAD_DIM ** (-0.5)
NZ = 8
NX = 4
NB = NX * NX
HD = 3
W = HD * HEAD_DIM
ALL = NZ * W
TXT = 256
HALF = TXT // 2
ROWS = 64
KEYS = 256
SLAB_Q = NB * ROWS
STEP = 256
SILENT = 1e30
BF = jnp.bfloat16
F32 = jnp.float32
MESH = pl.DeviceIdType.MESH

TREE = (
    ((1, 0), (0, 0), (1, 0)),
    ((-1, 0), (0, 0), (-1, 0)),
    ((0, 1), (0, 0), (0, 1)),
    ((0, -1), (0, 0), (0, -1)),
    ((1, 1), (0, 0), (1, 1)),
    ((1, -1), (0, 0), (1, -1)),
    ((-1, 1), (0, 0), (-1, 1)),
    ((-1, -1), (0, 0), (-1, -1)),
    ((2, 0), (-1, 0), (-1, 0)),
    ((0, 2), (0, -1), (0, -1)),
    ((2, 1), (1, 1), (1, 0)),
    ((2, -1), (-1, -1), (-1, 0)),
    ((1, 2), (1, 1), (0, 1)),
    ((-1, 2), (-1, 1), (0, 1)),
    ((2, 2), (1, -1), (1, -1)),
)
EDGES = len(TREE)
BELOW = {child: [k for k, e in enumerate(TREE) if e[1] == child] for child, _, _ in TREE}
RELAYS = (1, 3, 4, 7, 6, 5)
LEAVES = (14, 8, 9, 10, 11, 12, 13, 0, 2)
GATHERED = ((0, 1), (1, 2))
SUMMED = ((0, 2), (2, 1))
AROUND = [e[2] for e in TREE[:8]]


def tables():
    place = np.arange(512, dtype=np.float64)[:, None]
    frequency = 10000.0 ** (-np.arange(32, dtype=np.float64) / 32)
    angles = np.tile(place * frequency[None, :], (1, 4))
    sign = np.where(np.arange(128) < 64, -1.0, 1.0)
    return np.stack([np.cos(angles), np.sin(angles) * sign]).astype(np.float32)


def nt(a, b):
    return lax.dot_general(a, b, (((1,), (1,)), ((), ())), preferred_element_type=F32)


def nn(a, b):
    return lax.dot_general(a, b, (((1,), (0,)), ((), ())), preferred_element_type=F32)


def turn(x, cosine, sine):
    return x * cosine + pltpu.roll(x, 64, 1) * sine


def turn_back(x, cosine, sine):
    return x * cosine - pltpu.roll(x, 64, 1) * sine


def cols(n):
    return slice(n * HEAD_DIM, (n + 1) * HEAD_DIM)


def attend(keys, keys_t, values, queries, cotan, logsum, delta, mask=None):
    p = jnp.exp(nt(keys, queries) * FACTOR - logsum)
    if mask is not None:
        p = p * mask
    dv = nn(p.astype(BF), cotan)
    dp = nt(values, cotan)
    ds = (p * (dp - delta) * FACTOR).astype(BF)
    return nn(keys_t, ds).T, nn(ds, queries), dv


def kernel(
    off_ref, cnt_ref, sq_h, so_h, sg_h, sl_h, ik_h, iv_h, tq_h, tk_h, tv_h, to_h, tg_h, tl_h, tab_h,
    sqo, okv, txo,
    sq, so, sg, sl, ik, iv, tq, tk, tv, to, tg, tl, tab,
    qgs, dls, qgr, dlr, kvs, kv, qg, st, stp, tkr, tst, qtk, dqt, dkvt, xt,
    dq, dkv, xs, xk, dkvs, rs_s, rs_r, tk_s, tk_r, sqs, sqr, tx, tkx,
    s_in, s_z, r_zqg, r_zd, s_kv, r_kv, s_xy, r_xy, s_st, r_st, s_sib, r_sib, s_skv, r_skv, s_sd, r_sd,
    s_o, r_o, s_oq, r_oq, s_rs, r_rs, s_tx, r_tx, s_tk, r_tk, s_tkx, r_tkx,
):
    blk = lax.axis_index("blk")
    h = lax.axis_index("head")
    c = lax.rem(blk, 2)
    b = blk // 2
    bx = b // NX
    by = lax.rem(b, NX)
    lane = lax.broadcasted_iota(jnp.int32, (1, HEAD_DIM), 1)
    sub = lax.broadcasted_iota(jnp.int32, (8, 1), 0)
    first = lax.rem(lane, 64) < 32
    sib = {"blk": 2 * b + 1 - c}

    def zdev(t):
        return lax.rem(h + t, NZ)

    def chip(dx, dy):
        return lax.rem(bx + dx + NX, NX) * NX + lax.rem(by + dy + NX, NX)

    def on_chip(e):
        return {"blk": 2 * e + c}

    def remote(src, dst, ss, rs, dev):
        return pltpu.make_async_remote_copy(
            src_ref=src, dst_ref=dst, send_sem=ss, recv_sem=rs, device_id=dev, device_id_type=MESH
        )

    def rows_of(e, count):
        return pl.ds(pl.multiple_of(e * count, count), count)

    def wide(d):
        return rows_of(d, W)

    def fetch(i, src, dst):
        copy = pltpu.make_async_copy(src, dst, s_in.at[i])
        copy.start()
        return copy

    f_slab = [fetch(1, sq_h, sq), fetch(2, sg_h, sg), fetch(3, so_h, so)]
    f_tab = fetch(0, tab_h, tab)
    f_k = fetch(4, ik_h, ik)
    f_v = fetch(5, iv_h, iv)
    f_text = [
        fetch(6, tq_h, tq), fetch(7, tg_h, tg), fetch(8, to_h, to), fetch(9, tk_h, tk),
        fetch(10, tv_h, tv), fetch(11, tl_h, tl), fetch(12, sl_h, sl),
    ]

    bar = pltpu.get_barrier_semaphore()

    def greet_z(t, carry):
        pl.semaphore_signal(bar, inc=1, device_id={"head": zdev(t)}, device_id_type=MESH)
        return carry

    lax.fori_loop(1, NZ, greet_z, 0)
    for dx, dy in AROUND:
        pl.semaphore_signal(bar, inc=1, device_id=on_chip(chip(dx, dy)), device_id_type=MESH)
    pl.semaphore_signal(bar, inc=1, device_id=sib, device_id_type=MESH)

    cos_t, sin_t = tab.at[0], tab.at[1]

    def angles(row, start, count):
        ct = cos_t[pl.ds(start, count), :]
        sn = sin_t[pl.ds(start, count), :]
        cr = cos_t[pl.ds(row, 1), :]
        sr = sin_t[pl.ds(row, 1), :]
        return jnp.where(first, cr, ct), jnp.where(first, sr, sn)

    place = off_ref[0] + blk
    row_at = lax.broadcasted_iota(jnp.int32, (32, 1), 0) == place // 4
    col_at = lax.rem(place, 4)

    def slab_angles(start, count):
        result = []
        for table in (cos_t, sin_t):
            row = jnp.sum(jnp.where(row_at, table[:32, :], 0.0), axis=0, keepdims=True)
            col = table[pl.ds(start, count), :]
            for i in range(1, 4):
                col = jnp.where(col_at == i, table[pl.ds(64 * i + start, count), :], col)
            result.append(jnp.where(first, row, col))
        return result

    f_tab.wait()
    for copy in f_slab:
        copy.wait()
    cq, sn_q = slab_angles(pl.multiple_of(8 * h, 8), 8)
    for d in range(NZ):
        acc = jnp.zeros((8, HEAD_DIM), F32)
        for j in range(HD):
            n = d * HD + j
            g = sg[:, cols(n)].astype(F32)
            q = turn(sq[:, cols(n)].astype(F32), cq, sn_q)
            qgs[d, :, cols(j)] = jnp.concatenate([q, g], axis=0).astype(BF)
            own = jnp.sum(g * so[:, cols(n)].astype(F32), axis=1, keepdims=True)
            acc = jnp.where(lane == 8 * j + sub, own, acc)
        dls[d] = jnp.sum(acc, axis=0, keepdims=True)
    pl.semaphore_wait(bar, NZ + len(AROUND))

    def z_qg(t, d):
        return remote(qgs.at[d], qgr.at[h], s_z.at[0, t], r_zqg.at[h], {"head": d})

    def z_dl(t, d):
        return remote(dls.at[d], dlr.at[h], s_z.at[1, t], r_zd.at[h], {"head": d})

    def key_rows(s):
        return pl.ds(pl.multiple_of(c * KEYS + s * 32, 32), 32)

    def z_kv(j, t, d):
        return remote(
            kvs.at[d * HD + j], kv.at[j, :, key_rows(h), :], s_kv.at[j, t], r_kv.at[j, h], {"head": d}
        )

    def go_qg(t, carry):
        z_qg(t, zdev(t)).start()
        z_dl(t, zdev(t)).start()
        return carry

    lax.fori_loop(1, NZ, go_qg, 0)
    f_k.wait()
    f_v.wait()
    ck, sn_k = angles(blk, pl.multiple_of(32 * h, 32), 32)
    for j in range(HD):
        for d in range(NZ):
            n = d * HD + j
            kvs[n, 0] = turn(ik[:, cols(n)].astype(F32), ck, sn_k).astype(BF)
            kvs[n, 1] = iv[:, cols(n)]

        def go_kv(t, carry, j=j):
            z_kv(j, t, zdev(t)).start()
            return carry

        lax.fori_loop(1, NZ, go_kv, 0)
        kv[j, :, key_rows(h), :] = kvs[h * HD + j]
    qgr[h] = qgs[h]
    dlr[h] = dls[h]

    for copy in f_text:
        copy.wait()
    half = rows_of(c, HALF)
    text_at = pl.ds(pl.multiple_of(TXT + HALF * c, HALF), HALF)
    ct = cos_t[text_at, :]
    sn = sin_t[text_at, :]
    acc = jnp.zeros((HALF, HEAD_DIM), F32)
    for j in range(HD):
        g = tg[half, cols(j)]
        qg[j, 0, SLAB_Q:, :] = turn(tq[half, cols(j)].astype(F32), ct, sn).astype(BF)
        qg[j, 1, SLAB_Q:, :] = g
        own = jnp.sum(g.astype(F32) * to[half, cols(j)].astype(F32), axis=1, keepdims=True)
        acc = jnp.where(lane == j, own, acc)
        tkr[j] = turn(tk[:, cols(j)].astype(F32), cos_t[TXT:, :], sin_t[TXT:, :]).astype(BF)
    stp[:, SLAB_Q:] = acc.T[:8, :]
    stp[HD : 2 * HD, SLAB_Q:] = tl[:, half]

    def wait_qg(t, carry):
        s = zdev(t)
        remote(qgs.at[s], qgr.at[s], s_z.at[0, t], r_zqg.at[s], {"head": s}).wait_recv()
        remote(dls.at[s], dlr.at[s], s_z.at[1, t], r_zd.at[s], {"head": s}).wait_recv()
        return carry

    lax.fori_loop(1, NZ, wait_qg, 0)
    my_rows = rows_of(b, ROWS)
    odd = lax.rem(b, 2) == 1
    delta = dlr[...].reshape(NZ, HEAD_DIM)
    shift = ROWS * lax.rem(b, 2)
    here = (lane // 64) == lax.rem(b, 2)
    logs = jnp.concatenate([sl[...], sl[...]], axis=1)
    st[b] = jnp.zeros((8, HEAD_DIM), F32)
    moved = [pltpu.roll(delta[i : i + 1, :], 8 * i, 1) if i else delta[:1, :] for i in range(NZ)]
    for j in range(HD):
        row = jnp.zeros((1, HEAD_DIM), F32)
        for i in range(NZ):
            row = jnp.where(lane // 8 == i + j, moved[i], row)
        st[b, j : j + 1, :] = pltpu.roll(row, lax.rem(shift + HEAD_DIM - 8 * j, HEAD_DIM), 1)
    st[b, HD : 2 * HD, :] = jnp.where(here, logs, 0.0)

    def ag(i, k, s, e):
        start, count = GATHERED[i]
        block = qg.at[pl.ds(start, count), :, rows_of(s, ROWS), :]
        return remote(block, block, s_xy.at[i, k], r_xy.at[i, k], on_chip(e))

    def ag_st(k, s, e):
        return remote(st.at[s], st.at[s], s_st.at[k], r_st.at[k], on_chip(e))

    def source(k):
        return chip(-TREE[k][0][0], -TREE[k][0][1])

    def from_parent(k, copy):
        _, (px, py), (dx, dy) = TREE[k]
        return copy(k, chip(-px, -py), chip(dx, dy))

    def ag_of(j):
        return lambda k, s, e: ag(j, k, s, e)

    for j in range(HD):
        both = qgr[:, :, cols(j)].astype(F32)
        qg[j, 0, my_rows, :] = both[:, :8, :].reshape(ROWS, HEAD_DIM).astype(BF)
        qg[j, 1, my_rows, :] = both[:, 8:, :].reshape(ROWS, HEAD_DIM).astype(BF)
        for k in range(8):
            if j == 0:
                from_parent(k, ag_st).start()
                from_parent(k, ag_of(0)).start()
            if j == HD - 1:
                from_parent(k, ag_of(1)).start()

    def ag_relay(j):
        for k in RELAYS:
            if j == 0:
                ag_st(k, source(k), b).wait_recv()
            ag(j, k, source(k), b).wait_recv()
            for child in BELOW[TREE[k][0]]:
                if j == 0:
                    from_parent(child, ag_st).start()
                from_parent(child, ag_of(j)).start()

    def ag_rest(j):
        for k in range(EDGES):
            if k not in RELAYS:
                if j == 0:
                    ag_st(k, source(k), b).wait_recv()
                ag(j, k, source(k), b).wait_recv()

    pair = pl.multiple_of(16 * (b // 2), 16)
    own_st = st[b]
    own_st = jnp.where(odd, pltpu.roll(own_st, 64, 1), own_st)
    text_st = pltpu.roll(stp[:, SLAB_Q:], lax.rem(ROWS - pair + HEAD_DIM, HEAD_DIM), 1)
    mine_at = lane // 8 == ROWS // 8 + lax.rem(b, 2)
    stat_row = lax.broadcasted_iota(jnp.int32, (8, 1), 0)
    silent = jnp.where(jnp.logical_and(stat_row >= HD, stat_row < 2 * HD), SILENT, 0.0)
    tst[...] = jnp.where(lane < ROWS, own_st, jnp.where(mine_at, text_st, silent))
    key_index = lax.broadcasted_iota(jnp.int32, (TXT, 1), 0)
    mask = (key_index < cnt_ref[0]).astype(F32)

    def text_keys(j):
        for i in range(2):
            qtk[i, :ROWS, :] = qg[j, i, my_rows, :]
            qtk[i, ROWS : ROWS + 16, :] = qg[j, i, pl.ds(SLAB_Q + pair, 16), :]
            qtk[i, ROWS + 16 :, :] = jnp.zeros((HEAD_DIM - ROWS - 16, HEAD_DIM), BF)
        keys = tkr[j]
        one_q, one_k, one_v = attend(
            keys, keys.T, tv[:, cols(j)], qtk[0], qtk[1],
            tst[HD + j : HD + j + 1, :], tst[j : j + 1, :], mask,
        )
        dqt[j] = one_q
        dkvt[j, 0] = one_k
        dkvt[j, 1] = one_v

    mine = rows_of(c, KEYS)
    theirs = rows_of(1 - c, KEYS)

    def sib_kv(j, rows):
        part = kv.at[j, :, rows, :]
        return remote(part, part, s_skv.at[j], r_skv.at[j], sib)

    def share_kv(j):
        def wait_kv(t, carry):
            s = zdev(t)
            remote(
                kvs.at[s * HD + j], kv.at[j, :, key_rows(s), :], s_kv.at[j, t], r_kv.at[j, s], {"head": s}
            ).wait_recv()
            return carry

        lax.fori_loop(1, NZ, wait_kv, 0)
        sib_kv(j, mine).start()

    text_keys(0)
    ag_relay(0)
    text_keys(1)
    share_kv(0)
    text_keys(2)
    other = rows_of(1 - c, HALF)
    sib_t = remote(dkvt.at[:, :, other, :], xt, s_sib.at[0], r_sib.at[0], sib)
    sib_t.start()
    ag_rest(0)
    for i in range(NB // 2):
        stp[:, cols(i)] = st[2 * i] + st[2 * i + 1]

    def image_keys(j, keys_t, rows, start):
        one_q, one_k, one_v = attend(
            kv[j, 0], keys_t, kv[j, 1], qg[j, 0, rows, :], qg[j, 1, rows, :],
            stp[HD + j : HD + j + 1, rows], stp[j : j + 1, rows],
        )
        dq[j, rows, :] = one_q
        if start:
            dkv[j, 0] = one_k
            dkv[j, 1] = one_v
        else:
            dkv[j, 0] += one_k
            dkv[j, 1] += one_v

    def sib_d(j):
        return remote(xs.at[j], xk.at[j], s_sd.at[j], r_sd.at[j], sib)

    ck, sn_k = angles(blk, 0, KEYS)

    def token_rows(s):
        return rows_of(s, 32)

    def z_out(j, t, d):
        return remote(
            dkvs.at[j, :, token_rows(d), :], okv.at[h * HD + j], s_o.at[j, t], r_o.at[j, h], {"head": d}
        )

    def finish_kv(j):
        sib_d(j).wait()
        dkvs[j, 0] = turn_back(dkv[j, 0, mine, :] + xk[j, 0].astype(F32), ck, sn_k).astype(BF)
        dkvs[j, 1] = (dkv[j, 1, mine, :] + xk[j, 1].astype(F32)).astype(BF)

        def go_out(t, carry):
            z_out(j, t, zdev(t)).start()
            return carry

        lax.fori_loop(1, NZ, go_out, 0)
        okv[h * HD + j] = dkvs[j, :, token_rows(h), :]

    def make_sum(own, copy, sent, got, parts):
        def gather(e, below):
            for k in below:
                copy(k).wait_recv()
            values = []
            for i in range(parts):
                value = own(i, e)
                for k in below:
                    value = value + got(i, k)[...].astype(F32)
                values.append(value)
            return values

        def pass_on(some):
            for k in some:
                for i, value in enumerate(gather(source(k), BELOW[TREE[k][0]])):
                    sent(i, k)[...] = value.astype(BF)
                copy(k).start()

        return gather, pass_on

    def towards_root(k, src, dst, ss, rs):
        dx, dy = TREE[k][2]
        return remote(src, dst, ss, rs, on_chip(chip(-dx, -dy)))

    def rs_copy(i, k):
        start, count = SUMMED[i]
        heads = pl.ds(start, count)
        return towards_root(k, rs_s.at[heads, k], rs_r.at[heads, k], s_rs.at[i, k], r_rs.at[i, k])

    def tk_copy(k):
        return towards_root(k, tk_s.at[k], tk_r.at[k], s_tk.at[k], r_tk.at[k])

    def own_rows(start):
        def own(i, e):
            j = start + i
            text = dq[j, pl.ds(pl.multiple_of(SLAB_Q + e * 8, 8), 8), :]
            return jnp.concatenate([dq[j, rows_of(e, ROWS), :], text, jnp.zeros_like(text)], axis=0)

        return own

    def own_text(_, e):
        at = rows_of(e, 8)
        at_half = pl.ds(pl.multiple_of(HALF * c + e * 8, 8), 8)
        heads = [
            jnp.concatenate([dkvt[j, i, at_half, :] + xt[j, i, at, :] for i in range(2)], axis=0)
            for j in range(HD)
        ]
        return jnp.concatenate(heads, axis=1)

    rs_sums = [
        make_sum(
            own_rows(start),
            lambda k, i=i: rs_copy(i, k),
            lambda i, k, start=start: rs_s.at[start + i, k],
            lambda i, k, start=start: rs_r.at[start + i, k],
            count,
        )
        for i, (start, count) in enumerate(SUMMED)
    ]
    tk_gather, tk_pass = make_sum(
        own_text, tk_copy, lambda i, k: tk_s.at[k], lambda i, k: tk_r.at[k], 1
    )

    def tx_copy(k, s, e):
        return remote(tx.at[c, s], tx.at[c, s], s_tx.at[k], r_tx.at[k], on_chip(e))

    def tkx_copy(k, s, e):
        return remote(tkx.at[c, s], tkx.at[c, s], s_tkx.at[k], r_tkx.at[k], on_chip(e))

    def spread_out(copy):
        for k in range(8):
            from_parent(k, copy).start()

    def spread_on(copy):
        for k in RELAYS:
            copy(k, source(k), b).wait_recv()
            for child in BELOW[TREE[k][0]]:
                from_parent(child, copy).start()

    def spread_end(copy):
        for k in range(EDGES):
            if k not in RELAYS:
                copy(k, source(k), b).wait_recv()

    own_at = pl.ds(pl.multiple_of(TXT + HALF * c + 8 * b, 8), 8)
    ct = cos_t[own_at, :]
    sn = sin_t[own_at, :]

    def text_key_result():
        (total,) = tk_gather(b, range(8))
        for j in range(HD):
            tkx[c, b, :, cols(j)] = jnp.concatenate(
                [turn_back(total[:8, cols(j)], ct, sn), total[8:, cols(j)]], axis=0
            ).astype(BF)
        spread_out(tkx_copy)

    sib_tkx = remote(tkx.at[c], tkx.at[c], s_sib.at[2], r_sib.at[2], sib)
    sib_tx = remote(tx.at[c], tx.at[c], s_sib.at[1], r_sib.at[1], sib)

    sib_t.wait()
    tk_pass(LEAVES)
    for j in range(HD):
        if j == 1:
            ag_rest(1)
        sib_kv(j, theirs).wait_recv()
        if j == 0:
            ag_relay(1)
        keys_t = kv[j, 0].T
        image_keys(j, keys_t, slice(SLAB_Q, SLAB_Q + HALF), True)
        for i in range(SLAB_Q // STEP):
            image_keys(j, keys_t, slice(i * STEP, (i + 1) * STEP), False)
            if i == 1 and j > 0:
                finish_kv(j - 1)
        xs[j] = dkv[j, :, theirs, :].astype(BF)
        sib_d(j).start()
        if j < HD - 1:
            share_kv(j + 1)
        if j == 0:
            tk_pass(RELAYS)
        else:
            rs_sums[j - 1][1](LEAVES)
        if j == HD - 1:
            rs_sums[0][1](RELAYS)
        if j == 1:
            text_key_result()
        if j == 2:
            spread_on(tkx_copy)
    finish_kv(HD - 1)
    rs_sums[1][1](RELAYS)

    cq, sn_q = slab_angles(0, ROWS)
    parts = []
    text_parts = []
    totals = rs_sums[0][0](b, range(8)) + rs_sums[1][0](b, range(8))
    for j, total in enumerate(totals):
        extra = jnp.where(odd, dqt[j, ROWS + 8 : ROWS + 16, :], dqt[j, ROWS : ROWS + 8, :])
        text_parts.append(turn_back(total[ROWS : ROWS + 8, :] + extra, ct, sn))
        parts.append(turn_back(total[:ROWS, :] + dqt[j, :ROWS, :], cq, sn_q).reshape(NZ, 8, HEAD_DIM))
    tx[c, b, :, :HEAD_DIM] = jnp.concatenate([text_parts[0], text_parts[2]], axis=0).astype(BF)
    tx[c, b, :, HEAD_DIM:] = jnp.concatenate(
        [text_parts[1], jnp.zeros_like(text_parts[1])], axis=0
    ).astype(BF)
    spread_out(tx_copy)
    sqs[:, :, :HEAD_DIM] = jnp.concatenate([parts[0], parts[2]], axis=1).astype(BF)
    sqs[:, :, HEAD_DIM:] = jnp.concatenate([parts[1], jnp.zeros_like(parts[1])], axis=1).astype(BF)

    def out_q(t, d):
        return remote(sqs.at[d], sqr.at[h], s_oq.at[t], r_oq.at[h], {"head": d})

    def go_oq(t, carry):
        out_q(t, zdev(t)).start()
        return carry

    lax.fori_loop(1, NZ, go_oq, 0)
    sqr[h] = sqs[h]
    spread_end(tkx_copy)
    sib_tkx.start()
    spread_on(tx_copy)
    spread_end(tx_copy)
    sib_tx.start()

    def wait_oq(t, carry):
        s = zdev(t)
        remote(sqs.at[s], sqr.at[s], s_oq.at[t], r_oq.at[s], {"head": s}).wait_recv()
        return carry

    lax.fori_loop(1, NZ, wait_oq, 0)
    for s in range(NZ):
        piece = sqr[s].astype(F32)
        sqo[:, s * W : s * W + 128] = piece[:8, :128].astype(BF)
        sqo[:, s * W + 128 : s * W + 256] = piece[:8, 128:].astype(BF)
        sqo[:, s * W + 256 : s * W + 384] = piece[8:, :128].astype(BF)
    remote(tkx.at[1 - c], tkx.at[1 - c], s_sib.at[2], r_sib.at[2], sib).wait_recv()
    for core in range(2):
        rows = slice(core * HALF, (core + 1) * HALF)
        block = tkx[core].astype(F32)
        txo[1, rows, :] = block[:, :8, :].reshape(HALF, W).astype(BF)
        txo[2, rows, :] = block[:, 8:, :].reshape(HALF, W).astype(BF)
    remote(tx.at[1 - c], tx.at[1 - c], s_sib.at[1], r_sib.at[1], sib).wait_recv()
    for core in range(2):
        rows = slice(core * HALF, (core + 1) * HALF)
        block = tx[core].astype(F32)
        txo[0, rows, :HEAD_DIM] = block[:, :8, :HEAD_DIM].reshape(HALF, HEAD_DIM).astype(BF)
        txo[0, rows, HEAD_DIM : 2 * HEAD_DIM] = block[:, :8, HEAD_DIM:].reshape(HALF, HEAD_DIM).astype(BF)
        txo[0, rows, 2 * HEAD_DIM :] = block[:, 8:, :HEAD_DIM].reshape(HALF, HEAD_DIM).astype(BF)
    for j in range(HD):

        def wait_out(t, carry, j=j):
            s = zdev(t)
            remote(
                dkvs.at[j, :, token_rows(s), :], okv.at[s * HD + j], s_o.at[j, t], r_o.at[j, s], {"head": s}
            ).wait_recv()
            return carry

        lax.fori_loop(1, NZ, wait_out, 0)

    def drain_z(t, carry):
        d = zdev(t)
        z_qg(t, d).wait_send()
        z_dl(t, d).wait_send()
        out_q(t, d).wait_send()
        for j in range(HD):
            z_kv(j, t, d).wait_send()
            z_out(j, t, d).wait_send()
        return carry

    lax.fori_loop(1, NZ, drain_z, 0)
    for k in range(EDGES):
        from_parent(k, ag_st).wait_send()
        from_parent(k, tx_copy).wait_send()
        from_parent(k, tkx_copy).wait_send()
        tk_copy(k).wait_send()
        for i in range(2):
            from_parent(k, ag_of(i)).wait_send()
            rs_copy(i, k).wait_send()
    for j in range(HD):
        sib_kv(j, mine).wait_send()
    sib_tx.wait_send()
    sib_tkx.wait_send()


def deliver(sqo, okv, txo, sqg, ikg, ivg, tqg, tkg, tvg):
    sqg[...] = sqo[...]
    for n in range(NZ * HD):
        ikg[:, cols(n)] = okv[n, 0]
        ivg[:, cols(n)] = okv[n, 1]
    tqg[...] = txo[0]
    tkg[...] = txo[1]
    tvg[...] = txo[2]


def on_device(
    slab_query, slab_output, slab_cotangent, slab_logsum, image_keys, image_values,
    text_query, text_keys, text_values, text_output, text_cotangent, text_logsum,
    text_count, slab_offsets,
):
    vmem = pl.BlockSpec(memory_space=pltpu.VMEM)
    smem = pl.BlockSpec(memory_space=pltpu.SMEM)
    hbm = pl.BlockSpec(memory_space=pltpu.HBM)
    dma = pltpu.SemaphoreType.DMA
    slab = pltpu.VMEM((8, ALL), BF)
    text = pltpu.VMEM((TXT, W), BF)
    sqo, okv, txo = pl.pallas_call(
        kernel,
        out_shape=[
            jax.ShapeDtypeStruct((8, ALL), BF),
            jax.ShapeDtypeStruct((NZ * HD, 2, 32, HEAD_DIM), BF),
            jax.ShapeDtypeStruct((3, TXT, W), BF),
        ],
        in_specs=[smem, smem] + [hbm] * 13,
        out_specs=[vmem] * 3,
        scratch_shapes=[
            slab, slab, slab,
            pltpu.VMEM((HD, ROWS), F32),
            pltpu.VMEM((32, ALL), BF),
            pltpu.VMEM((32, ALL), BF),
            text, text, text, text, text,
            pltpu.VMEM((HD, TXT), F32),
            pltpu.VMEM((2, 512, HEAD_DIM), F32),
            pltpu.VMEM((NZ, 16, W), BF),
            pltpu.VMEM((NZ, 1, HEAD_DIM), F32),
            pltpu.VMEM((NZ, 16, W), BF),
            pltpu.VMEM((NZ, 1, HEAD_DIM), F32),
            pltpu.VMEM((NZ * HD, 2, 32, HEAD_DIM), BF),
            pltpu.VMEM((HD, 2, 2 * KEYS, HEAD_DIM), BF),
            pltpu.VMEM((HD, 2, SLAB_Q + HALF, HEAD_DIM), BF),
            pltpu.VMEM((NB, 8, HEAD_DIM), F32),
            pltpu.VMEM((8, SLAB_Q + HALF), F32),
            pltpu.VMEM((HD, TXT, HEAD_DIM), BF),
            pltpu.VMEM((8, HEAD_DIM), F32),
            pltpu.VMEM((2, HEAD_DIM, HEAD_DIM), BF),
            pltpu.VMEM((HD, HEAD_DIM, HEAD_DIM), F32),
            pltpu.VMEM((HD, 2, TXT, HEAD_DIM), F32),
            pltpu.VMEM((HD, 2, HALF, HEAD_DIM), F32),
            pltpu.VMEM((HD, SLAB_Q + HALF, HEAD_DIM), F32),
            pltpu.VMEM((HD, 2, 2 * KEYS, HEAD_DIM), F32),
            pltpu.VMEM((HD, 2, KEYS, HEAD_DIM), BF),
            pltpu.VMEM((HD, 2, KEYS, HEAD_DIM), BF),
            pltpu.VMEM((HD, 2, KEYS, HEAD_DIM), BF),
            pltpu.VMEM((HD, EDGES, 80, HEAD_DIM), BF),
            pltpu.VMEM((HD, EDGES, 80, HEAD_DIM), BF),
            pltpu.VMEM((EDGES, 16, W), BF),
            pltpu.VMEM((EDGES, 16, W), BF),
            pltpu.VMEM((NZ, 16, 256), BF),
            pltpu.VMEM((NZ, 16, 256), BF),
            pltpu.VMEM((2, NB, 16, 256), BF),
            pltpu.VMEM((2, NB, 16, W), BF),
            dma((13,)),
            dma((2, NZ)), dma((NZ,)), dma((NZ,)),
            dma((HD, NZ)), dma((HD, NZ)),
            dma((2, EDGES)), dma((2, EDGES)),
            dma((EDGES,)), dma((EDGES,)),
            dma((3,)), dma((3,)),
            dma((HD,)), dma((HD,)), dma((HD,)), dma((HD,)),
            dma((HD, NZ)), dma((HD, NZ)),
            dma((NZ,)), dma((NZ,)),
            dma((2, EDGES)), dma((2, EDGES)),
            dma((EDGES,)), dma((EDGES,)),
            dma((EDGES,)), dma((EDGES,)),
            dma((EDGES,)), dma((EDGES,)),
        ],
        compiler_params=pltpu.CompilerParams(
            collective_id=0, has_side_effects=True, vmem_limit_bytes=63 * 1024 * 1024
        ),
        cost_estimate=pl.CostEstimate(
            flops=2_500_000_000, bytes_accessed=4_000_000, transcendentals=2_000_000
        ),
        name="joint_backward",
    )(
        slab_offsets, text_count, slab_query, slab_output, slab_cotangent, slab_logsum.T,
        image_keys, image_values, text_query, text_keys, text_values, text_output,
        text_cotangent, text_logsum.T, tables(),
    )
    shapes = [
        jax.ShapeDtypeStruct(x.shape, BF)
        for x in (slab_query, image_keys, image_values, text_query, text_keys, text_values)
    ]
    return pl.pallas_call(
        deliver, out_shape=shapes, in_specs=[vmem] * 3, out_specs=[vmem] * 6, name="deliver"
    )(sqo, okv, txo)


def solution(mesh):
    tokens = P(("rep", "blk", "head"), None)
    text = P("rep", "head")
    in_specs = (
        tokens, tokens, tokens, P(("rep", "blk"), "head"), tokens, tokens,
        text, text, text, text, text, text, P("rep"), P("rep"),
    )
    out_specs = (tokens, tokens, tokens, text, text, text)
    return jax.shard_map(
        on_device, mesh=mesh, in_specs=in_specs, out_specs=out_specs, check_vma=False
    )
```

```python
import jax
import jax.numpy as jnp
import numpy as np
from jax import lax
from jax.experimental import pallas as pl
from jax.experimental.pallas import tpu as pltpu
from jax.sharding import PartitionSpec as P

HEAD_DIM = 128
FACTOR = HEAD_DIM ** (-0.5)
NZ = 8
NX = 4
NB = NX * NX
HD = 3
W = HD * HEAD_DIM
ALL = NZ * W
TXT = 256
HALF = TXT // 2
ROWS = 64
KEYS = 256
SLAB_Q = NB * ROWS
STEP = 256
SILENT = 1e30
BF = jnp.bfloat16
F32 = jnp.float32
MESH = pl.DeviceIdType.MESH

TREE = (
    ((1, 0), (0, 0), (1, 0)),
    ((-1, 0), (0, 0), (-1, 0)),
    ((0, 1), (0, 0), (0, 1)),
    ((0, -1), (0, 0), (0, -1)),
    ((1, 1), (0, 0), (1, 1)),
    ((1, -1), (0, 0), (1, -1)),
    ((-1, 1), (0, 0), (-1, 1)),
    ((-1, -1), (0, 0), (-1, -1)),
    ((2, 0), (-1, 0), (-1, 0)),
    ((0, 2), (0, -1), (0, -1)),
    ((2, 1), (1, 1), (1, 0)),
    ((2, -1), (-1, -1), (-1, 0)),
    ((1, 2), (1, 1), (0, 1)),
    ((-1, 2), (-1, 1), (0, 1)),
    ((2, 2), (1, -1), (1, -1)),
)
EDGES = len(TREE)
BELOW = {child: [k for k, e in enumerate(TREE) if e[1] == child] for child, _, _ in TREE}
RELAYS = (1, 3, 4, 7, 6, 5)
LEAVES = (14, 8, 9, 10, 11, 12, 13, 0, 2)
AROUND = [e[2] for e in TREE[:8]]


def tables():
    place = np.arange(512, dtype=np.float64)[:, None]
    frequency = 10000.0 ** (-np.arange(32, dtype=np.float64) / 32)
    angles = np.tile(place * frequency[None, :], (1, 4))
    sign = np.where(np.arange(128) < 64, -1.0, 1.0)
    return np.stack([np.cos(angles), np.sin(angles) * sign]).astype(np.float32)


def nt(a, b):
    return lax.dot_general(a, b, (((1,), (1,)), ((), ())), preferred_element_type=F32)


def nn(a, b):
    return lax.dot_general(a, b, (((1,), (0,)), ((), ())), preferred_element_type=F32)


def turn(x, cosine, sine):
    return x * cosine + pltpu.roll(x, 64, 1) * sine


def turn_back(x, cosine, sine):
    return x * cosine - pltpu.roll(x, 64, 1) * sine


def cols(n):
    return slice(n * HEAD_DIM, (n + 1) * HEAD_DIM)


def attend(keys, keys_t, values, queries, cotan, logsum, delta, mask=None):
    p = jnp.exp(nt(keys, queries) * FACTOR - logsum)
    if mask is not None:
        p = p * mask
    dv = nn(p.astype(BF), cotan)
    dp = nt(values, cotan)
    ds = (p * (dp - delta) * FACTOR).astype(BF)
    return nn(keys_t, ds).T, nn(ds, queries), dv


def kernel(
    off_ref, cnt_ref, sq_h, so_h, sg_h, sl_h, ik_h, iv_h, tq_h, tk_h, tv_h, to_h, tg_h, tl_h, tab_h,
    sqo, okv, txo,
    sq, so, sg, sl, ik, iv, tq, tk, tv, to, tg, tl, tab,
    qgs, dls, qgr, dlr, kvs, kv, qg, st, stp, tkr, tst, qtk, dqt, dkvt, xt,
    dq, dkv, xs, xk, dkvs, rs_s, rs_r, tk_s, tk_r, sqs, sqr, tx, tkx,
    s_in, s_z, r_zqg, r_zd, s_kv, r_kv, s_xy, r_xy, s_st, r_st, s_sib, r_sib, s_skv, r_skv, s_sd, r_sd,
    s_o, r_o, s_oq, r_oq, s_rs, r_rs, s_tx, r_tx, s_tk, r_tk, s_tkx, r_tkx,
):
    blk = lax.axis_index("blk")
    h = lax.axis_index("head")
    c = lax.rem(blk, 2)
    b = blk // 2
    bx = b // NX
    by = lax.rem(b, NX)
    lane = lax.broadcasted_iota(jnp.int32, (1, HEAD_DIM), 1)
    sub = lax.broadcasted_iota(jnp.int32, (8, 1), 0)
    first = lax.rem(lane, 64) < 32
    sib = {"blk": 2 * b + 1 - c}

    def zdev(t):
        return lax.rem(h + t, NZ)

    def chip(dx, dy):
        return lax.rem(bx + dx + NX, NX) * NX + lax.rem(by + dy + NX, NX)

    def on_chip(e):
        return {"blk": 2 * e + c}

    def remote(src, dst, ss, rs, dev):
        return pltpu.make_async_remote_copy(
            src_ref=src, dst_ref=dst, send_sem=ss, recv_sem=rs, device_id=dev, device_id_type=MESH
        )

    def rows_of(e, count):
        return pl.ds(pl.multiple_of(e * count, count), count)

    def wide(d):
        return rows_of(d, W)

    def fetch(i, src, dst):
        copy = pltpu.make_async_copy(src, dst, s_in.at[i])
        copy.start()
        return copy

    f_slab = [fetch(1, sq_h, sq), fetch(2, sg_h, sg), fetch(3, so_h, so)]
    f_tab = fetch(0, tab_h, tab)
    f_k = fetch(4, ik_h, ik)
    f_v = fetch(5, iv_h, iv)
    f_text = [
        fetch(6, tq_h, tq), fetch(7, tg_h, tg), fetch(8, to_h, to), fetch(9, tk_h, tk),
        fetch(10, tv_h, tv), fetch(11, tl_h, tl), fetch(12, sl_h, sl),
    ]

    bar = pltpu.get_barrier_semaphore()

    def greet_z(t, carry):
        pl.semaphore_signal(bar, inc=1, device_id={"head": zdev(t)}, device_id_type=MESH)
        return carry

    lax.fori_loop(1, NZ, greet_z, 0)
    for dx, dy in AROUND:
        pl.semaphore_signal(bar, inc=1, device_id=on_chip(chip(dx, dy)), device_id_type=MESH)
    pl.semaphore_signal(bar, inc=1, device_id=sib, device_id_type=MESH)

    cos_t, sin_t = tab.at[0], tab.at[1]

    def angles(row, start, count):
        ct = cos_t[pl.ds(start, count), :]
        sn = sin_t[pl.ds(start, count), :]
        cr = cos_t[pl.ds(row, 1), :]
        sr = sin_t[pl.ds(row, 1), :]
        return jnp.where(first, cr, ct), jnp.where(first, sr, sn)

    place = off_ref[0] + blk
    row_at = lax.broadcasted_iota(jnp.int32, (32, 1), 0) == place // 4
    col_at = lax.rem(place, 4)

    def slab_angles(start, count):
        result = []
        for table in (cos_t, sin_t):
            row = jnp.sum(jnp.where(row_at, table[:32, :], 0.0), axis=0, keepdims=True)
            col = table[pl.ds(start, count), :]
            for i in range(1, 4):
                col = jnp.where(col_at == i, table[pl.ds(64 * i + start, count), :], col)
            result.append(jnp.where(first, row, col))
        return result

    f_tab.wait()
    for copy in f_slab:
        copy.wait()
    cq, sn_q = slab_angles(pl.multiple_of(8 * h, 8), 8)
    for d in range(NZ):
        acc = jnp.zeros((8, HEAD_DIM), F32)
        for j in range(HD):
            n = d * HD + j
            g = sg[:, cols(n)].astype(F32)
            q = turn(sq[:, cols(n)].astype(F32), cq, sn_q)
            qgs[d, :, cols(j)] = jnp.concatenate([q, g], axis=0).astype(BF)
            own = jnp.sum(g * so[:, cols(n)].astype(F32), axis=1, keepdims=True)
            acc = jnp.where(lane == 8 * j + sub, own, acc)
        dls[d] = jnp.sum(acc, axis=0, keepdims=True)
    pl.semaphore_wait(bar, NZ + len(AROUND))

    def z_qg(t, d):
        return remote(qgs.at[d], qgr.at[h], s_z.at[0, t], r_zqg.at[h], {"head": d})

    def z_dl(t, d):
        return remote(dls.at[d], dlr.at[h], s_z.at[1, t], r_zd.at[h], {"head": d})

    def key_rows(s):
        return pl.ds(pl.multiple_of(c * KEYS + s * 32, 32), 32)

    def z_kv(j, t, d):
        return remote(
            kvs.at[d * HD + j], kv.at[j, :, key_rows(h), :], s_kv.at[j, t], r_kv.at[j, h], {"head": d}
        )

    def go_qg(t, carry):
        z_qg(t, zdev(t)).start()
        z_dl(t, zdev(t)).start()
        return carry

    lax.fori_loop(1, NZ, go_qg, 0)
    f_k.wait()
    f_v.wait()
    ck, sn_k = angles(blk, pl.multiple_of(32 * h, 32), 32)
    for j in range(HD):
        for d in range(NZ):
            n = d * HD + j
            kvs[n, 0] = turn(ik[:, cols(n)].astype(F32), ck, sn_k).astype(BF)
            kvs[n, 1] = iv[:, cols(n)]

        def go_kv(t, carry, j=j):
            z_kv(j, t, zdev(t)).start()
            return carry

        lax.fori_loop(1, NZ, go_kv, 0)
        kv[j, :, key_rows(h), :] = kvs[h * HD + j]
    qgr[h] = qgs[h]
    dlr[h] = dls[h]

    for copy in f_text:
        copy.wait()
    half = rows_of(c, HALF)
    text_at = pl.ds(pl.multiple_of(TXT + HALF * c, HALF), HALF)
    ct = cos_t[text_at, :]
    sn = sin_t[text_at, :]
    acc = jnp.zeros((HALF, HEAD_DIM), F32)
    for j in range(HD):
        g = tg[half, cols(j)]
        qg[j, 0, SLAB_Q:, :] = turn(tq[half, cols(j)].astype(F32), ct, sn).astype(BF)
        qg[j, 1, SLAB_Q:, :] = g
        own = jnp.sum(g.astype(F32) * to[half, cols(j)].astype(F32), axis=1, keepdims=True)
        acc = jnp.where(lane == j, own, acc)
        tkr[j] = turn(tk[:, cols(j)].astype(F32), cos_t[TXT:, :], sin_t[TXT:, :]).astype(BF)
    stp[:, SLAB_Q:] = acc.T[:8, :]
    stp[HD : 2 * HD, SLAB_Q:] = tl[:, half]

    def wait_qg(t, carry):
        s = zdev(t)
        remote(qgs.at[s], qgr.at[s], s_z.at[0, t], r_zqg.at[s], {"head": s}).wait_recv()
        remote(dls.at[s], dlr.at[s], s_z.at[1, t], r_zd.at[s], {"head": s}).wait_recv()
        return carry

    lax.fori_loop(1, NZ, wait_qg, 0)
    my_rows = rows_of(b, ROWS)
    odd = lax.rem(b, 2) == 1
    delta = dlr[...].reshape(NZ, HEAD_DIM)
    shift = ROWS * lax.rem(b, 2)
    here = (lane // 64) == lax.rem(b, 2)
    logs = jnp.concatenate([sl[...], sl[...]], axis=1)
    st[b] = jnp.zeros((8, HEAD_DIM), F32)
    moved = [pltpu.roll(delta[i : i + 1, :], 8 * i, 1) if i else delta[:1, :] for i in range(NZ)]
    for j in range(HD):
        row = jnp.zeros((1, HEAD_DIM), F32)
        for i in range(NZ):
            row = jnp.where(lane // 8 == i + j, moved[i], row)
        st[b, j : j + 1, :] = pltpu.roll(row, lax.rem(shift + HEAD_DIM - 8 * j, HEAD_DIM), 1)
    st[b, HD : 2 * HD, :] = jnp.where(here, logs, 0.0)

    def ag(j, k, s, e):
        block = qg.at[j, :, rows_of(s, ROWS), :]
        return remote(block, block, s_xy.at[j, k], r_xy.at[j, k], on_chip(e))

    def ag_st(k, s, e):
        return remote(st.at[s], st.at[s], s_st.at[k], r_st.at[k], on_chip(e))

    def source(k):
        return chip(-TREE[k][0][0], -TREE[k][0][1])

    def from_parent(k, copy):
        _, (px, py), (dx, dy) = TREE[k]
        return copy(k, chip(-px, -py), chip(dx, dy))

    def ag_of(j):
        return lambda k, s, e: ag(j, k, s, e)

    for j in range(HD):
        both = qgr[:, :, cols(j)].astype(F32)
        qg[j, 0, my_rows, :] = both[:, :8, :].reshape(ROWS, HEAD_DIM).astype(BF)
        qg[j, 1, my_rows, :] = both[:, 8:, :].reshape(ROWS, HEAD_DIM).astype(BF)
        for k in range(8):
            if j == 0:
                from_parent(k, ag_st).start()
            from_parent(k, ag_of(j)).start()

    def ag_relay(j):
        for k in RELAYS:
            if j == 0:
                ag_st(k, source(k), b).wait_recv()
            ag(j, k, source(k), b).wait_recv()
            for child in BELOW[TREE[k][0]]:
                if j == 0:
                    from_parent(child, ag_st).start()
                from_parent(child, ag_of(j)).start()

    def ag_rest(j):
        for k in range(EDGES):
            if k not in RELAYS:
                if j == 0:
                    ag_st(k, source(k), b).wait_recv()
                ag(j, k, source(k), b).wait_recv()

    pair = pl.multiple_of(16 * (b // 2), 16)
    own_st = st[b]
    own_st = jnp.where(odd, pltpu.roll(own_st, 64, 1), own_st)
    text_st = pltpu.roll(stp[:, SLAB_Q:], lax.rem(ROWS - pair + HEAD_DIM, HEAD_DIM), 1)
    mine_at = lane // 8 == ROWS // 8 + lax.rem(b, 2)
    stat_row = lax.broadcasted_iota(jnp.int32, (8, 1), 0)
    silent = jnp.where(jnp.logical_and(stat_row >= HD, stat_row < 2 * HD), SILENT, 0.0)
    tst[...] = jnp.where(lane < ROWS, own_st, jnp.where(mine_at, text_st, silent))
    key_index = lax.broadcasted_iota(jnp.int32, (TXT, 1), 0)
    mask = (key_index < cnt_ref[0]).astype(F32)

    def text_keys(j):
        for i in range(2):
            qtk[i, :ROWS, :] = qg[j, i, my_rows, :]
            qtk[i, ROWS : ROWS + 16, :] = qg[j, i, pl.ds(SLAB_Q + pair, 16), :]
            qtk[i, ROWS + 16 :, :] = jnp.zeros((HEAD_DIM - ROWS - 16, HEAD_DIM), BF)
        keys = tkr[j]
        one_q, one_k, one_v = attend(
            keys, keys.T, tv[:, cols(j)], qtk[0], qtk[1],
            tst[HD + j : HD + j + 1, :], tst[j : j + 1, :], mask,
        )
        dqt[j] = one_q
        dkvt[j, 0] = one_k
        dkvt[j, 1] = one_v

    mine = rows_of(c, KEYS)
    theirs = rows_of(1 - c, KEYS)

    def sib_kv(j, rows):
        part = kv.at[j, :, rows, :]
        return remote(part, part, s_skv.at[j], r_skv.at[j], sib)

    def share_kv(j):
        def wait_kv(t, carry):
            s = zdev(t)
            remote(
                kvs.at[s * HD + j], kv.at[j, :, key_rows(s), :], s_kv.at[j, t], r_kv.at[j, s], {"head": s}
            ).wait_recv()
            return carry

        lax.fori_loop(1, NZ, wait_kv, 0)
        sib_kv(j, mine).start()

    text_keys(0)
    ag_relay(0)
    share_kv(0)
    ag_relay(1)
    other = rows_of(1 - c, HALF)
    sib_t = remote(dkvt.at[:, :, other, :], xt, s_sib.at[0], r_sib.at[0], sib)
    ag_rest(0)
    for i in range(NB // 2):
        stp[:, cols(i)] = st[2 * i] + st[2 * i + 1]

    def image_keys(j, keys_t, rows, start):
        one_q, one_k, one_v = attend(
            kv[j, 0], keys_t, kv[j, 1], qg[j, 0, rows, :], qg[j, 1, rows, :],
            stp[HD + j : HD + j + 1, rows], stp[j : j + 1, rows],
        )
        dq[j, rows, :] = one_q
        if start:
            dkv[j, 0] = one_k
            dkv[j, 1] = one_v
        else:
            dkv[j, 0] += one_k
            dkv[j, 1] += one_v

    def sib_d(j):
        return remote(xs.at[j], xk.at[j], s_sd.at[j], r_sd.at[j], sib)

    ck, sn_k = angles(blk, 0, KEYS)

    def token_rows(s):
        return rows_of(s, 32)

    def z_out(j, t, d):
        return remote(
            dkvs.at[j, :, token_rows(d), :], okv.at[h * HD + j], s_o.at[j, t], r_o.at[j, h], {"head": d}
        )

    def finish_kv(j):
        sib_d(j).wait()
        dkvs[j, 0] = turn_back(dkv[j, 0, mine, :] + xk[j, 0].astype(F32), ck, sn_k).astype(BF)
        dkvs[j, 1] = (dkv[j, 1, mine, :] + xk[j, 1].astype(F32)).astype(BF)

        def go_out(t, carry):
            z_out(j, t, zdev(t)).start()
            return carry

        lax.fori_loop(1, NZ, go_out, 0)
        okv[h * HD + j] = dkvs[j, :, token_rows(h), :]

    def make_sum(own, copy, sent, got):
        def gather(e, below):
            value = own(e)
            for k in below:
                copy(k).wait_recv()
                value = value + got[k].astype(F32)
            return value

        def pass_on(some):
            for k in some:
                sent[k] = gather(source(k), BELOW[TREE[k][0]]).astype(BF)
                copy(k).start()

        return gather, pass_on

    def towards_root(k, src, dst, ss, rs):
        dx, dy = TREE[k][2]
        return remote(src, dst, ss, rs, on_chip(chip(-dx, -dy)))

    def rs_copy(j, k):
        return towards_root(k, rs_s.at[j, k], rs_r.at[j, k], s_rs.at[j, k], r_rs.at[j, k])

    def tk_copy(k):
        return towards_root(k, tk_s.at[k], tk_r.at[k], s_tk.at[k], r_tk.at[k])

    def own_rows(j):
        def own(e):
            text = dq[j, pl.ds(pl.multiple_of(SLAB_Q + e * 8, 8), 8), :]
            return jnp.concatenate([dq[j, rows_of(e, ROWS), :], text, jnp.zeros_like(text)], axis=0)

        return own

    def own_text(e):
        at = rows_of(e, 8)
        at_half = pl.ds(pl.multiple_of(HALF * c + e * 8, 8), 8)
        heads = [
            jnp.concatenate([dkvt[j, i, at_half, :] + xt[j, i, at, :] for i in range(2)], axis=0)
            for j in range(HD)
        ]
        return jnp.concatenate(heads, axis=1)

    rs_sums = [
        make_sum(own_rows(j), lambda k, j=j: rs_copy(j, k), rs_s.at[j], rs_r.at[j]) for j in range(HD)
    ]
    tk_gather, tk_pass = make_sum(own_text, tk_copy, tk_s, tk_r)

    def tx_copy(k, s, e):
        return remote(tx.at[c, s], tx.at[c, s], s_tx.at[k], r_tx.at[k], on_chip(e))

    def tkx_copy(k, s, e):
        return remote(tkx.at[c, s], tkx.at[c, s], s_tkx.at[k], r_tkx.at[k], on_chip(e))

    def spread_out(copy):
        for k in range(8):
            from_parent(k, copy).start()

    def spread_on(copy):
        for k in RELAYS:
            copy(k, source(k), b).wait_recv()
            for child in BELOW[TREE[k][0]]:
                from_parent(child, copy).start()

    def spread_end(copy):
        for k in range(EDGES):
            if k not in RELAYS:
                copy(k, source(k), b).wait_recv()

    own_at = pl.ds(pl.multiple_of(TXT + HALF * c + 8 * b, 8), 8)
    ct = cos_t[own_at, :]
    sn = sin_t[own_at, :]

    def text_key_result():
        total = tk_gather(b, range(8))
        for j in range(HD):
            tkx[c, b, :, cols(j)] = jnp.concatenate(
                [turn_back(total[:8, cols(j)], ct, sn), total[8:, cols(j)]], axis=0
            ).astype(BF)
        spread_out(tkx_copy)

    sib_tkx = remote(tkx.at[c], tkx.at[c], s_sib.at[2], r_sib.at[2], sib)
    sib_tx = remote(tx.at[c], tx.at[c], s_sib.at[1], r_sib.at[1], sib)

    for j in range(HD):
        if j > 0:
            ag_rest(j)
        sib_kv(j, theirs).wait_recv()
        if j == 0:
            ag_relay(2)
        keys_t = kv[j, 0].T
        image_keys(j, keys_t, slice(SLAB_Q, SLAB_Q + HALF), True)
        for i in range(SLAB_Q // STEP):
            image_keys(j, keys_t, slice(i * STEP, (i + 1) * STEP), False)
            if i == 1 and j > 0:
                finish_kv(j - 1)
        xs[j] = dkv[j, :, theirs, :].astype(BF)
        sib_d(j).start()
        if j < HD - 1:
            share_kv(j + 1)
            text_keys(j + 1)
        if j == 1:
            sib_t.start()
        rs_sums[j][1](LEAVES)
        if j > 0:
            rs_sums[j - 1][1](RELAYS)
        if j == 1:
            sib_t.wait()
            tk_pass(LEAVES)
        if j == 2:
            tk_pass(RELAYS)
    finish_kv(HD - 1)
    rs_sums[HD - 1][1](RELAYS)
    text_key_result()

    cq, sn_q = slab_angles(0, ROWS)
    parts = []
    text_parts = []
    for j in range(HD):
        total = rs_sums[j][0](b, range(8))
        extra = jnp.where(odd, dqt[j, ROWS + 8 : ROWS + 16, :], dqt[j, ROWS : ROWS + 8, :])
        text_parts.append(turn_back(total[ROWS : ROWS + 8, :] + extra, ct, sn))
        parts.append(turn_back(total[:ROWS, :] + dqt[j, :ROWS, :], cq, sn_q).reshape(NZ, 8, HEAD_DIM))
    tx[c, b, :, :HEAD_DIM] = jnp.concatenate([text_parts[0], text_parts[2]], axis=0).astype(BF)
    tx[c, b, :, HEAD_DIM:] = jnp.concatenate(
        [text_parts[1], jnp.zeros_like(text_parts[1])], axis=0
    ).astype(BF)
    spread_out(tx_copy)
    sqs[:, :, :HEAD_DIM] = jnp.concatenate([parts[0], parts[2]], axis=1).astype(BF)
    sqs[:, :, HEAD_DIM:] = jnp.concatenate([parts[1], jnp.zeros_like(parts[1])], axis=1).astype(BF)

    def out_q(t, d):
        return remote(sqs.at[d], sqr.at[h], s_oq.at[t], r_oq.at[h], {"head": d})

    def go_oq(t, carry):
        out_q(t, zdev(t)).start()
        return carry

    lax.fori_loop(1, NZ, go_oq, 0)
    sqr[h] = sqs[h]
    spread_on(tkx_copy)
    spread_on(tx_copy)
    spread_end(tkx_copy)
    sib_tkx.start()
    spread_end(tx_copy)
    sib_tx.start()

    def wait_oq(t, carry):
        s = zdev(t)
        remote(sqs.at[s], sqr.at[s], s_oq.at[t], r_oq.at[s], {"head": s}).wait_recv()
        return carry

    lax.fori_loop(1, NZ, wait_oq, 0)
    for s in range(NZ):
        piece = sqr[s].astype(F32)
        sqo[:, s * W : s * W + 128] = piece[:8, :128].astype(BF)
        sqo[:, s * W + 128 : s * W + 256] = piece[:8, 128:].astype(BF)
        sqo[:, s * W + 256 : s * W + 384] = piece[8:, :128].astype(BF)
    remote(tkx.at[1 - c], tkx.at[1 - c], s_sib.at[2], r_sib.at[2], sib).wait_recv()
    for core in range(2):
        rows = slice(core * HALF, (core + 1) * HALF)
        block = tkx[core].astype(F32)
        txo[1, rows, :] = block[:, :8, :].reshape(HALF, W).astype(BF)
        txo[2, rows, :] = block[:, 8:, :].reshape(HALF, W).astype(BF)
    remote(tx.at[1 - c], tx.at[1 - c], s_sib.at[1], r_sib.at[1], sib).wait_recv()
    for core in range(2):
        rows = slice(core * HALF, (core + 1) * HALF)
        block = tx[core].astype(F32)
        txo[0, rows, :HEAD_DIM] = block[:, :8, :HEAD_DIM].reshape(HALF, HEAD_DIM).astype(BF)
        txo[0, rows, HEAD_DIM : 2 * HEAD_DIM] = block[:, :8, HEAD_DIM:].reshape(HALF, HEAD_DIM).astype(BF)
        txo[0, rows, 2 * HEAD_DIM :] = block[:, 8:, :HEAD_DIM].reshape(HALF, HEAD_DIM).astype(BF)
    for j in range(HD):

        def wait_out(t, carry, j=j):
            s = zdev(t)
            remote(
                dkvs.at[j, :, token_rows(s), :], okv.at[s * HD + j], s_o.at[j, t], r_o.at[j, s], {"head": s}
            ).wait_recv()
            return carry

        lax.fori_loop(1, NZ, wait_out, 0)

    def drain_z(t, carry):
        d = zdev(t)
        z_qg(t, d).wait_send()
        z_dl(t, d).wait_send()
        out_q(t, d).wait_send()
        for j in range(HD):
            z_kv(j, t, d).wait_send()
            z_out(j, t, d).wait_send()
        return carry

    lax.fori_loop(1, NZ, drain_z, 0)
    for k in range(EDGES):
        from_parent(k, ag_st).wait_send()
        from_parent(k, tx_copy).wait_send()
        from_parent(k, tkx_copy).wait_send()
        tk_copy(k).wait_send()
        for j in range(HD):
            from_parent(k, ag_of(j)).wait_send()
            rs_copy(j, k).wait_send()
    for j in range(HD):
        sib_kv(j, mine).wait_send()
    sib_tx.wait_send()
    sib_tkx.wait_send()


def deliver(sqo, okv, txo, sqg, ikg, ivg, tqg, tkg, tvg):
    sqg[...] = sqo[...]
    for n in range(NZ * HD):
        ikg[:, cols(n)] = okv[n, 0]
        ivg[:, cols(n)] = okv[n, 1]
    tqg[...] = txo[0]
    tkg[...] = txo[1]
    tvg[...] = txo[2]


def on_device(
    slab_query, slab_output, slab_cotangent, slab_logsum, image_keys, image_values,
    text_query, text_keys, text_values, text_output, text_cotangent, text_logsum,
    text_count, slab_offsets,
):
    vmem = pl.BlockSpec(memory_space=pltpu.VMEM)
    smem = pl.BlockSpec(memory_space=pltpu.SMEM)
    hbm = pl.BlockSpec(memory_space=pltpu.HBM)
    dma = pltpu.SemaphoreType.DMA
    slab = pltpu.VMEM((8, ALL), BF)
    text = pltpu.VMEM((TXT, W), BF)
    sqo, okv, txo = pl.pallas_call(
        kernel,
        out_shape=[
            jax.ShapeDtypeStruct((8, ALL), BF),
            jax.ShapeDtypeStruct((NZ * HD, 2, 32, HEAD_DIM), BF),
            jax.ShapeDtypeStruct((3, TXT, W), BF),
        ],
        in_specs=[smem, smem] + [hbm] * 13,
        out_specs=[vmem] * 3,
        scratch_shapes=[
            slab, slab, slab,
            pltpu.VMEM((HD, ROWS), F32),
            pltpu.VMEM((32, ALL), BF),
            pltpu.VMEM((32, ALL), BF),
            text, text, text, text, text,
            pltpu.VMEM((HD, TXT), F32),
            pltpu.VMEM((2, 512, HEAD_DIM), F32),
            pltpu.VMEM((NZ, 16, W), BF),
            pltpu.VMEM((NZ, 1, HEAD_DIM), F32),
            pltpu.VMEM((NZ, 16, W), BF),
            pltpu.VMEM((NZ, 1, HEAD_DIM), F32),
            pltpu.VMEM((NZ * HD, 2, 32, HEAD_DIM), BF),
            pltpu.VMEM((HD, 2, 2 * KEYS, HEAD_DIM), BF),
            pltpu.VMEM((HD, 2, SLAB_Q + HALF, HEAD_DIM), BF),
            pltpu.VMEM((NB, 8, HEAD_DIM), F32),
            pltpu.VMEM((8, SLAB_Q + HALF), F32),
            pltpu.VMEM((HD, TXT, HEAD_DIM), BF),
            pltpu.VMEM((8, HEAD_DIM), F32),
            pltpu.VMEM((2, HEAD_DIM, HEAD_DIM), BF),
            pltpu.VMEM((HD, HEAD_DIM, HEAD_DIM), F32),
            pltpu.VMEM((HD, 2, TXT, HEAD_DIM), F32),
            pltpu.VMEM((HD, 2, HALF, HEAD_DIM), F32),
            pltpu.VMEM((HD, SLAB_Q + HALF, HEAD_DIM), F32),
            pltpu.VMEM((HD, 2, 2 * KEYS, HEAD_DIM), F32),
            pltpu.VMEM((HD, 2, KEYS, HEAD_DIM), BF),
            pltpu.VMEM((HD, 2, KEYS, HEAD_DIM), BF),
            pltpu.VMEM((HD, 2, KEYS, HEAD_DIM), BF),
            pltpu.VMEM((HD, EDGES, 80, HEAD_DIM), BF),
            pltpu.VMEM((HD, EDGES, 80, HEAD_DIM), BF),
            pltpu.VMEM((EDGES, 16, W), BF),
            pltpu.VMEM((EDGES, 16, W), BF),
            pltpu.VMEM((NZ, 16, 256), BF),
            pltpu.VMEM((NZ, 16, 256), BF),
            pltpu.VMEM((2, NB, 16, 256), BF),
            pltpu.VMEM((2, NB, 16, W), BF),
            dma((13,)),
            dma((2, NZ)), dma((NZ,)), dma((NZ,)),
            dma((HD, NZ)), dma((HD, NZ)),
            dma((HD, EDGES)), dma((HD, EDGES)),
            dma((EDGES,)), dma((EDGES,)),
            dma((3,)), dma((3,)),
            dma((HD,)), dma((HD,)), dma((HD,)), dma((HD,)),
            dma((HD, NZ)), dma((HD, NZ)),
            dma((NZ,)), dma((NZ,)),
            dma((HD, EDGES)), dma((HD, EDGES)),
            dma((EDGES,)), dma((EDGES,)),
            dma((EDGES,)), dma((EDGES,)),
            dma((EDGES,)), dma((EDGES,)),
        ],
        compiler_params=pltpu.CompilerParams(
            collective_id=0, has_side_effects=True, vmem_limit_bytes=63 * 1024 * 1024
        ),
        cost_estimate=pl.CostEstimate(
            flops=2_500_000_000, bytes_accessed=4_000_000, transcendentals=2_000_000
        ),
        name="joint_backward",
    )(
        slab_offsets, text_count, slab_query, slab_output, slab_cotangent, slab_logsum.T,
        image_keys, image_values, text_query, text_keys, text_values, text_output,
        text_cotangent, text_logsum.T, tables(),
    )
    shapes = [
        jax.ShapeDtypeStruct(x.shape, BF)
        for x in (slab_query, image_keys, image_values, text_query, text_keys, text_values)
    ]
    return pl.pallas_call(
        deliver, out_shape=shapes, in_specs=[vmem] * 3, out_specs=[vmem] * 6, name="deliver"
    )(sqo, okv, txo)


def solution(mesh):
    tokens = P(("rep", "blk", "head"), None)
    text = P("rep", "head")
    in_specs = (
        tokens, tokens, tokens, P(("rep", "blk"), "head"), tokens, tokens,
        text, text, text, text, text, text, P("rep"), P("rep"),
    )
    out_specs = (tokens, tokens, tokens, text, text, text)
    return jax.shard_map(
        on_device, mesh=mesh, in_specs=in_specs, out_specs=out_specs, check_vma=False
    )
```
